256 devices in a mesh: group: 32 (over x, y, core), tp: 8 (over z).
Axes of the slice: x: 4, y: 4, z: 8, core: 2. Of those that a mesh axis runs over, the one named last changes fastest.
Arguments:
- keys_cache: bfloat16 [4096, 8, 128, 128], P('group', 'tp'), may hold values from -6 to 6
- values_cache: bfloat16 [4096, 8, 128, 128], P('group', 'tp'), may hold values from -6 to 6
- lengths: int32 [4096], P('group'), may hold values from 16 to 128, as said below
- guard_flags: int32 [4096], P('group'), may hold values from 0 to 1
- migrations: int32 [832, 3], P('group'), may hold values from 0 to 127, as said below
- queries: bfloat16 [4096, 4, 4096], P('group', None, 'tp'), may hold values from -6 to 6
- new_keys: bfloat16 [4096, 4, 1024], P('group', None, 'tp'), may hold values from -6 to 6
- new_values: bfloat16 [4096, 4, 1024], P('group', None, 'tp'), may hold values from -6 to 6
- out_weight: bfloat16 [4096, 4096], P('tp'), may hold values from -0.375 to 0.375
Outputs:
- attended: bfloat16 [4096, 4, 4096], P('group', None, 'tp')
The draws below stay inside these ranges and needn't reach their ends.
Inputs may be any that keep to these rules, and one draw needn't show every extreme that they name: `lengths`: some slot has exactly 128 positions. `migrations`: each group's list holds 26 moves. A move takes a row with guard flag 0 of its own group to a slot with guard flag 1 of another group. No two moves share a source row or a destination slot. Every group receives exactly 26 rows, and a group sends either 0 or exactly 2 rows to each other group.
All inputs are finite; a program needn't handle non-finite values.
Results may differ from the reference program's by a relative error of at most 0.0057.
Values may be sent and summed in bfloat16 or wider, within the bound.
No kernel may reach another device: no remote copies, remote signals or barrier semaphores. Data moves between devices by JAX's collectives and lax.ppermute only.
A program may use at most 128 MiB of HBM per device.

```python
import jax
import jax.numpy as jnp
from jax import lax

KV_HEADS = 8
HEAD = 128
QPK = 4
DW_OUT = 4096
ROWS = 128
CACHE = 128
STEPS = 4
CAP = 2
MOVES = 26
GROUPS = 32


def group_order(subkey):
    return jax.random.permutation(subkey, ROWS)


def migration_plan(key):
    plan_key = jax.random.fold_in(key, 53)
    order_key, offset_key, shuffle_key, spare_key = jax.random.split(plan_key, 4)
    slot_orders = jax.vmap(group_order)(jax.random.split(order_key, GROUPS)).astype(jnp.int32)
    offsets = (jax.random.permutation(offset_key, GROUPS - 1)[:MOVES // CAP] + 1).astype(jnp.int32)
    shuffle = jax.random.permutation(shuffle_key, GROUPS).astype(jnp.int32)
    position = jnp.argsort(shuffle).astype(jnp.int32)
    spare_count = jax.random.randint(spare_key, (GROUPS,), 0, 4).astype(jnp.int32)
    return (slot_orders, offsets, shuffle, position, spare_count)


def draw_keys_cache(key, part):
    key = jax.random.fold_in(key, 11)
    normal_part = jax.random.normal(key, (GROUPS * ROWS, KV_HEADS, CACHE, HEAD), jnp.float32)
    normal_part = jnp.clip(normal_part, -6.0, 6.0)
    return normal_part.astype(jnp.bfloat16)


def draw_queries(key, part):
    key = jax.random.fold_in(key, 31)
    normal_part = jax.random.normal(key, (GROUPS * ROWS, STEPS, KV_HEADS, QPK, HEAD), jnp.float32)
    normal_part = jnp.clip(normal_part, -6.0, 6.0)
    return normal_part.reshape(GROUPS * ROWS, STEPS, KV_HEADS * QPK * HEAD).astype(jnp.bfloat16)


def draw_lengths(key, part):
    key = jax.random.fold_in(key, 23)
    first_key, second_key = jax.random.split(key)
    drawn = jax.random.randint(first_key, (GROUPS * ROWS,), CACHE // 8, CACHE + 1)
    longest = jax.random.randint(second_key, (), 0, GROUPS * ROWS)
    return drawn.at[longest].set(CACHE).astype(jnp.int32)


def draw_guard_flags(key, part):
    slot_orders, offsets, shuffle, position, spare_count = migration_plan(key)
    slot_rank = jnp.argsort(slot_orders, axis=1)
    ended_flag = (slot_rank >= MOVES) & (slot_rank < 2 * MOVES + spare_count[:, None])
    return ended_flag.reshape(-1).astype(jnp.int32)


def draw_migrations(key, part):
    slot_orders, offsets, shuffle, position, spare_count = migration_plan(key)
    move_ids = jnp.arange(MOVES, dtype=jnp.int32)
    offset_ids = move_ids // CAP
    group_ids = jnp.arange(GROUPS, dtype=jnp.int32)[:, None]
    destination = shuffle[(position[group_ids] + offsets[offset_ids][None, :]) % GROUPS]
    source_row = slot_orders[:, :MOVES]
    target_slot = slot_orders[destination, MOVES + move_ids[None, :]]
    stacked = jnp.stack([source_row, destination, target_slot], axis=-1)
    return stacked.reshape(GROUPS * MOVES, 3).astype(jnp.int32)


def block_levels(stream_key, extent, pieces, low, top_value):
    gain, own = 1.0, jax.random.fold_in(stream_key, 6)
    for dim, blocks in pieces:
        draws = jnp.exp(jax.random.uniform(jax.random.fold_in(own, dim), (blocks,), jnp.float32, low / len(pieces), top_value / len(pieces)))
        gain = gain * jnp.repeat(draws, extent[dim] // blocks).reshape([-1 if axis == dim else 1 for axis in range(len(extent))])
    return gain


def normal_values(stream_key, dims, deviation, reach, cuts=(), kind=jnp.bfloat16):
    entries = deviation * jax.random.normal(stream_key, dims, jnp.float32)
    if cuts:
        entries = entries * block_levels(stream_key, dims, cuts, -0.22, 0.18)
    return jnp.clip(entries, -reach, reach).astype(kind)


def setup_inputs(seed: int = 0) -> dict:
    seeds = jax.random.split(jax.random.key(seed), 10)
    keys_cache = draw_keys_cache(jax.random.fold_in(seeds[9], 71), 0)
    values_cache = normal_values(seeds[1], (GROUPS * ROWS, KV_HEADS, CACHE, HEAD), 1.0, 6.0, ((0, 32), (1, 8)))
    lengths = draw_lengths(jax.random.fold_in(seeds[9], 71), 0)
    guard_flags = draw_guard_flags(jax.random.fold_in(seeds[9], 71), 0)
    migrations = draw_migrations(jax.random.fold_in(seeds[9], 71), 0)
    queries = draw_queries(jax.random.fold_in(seeds[9], 71), 0)
    new_keys = normal_values(seeds[6], (GROUPS * ROWS, STEPS, KV_HEADS * HEAD), 1.0, 6.0, ((0, 32), (2, 8)))
    new_values = normal_values(seeds[7], (GROUPS * ROWS, STEPS, KV_HEADS * HEAD), 1.0, 6.0, ((0, 32), (2, 8)))
    out_weight = normal_values(seeds[8], (KV_HEADS * QPK * HEAD, DW_OUT), (KV_HEADS * QPK * HEAD * 8 // CACHE) ** -0.5, 0.375, ((0, 8),))
    return {"keys_cache": keys_cache, "values_cache": values_cache, "lengths": lengths, "guard_flags": guard_flags, "migrations": migrations, "queries": queries, "new_keys": new_keys, "new_values": new_values, "out_weight": out_weight}


def attend_row(queried, cached_keys, cached_values, fresh_keys, fresh_values, length):
    score_scale = HEAD ** -0.5
    cache_scores = jnp.einsum("tkqd,kld->tkql", queried, cached_keys) * score_scale
    fresh_scores = jnp.einsum("tkqd,skd->tkqs", queried, fresh_keys) * score_scale
    positions = jnp.arange(CACHE, dtype=jnp.int32)
    cache_scores = jnp.where(positions[None, None, None, :] < length, cache_scores, -jnp.inf)
    step_ids = jnp.arange(STEPS, dtype=jnp.int32)
    visible = step_ids[None, :] <= step_ids[:, None]
    fresh_scores = jnp.where(visible[:, None, None, :], fresh_scores, -jnp.inf)
    highest = jnp.maximum(jnp.max(cache_scores, axis=-1), jnp.max(fresh_scores, axis=-1))[..., None]
    cache_exp = jnp.exp(cache_scores - highest)
    fresh_exp = jnp.exp(fresh_scores - highest)
    denominator = jnp.sum(cache_exp, axis=-1, keepdims=True) + jnp.sum(fresh_exp, axis=-1, keepdims=True)
    cache_weight = (cache_exp / denominator).astype(jnp.bfloat16)
    fresh_weight = (fresh_exp / denominator).astype(jnp.bfloat16)
    cache_weight, fresh_weight = lax.optimization_barrier((cache_weight, fresh_weight))
    mixture = jnp.einsum("tkql,kld->tkqd", cache_weight.astype(jnp.float32), cached_values)
    mixture = mixture + jnp.einsum("tkqs,skd->tkqd", fresh_weight.astype(jnp.float32), fresh_values)
    return mixture.astype(jnp.bfloat16)


def reference(keys_cache, values_cache, lengths, guard_flags, migrations, queries, new_keys, new_values, out_weight):
    total_rows = GROUPS * ROWS
    sender = jnp.repeat(jnp.arange(GROUPS, dtype=jnp.int32), MOVES)
    source = sender * ROWS + migrations[:, 0]
    target = migrations[:, 1] * ROWS + migrations[:, 2]
    source_of = jnp.arange(total_rows, dtype=jnp.int32).at[target].set(source)
    live_slot = (guard_flags == 0).at[source].set(False).at[target].set(True)

    def one_row(row_index):
        anchor = source_of[row_index]
        queried = queries[row_index].astype(jnp.float32).reshape(STEPS, KV_HEADS, QPK, HEAD)
        cached_keys = keys_cache[anchor].astype(jnp.float32)
        cached_values = values_cache[anchor].astype(jnp.float32)
        fresh_keys = new_keys[row_index].astype(jnp.float32).reshape(STEPS, KV_HEADS, HEAD)
        fresh_values = new_values[row_index].astype(jnp.float32).reshape(STEPS, KV_HEADS, HEAD)
        head_output = attend_row(queried, cached_keys, cached_values, fresh_keys, fresh_values, lengths[anchor])
        return head_output.reshape(STEPS, KV_HEADS * QPK * HEAD)

    head_output = lax.map(one_row, jnp.arange(total_rows, dtype=jnp.int32))
    flat_heads = head_output.reshape(total_rows * STEPS, KV_HEADS * QPK * HEAD)
    mixture = jnp.dot(flat_heads, out_weight, preferred_element_type=jnp.float32)
    mixture = mixture.reshape(total_rows, STEPS, DW_OUT)
    return jnp.where(live_slot[:, None, None], mixture, 0.0).astype(jnp.bfloat16)
```

```python
import functools

import jax
import jax.numpy as jnp
from jax import lax
from jax.experimental import pallas as pl
from jax.experimental.pallas import tpu as pltpu
from jax.sharding import PartitionSpec as P

CAP = 2
F32, BF16, I32 = jnp.float32, jnp.bfloat16, jnp.int32
FRESH = 16
VMEM = pl.BlockSpec(memory_space=pltpu.VMEM)
SMEM = pl.BlockSpec(memory_space=pltpu.SMEM)
ANY = pl.BlockSpec(memory_space=pl.ANY)


def call(kernel, out_shape, in_specs, scratch=(), flops=0, nbytes=0, exps=0, limit=32):
    single = isinstance(out_shape, jax.ShapeDtypeStruct)
    return pl.pallas_call(
        kernel,
        out_shape=out_shape,
        in_specs=in_specs,
        out_specs=VMEM if single else [VMEM] * len(out_shape),
        scratch_shapes=list(scratch),
        cost_estimate=pl.CostEstimate(
            flops=flops, bytes_accessed=nbytes, transcendentals=exps
        ),
        compiler_params=pltpu.CompilerParams(vmem_limit_bytes=limit << 20),
    )


def table_kernel(moves_ref, table_ref):
    groups, lanes = table_ref.shape
    moves = moves_ref.shape[1]
    target = moves_ref[1:2, :]
    slot = (moves_ref[2:3, :] + 1).astype(F32)
    hit = lax.broadcasted_iota(I32, (groups, moves), 0) == target
    earlier = lax.broadcasted_iota(I32, (moves, moves), 0) < lax.broadcasted_iota(
        I32, (moves, moves), 1
    )
    before = jnp.dot(
        hit.astype(F32), earlier.astype(F32), preferred_element_type=F32
    ).astype(I32)
    lane = lax.broadcasted_iota(I32, (groups, lanes), 1)
    table = jnp.zeros((groups, lanes), I32)
    for c in range(CAP):
        entry = jnp.sum(
            jnp.where(hit & (before == c), slot, 0.0), axis=1, keepdims=True
        ).astype(I32)
        table = jnp.where(lane == c, entry, table)
    table_ref[...] = table


def payload_kernel(table_ref, query_ref, key_ref, value_ref, out_ref):
    wide, narrow = query_ref.shape[2], key_ref.shape[2]
    for e in range(out_ref.shape[0]):
        slot = jnp.maximum(table_ref[e // CAP, e % CAP] - 1, 0)
        out_ref[e, :, 0:wide] = query_ref[slot]
        out_ref[e, :, wide : wide + narrow] = key_ref[slot]
        out_ref[e, :, wide + narrow : wide + 2 * narrow] = value_ref[slot]


def fetch(keys_ref, values_ref, kbuf, vbuf, ksem, vsem, row_of, rows, batch):
    cache = keys_ref.shape[2]

    def start(i, carry):
        row = row_of(i)
        pltpu.make_async_copy(
            keys_ref.at[row, 0], kbuf.at[i, pl.ds(0, cache)], ksem.at[i // batch]
        ).start()
        pltpu.make_async_copy(
            values_ref.at[row, 0], vbuf.at[i, pl.ds(0, cache)], vsem.at[i // batch]
        ).start()
        return carry

    lax.fori_loop(0, rows, start, 0)


def await_batch(cache_ref, buf, sem, b, batch):
    cache = cache_ref.shape[2]
    pltpu.make_async_copy(
        cache_ref.at[pl.ds(0, batch), 0],
        buf.at[pl.ds(b * batch, batch), pl.ds(0, cache)],
        sem.at[b],
    ).wait()


def attend(
    rows, batch, keys_ref, values_ref, kbuf, vbuf, ksem, vsem, score, weight, query_of, fresh_of, length_of, put
):
    cache, head = keys_ref.shape[2], keys_ref.shape[3]
    positions = cache + FRESH

    def stack(value):
        heads = value.shape[1] // head
        value = value.astype(F32)
        parts = [value[:, h * head : (h + 1) * head] for h in range(heads)]
        return jnp.concatenate(parts, axis=0)

    def fresh_rows(value):
        value = value.astype(F32)
        pad = jnp.zeros((FRESH - value.shape[0], head), F32)
        return jnp.concatenate([value, pad], axis=0).astype(BF16)

    steps = query_of(0).shape[0]
    lines = query_of(0).shape[1] // head * steps

    def scores(b, carry):
        for u in range(batch):
            i = b * batch + u
            fresh_key, fresh_value = fresh_of(i)
            kbuf[i, cache:positions, :] = fresh_rows(fresh_key)
            vbuf[i, cache:positions, :] = fresh_rows(fresh_value)
        await_batch(keys_ref, kbuf, ksem, b, batch)
        lane = lax.broadcasted_iota(I32, (lines, positions), 1)
        step = lax.rem(lax.broadcasted_iota(I32, (lines, positions), 0), steps)
        visible = (lane >= cache) & (lane - cache <= step)
        for u in range(batch):
            i = b * batch + u
            products = lax.dot_general(
                stack(query_of(i)).astype(BF16),
                kbuf[i],
                (((1,), (1,)), ((), ())),
                preferred_element_type=F32,
            )
            score[pl.ds(pl.multiple_of(i * lines, lines), lines), :] = jnp.where(
                (lane < length_of(i)) | visible, products * head**-0.5, -jnp.inf
            )
        return carry

    lax.fori_loop(0, rows // batch, scores, 0)

    def soften(b, carry):
        chunk = pl.ds(pl.multiple_of(b * batch * lines, lines), batch * lines)
        s = score[chunk, :]
        e = jnp.exp(s - jnp.max(s, axis=1, keepdims=True))
        weight[chunk, :] = (e * (1.0 / jnp.sum(e, axis=1, keepdims=True))).astype(BF16)
        return carry

    lax.fori_loop(0, rows // batch, soften, 0)

    def mix(b, carry):
        await_batch(values_ref, vbuf, vsem, b, batch)
        mixed = []
        for u in range(batch):
            i = b * batch + u
            mixed.append(
                jnp.dot(
                    weight[pl.ds(pl.multiple_of(i * lines, lines), lines), :],
                    vbuf[i],
                    preferred_element_type=F32,
                )
            )
        put(b, mixed)
        return carry

    lax.fori_loop(0, rows // batch, mix, 0)


def list_staying(moves_ref, flags_ref, gone, listed):
    slots, moves = flags_ref.shape[0], moves_ref.shape[1]

    def copy(i, carry):
        gone[i] = flags_ref[i]
        listed[i] = 0
        return carry

    lax.fori_loop(0, slots, copy, 0, unroll=8)

    def leave(m, carry):
        gone[moves_ref[0, m]] = 1
        return carry

    lax.fori_loop(0, moves, leave, 0, unroll=2)

    def enter(i, count):
        listed[count] = i
        return count + jnp.where(gone[i] == 0, 1, 0)

    return lax.fori_loop(0, slots, enter, 0, unroll=8)


def staying_kernel(
    place_ref, moves_ref, flags_ref, lengths_ref, query_ref, key_ref, value_ref, keys_ref, values_ref, weight_ref,
    up_ref, down_ref, own_ref, terms_ref,
    gone, listed, kbuf, vbuf, score, weight, heads, wbuf, ksem, vsem, wsem,
):
    rows, batch = kbuf.shape[0], kbuf.shape[0] // ksem.shape[0]
    steps, head = query_ref.shape[1], keys_ref.shape[3]
    ring, columns = 8, up_ref.shape[1]
    load = pltpu.make_async_copy(weight_ref, wbuf, wsem)
    list_staying(moves_ref, flags_ref, gone, listed)
    fetch(keys_ref, values_ref, kbuf, vbuf, ksem, vsem, lambda i: listed[i], rows, batch)
    load.start()

    def put(b, mixed):
        quads = len(mixed) // 4
        for j in range(quads):
            four = mixed[4 * j : 4 * j + 4]
            for h in range(query_ref.shape[2] // head):
                tile = jnp.concatenate([o[h * steps : (h + 1) * steps] for o in four], axis=0)
                at = pl.ds(pl.multiple_of((b * quads + j) * 16, 16), 16)
                heads[at, h * head : (h + 1) * head] = tile.astype(BF16)

    attend(
        rows, batch, keys_ref, values_ref, kbuf, vbuf, ksem, vsem, score, weight,
        lambda i: query_ref[listed[i]],
        lambda i: (key_ref[listed[i]], value_ref[listed[i]]),
        lambda i: lengths_ref[listed[i]],
        put,
    )
    load.wait()

    def block(k):
        at = lax.rem(place_ref[0] + k, ring) * columns
        return jnp.dot(
            heads[...],
            wbuf[:, pl.ds(pl.multiple_of(at, columns), columns)],
            preferred_element_type=F32,
        )

    far = block(ring // 2)
    cut = up_ref.shape[0]
    up_ref[...] = far[:cut].astype(BF16)
    down_ref[...] = far[cut:].astype(BF16)
    own_ref[...] = block(0)

    def rest(j, carry):
        terms_ref[j] = block(jnp.where(j < 3, j + 1, j + 2))
        return carry

    lax.fori_loop(0, 6, rest, 0)


def leaving_kernel(
    moves_ref, lengths_ref, asked_ref, keys_ref, values_ref,
    out_ref,
    count, entry, kbuf, vbuf, score, weight, ksem, vsem,
):
    rows, batch = kbuf.shape[0], kbuf.shape[0] // ksem.shape[0]
    steps, head = asked_ref.shape[1], keys_ref.shape[3]
    wide = out_ref.shape[2]
    fetch(keys_ref, values_ref, kbuf, vbuf, ksem, vsem, lambda i: moves_ref[0, i], rows, batch)
    for g in range(count.shape[0]):
        count[g] = 0

    def enter(m, carry):
        target = moves_ref[1, m]
        entry[m] = target * CAP + count[target]
        count[target] = count[target] + 1
        return carry

    lax.fori_loop(0, rows, enter, 0, unroll=2)
    out_ref[...] = jnp.zeros(out_ref.shape, BF16)

    def put(b, mixed):
        for u, o in enumerate(mixed):
            at = entry[b * batch + u]
            for h in range(wide // head):
                out_ref[at, :, h * head : (h + 1) * head] = o[h * steps : (h + 1) * steps].astype(BF16)

    attend(
        rows, batch, keys_ref, values_ref, kbuf, vbuf, ksem, vsem, score, weight,
        lambda i: asked_ref[entry[i], :, 0:wide],
        lambda i: (asked_ref[entry[i], :, wide : wide + head], asked_ref[entry[i], :, wide + head : wide + 2 * head]),
        lambda i: lengths_ref[moves_ref[0, i]],
        put,
    )


def list_arrived(table_ref, listed, entries):
    for i in range(listed.shape[0]):
        listed[i] = 0
    count = 0
    for e in range(entries):
        listed[count] = e
        count = count + jnp.where(table_ref[e // CAP, e % CAP] > 0, 1, 0)


def arrived_kernel(table_ref, back_ref, weight_ref, out_ref, listed, heads, wbuf, wsem):
    load = pltpu.make_async_copy(weight_ref, wbuf, wsem)
    load.start()
    entries, steps = back_ref.shape[0], back_ref.shape[1]
    list_arrived(table_ref, listed, entries)
    rows = out_ref.shape[1] // steps
    columns = out_ref.shape[2]
    for j in range(heads.shape[0] // 16):
        four = [back_ref[listed[min(4 * j + u, rows - 1)]].astype(F32) for u in range(4)]
        heads[16 * j : 16 * j + 16, :] = jnp.concatenate(four, axis=0).astype(BF16)
    load.wait()

    def one(k, carry):
        terms = jnp.dot(
            heads[...],
            wbuf[:, pl.ds(pl.multiple_of(k * columns, columns), columns)],
            preferred_element_type=F32,
        )
        out_ref[k] = terms[: out_ref.shape[1]].astype(BF16)
        return carry

    lax.fori_loop(0, out_ref.shape[0], one, 0)


def place_kernel(moves_ref, flags_ref, own_ref, up_ref, down_ref, out_ref, gone, listed, total):
    steps = out_ref.shape[1]
    total[...] = own_ref[...] + up_ref[...].astype(F32) + down_ref[...].astype(F32)
    count = list_staying(moves_ref, flags_ref, gone, listed)
    out_ref[...] = jnp.zeros(out_ref.shape, BF16)
    for i in range(own_ref.shape[0] // steps):

        @pl.when(i < count)
        def _():
            out_ref[listed[i]] = total[i * steps : (i + 1) * steps, :].astype(BF16)


def finish_kernel(table_ref, placed_ref, blocks_ref, out_ref, listed, total):
    steps = out_ref.shape[1]
    entries = table_ref.shape[0] * CAP
    list_arrived(table_ref, listed, entries)
    out_ref[...] = placed_ref[...]
    terms = blocks_ref[0].astype(F32)
    for k in range(1, blocks_ref.shape[0]):
        terms = terms + blocks_ref[k].astype(F32)
    total[...] = terms
    for n in range(blocks_ref.shape[1] // steps):
        e = listed[n]
        slot = jnp.maximum(table_ref[e // CAP, lax.rem(e, CAP)] - 1, 0)
        out_ref[slot] = total[n * steps : (n + 1) * steps, :].astype(BF16)


def on_device(
    keys_cache,
    values_cache,
    lengths,
    guard_flags,
    migrations,
    queries,
    new_keys,
    new_values,
    out_weight,
):
    shape = jax.ShapeDtypeStruct
    slots, _, cache, head = keys_cache.shape
    steps, wide = queries.shape[1:]
    moves = migrations.shape[0]
    groups, ring = lax.axis_size("group"), lax.axis_size("tp")
    columns = out_weight.shape[1] // ring
    entries = groups * CAP
    staying = slots - 2 * moves
    lines = wide // head * steps
    positions = cache + FRESH
    moves_t = migrations.T
    place = lax.axis_index("tp").astype(I32).reshape(1)

    def exchange(x, axis):
        return lax.all_to_all(x, axis, split_axis=0, concat_axis=0, tiled=True)

    table = call(table_kernel, shape((groups, 128), I32), [VMEM], nbytes=1 << 16)(moves_t)
    table = exchange(table.reshape(groups, 1, 128), "group").reshape(groups, 128)

    def scratch(rows, batches):
        return [
            pltpu.VMEM((rows, positions, head), BF16),
            pltpu.VMEM((rows, positions, head), BF16),
            pltpu.VMEM((rows * lines, positions), F32),
            pltpu.VMEM((rows * lines, positions), BF16),
        ]

    tokens = staying * steps
    cut = tokens // 32 * 16
    cut = cut if cut * 2 == tokens else cut + 16
    up, down, own, terms = call(
        staying_kernel,
        [
            shape((cut, columns), BF16),
            shape((tokens - cut, columns), BF16),
            shape((tokens, columns), F32),
            shape((6, tokens, columns), F32),
        ],
        [SMEM] * 4 + [VMEM] * 3 + [ANY] * 3,
        [pltpu.SMEM((slots + 8,), I32), pltpu.SMEM((slots + 8,), I32)]
        + scratch(staying, 19)
        + [
            pltpu.VMEM((tokens, wide), BF16),
            pltpu.VMEM(out_weight.shape, BF16),
            pltpu.SemaphoreType.DMA((staying // 4,)),
            pltpu.SemaphoreType.DMA((staying // 4,)),
            pltpu.SemaphoreType.DMA,
        ],
        flops=2 * tokens * wide * out_weight.shape[1],
        nbytes=20 << 20,
        exps=tokens * positions * 4,
    )(place, moves_t, guard_flags, lengths, queries, new_keys, new_values, keys_cache, values_cache, out_weight)

    ahead = [(i, (i + 1) % ring) for i in range(ring)]
    astern = [(i, (i - 1) % ring) for i in range(ring)]

    def hop(u, d):
        u, d = lax.optimization_barrier((u, d))
        return lax.ppermute(u, "tp", ahead), lax.ppermute(d, "tp", astern)

    up, down = hop(up, down)
    up = jnp.concatenate([up, jnp.zeros((tokens - cut, columns), BF16)], axis=0)
    down = jnp.concatenate([jnp.zeros((cut, columns), BF16), down], axis=0)
    for k in (3, 2, 1):
        up, down = hop(
            (terms[k - 1] + up.astype(F32)).astype(BF16),
            (terms[6 - k] + down.astype(F32)).astype(BF16),
        )

    asked = call(
        payload_kernel, shape((entries, steps, wide + 2 * head), BF16), [SMEM] + [VMEM] * 3, nbytes=2 << 20
    )(table, queries, new_keys, new_values)
    asked = exchange(asked, "group")
    back = call(
        leaving_kernel,
        shape((entries, steps, wide), BF16),
        [SMEM] * 2 + [VMEM] + [ANY] * 2,
        [pltpu.SMEM((groups,), I32), pltpu.SMEM((moves,), I32)]
        + scratch(moves, 2)
        + [pltpu.SemaphoreType.DMA((2,)), pltpu.SemaphoreType.DMA((2,))],
        nbytes=8 << 20,
    )(moves_t, lengths, asked, keys_cache, values_cache)
    back = exchange(back, "group")
    arrived = moves * steps
    blocks = call(
        arrived_kernel,
        shape((ring, arrived, columns), BF16),
        [SMEM, VMEM, ANY],
        [
            pltpu.SMEM((entries + 8,), I32),
            pltpu.VMEM((-(-arrived // 16) * 16, wide), BF16),
            pltpu.VMEM(out_weight.shape, BF16),
            pltpu.SemaphoreType.DMA,
        ],
        nbytes=6 << 20,
    )(table, back, out_weight)
    blocks = exchange(blocks, "tp")

    placed = call(
        place_kernel,
        shape((slots, steps, columns), BF16),
        [SMEM] * 2 + [VMEM] * 3,
        [
            pltpu.SMEM((slots + 8,), I32),
            pltpu.SMEM((slots + 8,), I32),
            pltpu.VMEM((tokens, columns), F32),
        ],
        nbytes=4 << 20,
    )(moves_t, guard_flags, own, up, down)
    return call(
        finish_kernel,
        shape((slots, steps, columns), BF16),
        [SMEM] + [VMEM] * 2,
        [pltpu.SMEM((entries + 8,), I32), pltpu.VMEM((arrived, columns), F32)],
        nbytes=2 << 20,
    )(table, placed, blocks)


def solution(mesh):
    return jax.shard_map(
        on_device,
        mesh=mesh,
        in_specs=(
            P("group", "tp", None, None),
            P("group", "tp", None, None),
            P("group"),
            P("group"),
            P("group", None),
            P("group", None, "tp"),
            P("group", None, "tp"),
            P("group", None, "tp"),
            P("tp", None),
        ),
        out_specs=P("group", None, "tp"),
        check_vma=False,
    )
```

```python
import functools

import jax
import jax.numpy as jnp
from jax import lax
from jax.experimental import pallas as pl
from jax.experimental.pallas import tpu as pltpu
from jax.sharding import PartitionSpec as P

CAP = 2
F32, BF16, I32 = jnp.float32, jnp.bfloat16, jnp.int32
FRESH = 16
STAY_BATCH, LEAVE_BATCH = 76, 26
VMEM = pl.BlockSpec(memory_space=pltpu.VMEM)
SMEM = pl.BlockSpec(memory_space=pltpu.SMEM)
ANY = pl.BlockSpec(memory_space=pltpu.HBM)


def call(kernel, out_shape, in_specs, scratch=(), flops=0, nbytes=0, exps=0, limit=32):
    single = isinstance(out_shape, jax.ShapeDtypeStruct)
    return pl.pallas_call(
        kernel,
        out_shape=out_shape,
        in_specs=in_specs,
        out_specs=VMEM if single else [VMEM] * len(out_shape),
        scratch_shapes=list(scratch),
        cost_estimate=pl.CostEstimate(
            flops=flops, bytes_accessed=nbytes, transcendentals=exps
        ),
        compiler_params=pltpu.CompilerParams(vmem_limit_bytes=limit << 20),
    )


STAY_SLOT, STAY_LENGTH, LEAVE_SLOT, LEAVE_ENTRY, LEAVE_LENGTH, STAY_COUNT = range(6)


def lanes(rows, columns):
    return lax.broadcasted_iota(I32, (rows, columns), 1)


def lines_of(rows, columns):
    return lax.broadcasted_iota(I32, (rows, columns), 0)


def upright(row):
    n = row.shape[1]
    return jnp.sum(jnp.where(lanes(n, n) == lines_of(n, n), row, 0.0), axis=1, keepdims=True)


def plan_kernel(moves_ref, flags_ref, lengths_ref, table_ref, plan_ref):
    groups, wide = table_ref.shape
    moves, slots = moves_ref.shape[1], flags_ref.shape[1]
    source, target = moves_ref[0:1, :], moves_ref[1:2, :]
    slot = (moves_ref[2:3, :] + 1).astype(F32)
    hit = lines_of(groups, moves) == target
    earlier = (lines_of(moves, moves) < lanes(moves, moves)).astype(F32)
    before = jnp.dot(hit.astype(F32), earlier, preferred_element_type=F32).astype(I32)
    table = jnp.zeros((groups, wide), I32)
    for c in range(CAP):
        entry = jnp.sum(jnp.where(hit & (before == c), slot, 0.0), axis=1, keepdims=True)
        table = jnp.where(lanes(groups, wide) == c, entry.astype(I32), table)
    table_ref[...] = table

    place = jnp.sum(jnp.where(hit, lines_of(groups, moves) * CAP + before, 0).astype(F32), axis=0, keepdims=True)
    lengths = lengths_ref[...].astype(F32)
    taken = (upright(source.astype(F32)).astype(I32) == lanes(moves, slots)).astype(F32)
    leave_length = jnp.sum(taken * lengths, axis=1, keepdims=True)
    leave_length = jnp.sum(
        jnp.where(lanes(moves, moves) == lines_of(moves, moves), leave_length, 0.0), axis=0, keepdims=True
    )
    gone = jnp.sum(taken, axis=0, keepdims=True)
    stays = ((flags_ref[...] == 0) & (gone == 0.0)).astype(F32)
    rank = jnp.sum(jnp.where(lanes(slots, slots) < lines_of(slots, slots), stays, 0.0), axis=1, keepdims=True)
    chosen = (rank.astype(I32) == lanes(slots, slots)) & (upright(stays) > 0.0)
    listed = jnp.sum(jnp.where(chosen, lines_of(slots, slots).astype(F32), 0.0), axis=0, keepdims=True)
    listed_length = jnp.sum(jnp.where(chosen, upright(lengths), 0.0), axis=0, keepdims=True)
    plan_ref[...] = jnp.zeros(plan_ref.shape, I32)
    plan_ref[STAY_SLOT : STAY_SLOT + 1, :] = listed.astype(I32)
    plan_ref[STAY_LENGTH : STAY_LENGTH + 1, :] = listed_length.astype(I32)
    plan_ref[LEAVE_SLOT : LEAVE_SLOT + 1, 0:moves] = source
    plan_ref[LEAVE_ENTRY : LEAVE_ENTRY + 1, 0:moves] = place.astype(I32)
    plan_ref[LEAVE_LENGTH : LEAVE_LENGTH + 1, 0:moves] = leave_length.astype(I32)
    plan_ref[STAY_COUNT : STAY_COUNT + 1, 0:1] = jnp.sum(stays, axis=1, keepdims=True).astype(I32)


HERE_ENTRY, HERE_SLOT = range(2)


def payload_kernel(slot_ref, table_ref, query_ref, key_ref, value_ref, out_ref, here_ref):
    wide, narrow = query_ref.shape[2], key_ref.shape[2]
    for e in range(out_ref.shape[0]):
        slot = jnp.maximum(slot_ref[e // CAP, e % CAP] - 1, 0)
        out_ref[e, :, 0:wide] = query_ref[slot]
        out_ref[e, :, wide : wide + narrow] = key_ref[slot]
        out_ref[e, :, wide + narrow : wide + 2 * narrow] = value_ref[slot]
    groups, width = table_ref.shape
    table = table_ref[...]
    there = (table > 0).astype(F32)
    earlier = (lanes(groups, groups) < lines_of(groups, groups)).astype(F32)
    before = jnp.dot(earlier, there, preferred_element_type=F32)
    whole = jnp.sum(there, axis=0, keepdims=True)
    entry = jnp.zeros((1, width), F32)
    slot = jnp.zeros((1, width), F32)
    base = jnp.zeros((1, 1), F32)
    for c in range(CAP):
        rank = (before[:, c : c + 1] + base).astype(I32)
        chosen = (rank == lanes(groups, width)) & (there[:, c : c + 1] > 0.0)
        entry += jnp.sum(jnp.where(chosen, (lines_of(groups, width) * CAP + c).astype(F32), 0.0), axis=0, keepdims=True)
        slot += jnp.sum(jnp.where(chosen, (table[:, c : c + 1] - 1).astype(F32), 0.0), axis=0, keepdims=True)
        base = base + whole[:, c : c + 1]
    here_ref[...] = jnp.zeros(here_ref.shape, I32)
    here_ref[HERE_ENTRY : HERE_ENTRY + 1, :] = entry.astype(I32)
    here_ref[HERE_SLOT : HERE_SLOT + 1, :] = slot.astype(I32)


def attend(rows, batch, kbuf, vbuf, score, weight, cache, steps, heads, row_of, query_of, fresh_of, length_of, await_keys, await_values, put):
    positions, head = kbuf.shape[1:]
    lines = heads * steps

    def fresh_rows(value):
        pad = jnp.zeros((FRESH - steps, head), F32)
        return jnp.concatenate([value.astype(F32), pad], axis=0).astype(BF16)

    def scores(b, carry):
        lane = lanes(lines, positions)
        step = lax.rem(lines_of(lines, positions), steps)
        visible = (lane >= cache) & (lane - cache <= step)
        for u in range(batch):
            i = b * batch + u
            fresh_key, fresh_value = fresh_of(i)
            kbuf[row_of(i), cache:positions, :] = fresh_rows(fresh_key)
            vbuf[row_of(i), cache:positions, :] = fresh_rows(fresh_value)
        for u in range(batch):
            i = b * batch + u
            query = query_of(i).astype(F32)
            query = jnp.concatenate([query[:, h * head : (h + 1) * head] for h in range(heads)], axis=0)
            products = lax.dot_general(
                query.astype(BF16), kbuf[row_of(i)], (((1,), (1,)), ((), ())), preferred_element_type=F32
            )
            score[pl.ds(pl.multiple_of(i * lines, lines), lines), :] = jnp.where(
                (lane < length_of(i)) | visible, products * head**-0.5, -jnp.inf
            )
        return carry

    await_keys()
    lax.fori_loop(0, rows // batch, scores, 0)

    def soften(b, carry):
        chunk = pl.ds(pl.multiple_of(b * batch * lines, lines), batch * lines)
        s = score[chunk, :]
        e = jnp.exp(s - jnp.max(s, axis=1, keepdims=True))
        weight[chunk, :] = (e * (1.0 / jnp.sum(e, axis=1, keepdims=True))).astype(BF16)
        return carry

    lax.fori_loop(0, rows // batch, soften, 0)

    def mix(b, carry):
        mixed = []
        for u in range(batch):
            i = b * batch + u
            mixed.append(
                jnp.dot(
                    weight[pl.ds(pl.multiple_of(i * lines, lines), lines), :],
                    vbuf[row_of(i)],
                    preferred_element_type=F32,
                )
            )
        put(b, mixed)
        return carry

    await_values()
    lax.fori_loop(0, rows // batch, mix, 0)


def staying_kernel(
    place_ref, plan_ref, query_ref, key_ref, value_ref, keys_ref, values_ref, weight_ref,
    up_ref, down_ref, own_ref, *rest,
):
    terms_refs, (kbuf, vbuf, score, weight, heads, wbuf, ksem, vsem, wsem) = rest[:6], rest[6:]
    steps, wide = query_ref.shape[1:]
    slots, _, cache, head = keys_ref.shape
    tokens = heads.shape[0]
    ring, columns = 8, up_ref.shape[1]
    loads = [
        [
            pltpu.make_async_copy(
                ref.at[pl.ds(c * 32, 32), 0], buf.at[pl.ds(c * 32, 32), pl.ds(0, cache)], sem.at[c]
            )
            for c in range(slots // 32)
        ]
        for ref, buf, sem in ((keys_ref, kbuf, ksem), (values_ref, vbuf, vsem))
    ]
    for copy in loads[0] + loads[1]:
        copy.start()
    load = pltpu.make_async_copy(weight_ref, wbuf, wsem)
    load.start()
    def put(b, mixed):
        quads = len(mixed) // 4
        for j in range(quads):
            four = mixed[4 * j : 4 * j + 4]
            for h in range(wide // head):
                tile = jnp.concatenate([o[h * steps : (h + 1) * steps] for o in four], axis=0)
                at = pl.ds(pl.multiple_of((b * quads + j) * 16, 16), 16)
                heads[at, h * head : (h + 1) * head] = tile.astype(BF16)

    def slot(i):
        return plan_ref[STAY_SLOT, i]

    attend(
        tokens // steps, STAY_BATCH, kbuf, vbuf, score, weight, cache, steps, wide // head,
        slot,
        lambda i: query_ref[slot(i)],
        lambda i: (key_ref[slot(i)], value_ref[slot(i)]),
        lambda i: plan_ref[STAY_LENGTH, i],
        lambda: [copy.wait() for copy in loads[0]],
        lambda: [copy.wait() for copy in loads[1]],
        put,
    )
    load.wait()

    def block(k):
        at = lax.rem(place_ref[0] + k, ring) * columns
        return jnp.dot(
            heads[...], wbuf[:, pl.ds(pl.multiple_of(at, columns), columns)], preferred_element_type=F32
        )

    far = block(ring // 2)
    cut = up_ref.shape[0]
    up_ref[...] = far[:cut].astype(BF16)
    down_ref[...] = far[cut:].astype(BF16)
    own_ref[...] = block(0)
    for k, ref in zip((1, 2, 3, 5, 6, 7), terms_refs):
        ref[...] = block(k)


def leaving_kernel(plan_ref, asked_ref, keys_ref, values_ref, out_ref, kbuf, vbuf, score, weight, ksem, vsem):
    rows, cache, head = kbuf.shape[0], keys_ref.shape[2], keys_ref.shape[3]
    steps, wide = out_ref.shape[1:]
    loads = [
        [
            pltpu.make_async_copy(ref.at[plan_ref[LEAVE_SLOT, i], 0], buf.at[i, pl.ds(0, cache)], sem.at[i])
            for i in range(rows)
        ]
        for ref, buf, sem in ((keys_ref, kbuf, ksem), (values_ref, vbuf, vsem))
    ]
    for copy in loads[0] + loads[1]:
        copy.start()
    out_ref[...] = jnp.zeros(out_ref.shape, BF16)

    def entry(i):
        return plan_ref[LEAVE_ENTRY, i]

    def put(b, mixed):
        for u, o in enumerate(mixed):
            at = entry(b * LEAVE_BATCH + u)
            for h in range(wide // head):
                out_ref[at, :, h * head : (h + 1) * head] = o[h * steps : (h + 1) * steps].astype(BF16)

    attend(
        rows, LEAVE_BATCH, kbuf, vbuf, score, weight, cache, steps, wide // head,
        lambda i: i,
        lambda i: asked_ref[entry(i), :, 0:wide],
        lambda i: (asked_ref[entry(i), :, wide : wide + head], asked_ref[entry(i), :, wide + head : wide + 2 * head]),
        lambda i: plan_ref[LEAVE_LENGTH, i],
        lambda: [copy.wait() for copy in loads[0]],
        lambda: [copy.wait() for copy in loads[1]],
        put,
    )


def arrived_kernel(here_ref, back_ref, weight_ref, out_ref, heads, wbuf, wsem):
    load = pltpu.make_async_copy(weight_ref, wbuf, wsem)
    load.start()
    steps = back_ref.shape[1]
    rows, columns = out_ref.shape[1] // steps, out_ref.shape[2]
    for j in range(heads.shape[0] // 16):
        four = [back_ref[here_ref[HERE_ENTRY, min(4 * j + u, rows - 1)]].astype(F32) for u in range(4)]
        heads[16 * j : 16 * j + 16, :] = jnp.concatenate(four, axis=0).astype(BF16)
    load.wait()
    for k in range(out_ref.shape[0]):
        terms = jnp.dot(heads[...], wbuf[:, k * columns : (k + 1) * columns], preferred_element_type=F32)
        out_ref[k] = terms[: out_ref.shape[1]].astype(BF16)


def place_kernel(plan_ref, own_ref, up_ref, down_ref, out_ref, total):
    steps = out_ref.shape[1]
    total[...] = own_ref[...] + up_ref[...].astype(F32) + down_ref[...].astype(F32)
    out_ref[...] = jnp.zeros(out_ref.shape, BF16)
    for i in range(own_ref.shape[0] // steps):

        @pl.when(i < plan_ref[STAY_COUNT, 0])
        def _():
            out_ref[plan_ref[STAY_SLOT, i]] = total[i * steps : (i + 1) * steps, :].astype(BF16)


def finish_kernel(here_ref, placed_ref, blocks_ref, out_ref, total):
    steps = out_ref.shape[1]
    out_ref[...] = placed_ref[...]
    terms = blocks_ref[0].astype(F32)
    for k in range(1, blocks_ref.shape[0]):
        terms = terms + blocks_ref[k].astype(F32)
    total[...] = terms
    for n in range(blocks_ref.shape[1] // steps):
        out_ref[here_ref[HERE_SLOT, n]] = total[n * steps : (n + 1) * steps, :].astype(BF16)


def on_device(
    keys_cache,
    values_cache,
    lengths,
    guard_flags,
    migrations,
    queries,
    new_keys,
    new_values,
    out_weight,
):
    shape = jax.ShapeDtypeStruct
    slots, _, cache, head = keys_cache.shape
    steps, wide = queries.shape[1:]
    moves = migrations.shape[0]
    groups, ring = lax.axis_size("group"), lax.axis_size("tp")
    columns = out_weight.shape[1] // ring
    entries = groups * CAP
    staying = slots - 2 * moves
    lines = wide // head * steps
    positions = cache + FRESH
    place = lax.axis_index("tp").astype(I32).reshape(1)
    barrier = lax.optimization_barrier
    keys_cache, values_cache, out_weight = (
        pltpu.with_memory_space_constraint(x, pltpu.HBM) for x in (keys_cache, values_cache, out_weight)
    )

    def exchange(x, axis):
        return lax.all_to_all(x, axis, split_axis=0, concat_axis=0, tiled=True)

    def scratch(held, rows):
        return [
            pltpu.VMEM((held, positions, head), BF16),
            pltpu.VMEM((held, positions, head), BF16),
            pltpu.VMEM((rows * lines, positions), F32),
            pltpu.VMEM((rows * lines, positions), BF16),
        ]

    table, plan = call(plan_kernel, [shape((groups, 128), I32), shape((8, slots), I32)], [VMEM] * 3, nbytes=1 << 16)(
        migrations.T, guard_flags.reshape(1, slots), lengths.reshape(1, slots)
    )
    table = exchange(table.reshape(groups, 1, 128), "group").reshape(groups, 128)

    tokens = staying * steps
    cut = -(-tokens // 32) * 16
    up, down, own, *terms = call(
        staying_kernel,
        [shape((cut, columns), BF16), shape((tokens - cut, columns), BF16)] + [shape((tokens, columns), F32)] * 7,
        [SMEM] * 2 + [VMEM] * 3 + [ANY] * 3,
        scratch(slots, staying)
        + [
            pltpu.VMEM((tokens, wide), BF16),
            pltpu.VMEM(out_weight.shape, BF16),
            pltpu.SemaphoreType.DMA((slots // 32,)),
            pltpu.SemaphoreType.DMA((slots // 32,)),
            pltpu.SemaphoreType.DMA,
        ],
        flops=2 * tokens * wide * out_weight.shape[1],
        nbytes=20 << 20,
        exps=tokens * positions * 4,
    )(place, plan, queries, new_keys, new_values, keys_cache, values_cache, out_weight)

    ahead = [(i, (i + 1) % ring) for i in range(ring)]
    astern = [(i, (i - 1) % ring) for i in range(ring)]

    def hop(u, d):
        return lax.ppermute(u, "tp", ahead), lax.ppermute(d, "tp", astern)

    def add(k, u, d):
        return (terms[k - 1] + u.astype(F32)).astype(BF16), (terms[6 - k] + d.astype(F32)).astype(BF16)

    table, up, down = barrier((table, up, down))
    up, down = hop(up, down)
    asked, here = call(
        payload_kernel,
        [shape((entries, steps, wide + 2 * head), BF16), shape((8, 128), I32)],
        [SMEM] + [VMEM] * 4,
        nbytes=2 << 20,
    )(table, table, queries, new_keys, new_values)
    asked = exchange(asked, "group")

    asked, up, down = barrier((asked, up, down))
    up = jnp.concatenate([up, jnp.zeros((tokens - cut, columns), BF16)], axis=0)
    down = jnp.concatenate([jnp.zeros((cut, columns), BF16), down], axis=0)
    up, down = hop(*barrier(add(3, up, down)))
    back = call(
        leaving_kernel,
        shape((entries, steps, wide), BF16),
        [SMEM] + [VMEM] + [ANY] * 2,
        scratch(moves, moves) + [pltpu.SemaphoreType.DMA((moves,)), pltpu.SemaphoreType.DMA((moves,))],
        nbytes=8 << 20,
    )(plan, asked, keys_cache, values_cache)
    back = exchange(back, "group")

    back, up, down = barrier((back, up, down))
    up, down = hop(*barrier(add(2, up, down)))
    arrived = moves * steps
    blocks = call(
        arrived_kernel,
        shape((ring, arrived, columns), BF16),
        [SMEM, VMEM, ANY],
        [
            pltpu.VMEM((-(-arrived // 16) * 16, wide), BF16),
            pltpu.VMEM(out_weight.shape, BF16),
            pltpu.SemaphoreType.DMA,
        ],
        nbytes=6 << 20,
    )(here, back, out_weight)
    blocks = exchange(blocks, "tp")
    up, down = hop(*barrier(add(1, up, down)))

    placed = call(
        place_kernel,
        shape((slots, steps, columns), BF16),
        [SMEM] + [VMEM] * 3,
        [pltpu.VMEM((tokens, columns), F32)],
        nbytes=4 << 20,
    )(plan, own, up, down)
    return call(
        finish_kernel,
        shape((slots, steps, columns), BF16),
        [SMEM] + [VMEM] * 2,
        [pltpu.VMEM((arrived, columns), F32)],
        nbytes=2 << 20,
    )(here, placed, blocks)


def solution(mesh):
    return jax.shard_map(
        on_device,
        mesh=mesh,
        in_specs=(
            P("group", "tp", None, None),
            P("group", "tp", None, None),
            P("group"),
            P("group"),
            P("group", None),
            P("group", None, "tp"),
            P("group", None, "tp"),
            P("group", None, "tp"),
            P("tp", None),
        ),
        out_specs=P("group", None, "tp"),
        check_vma=False,
    )
```

```python
import functools

import jax
import jax.numpy as jnp
from jax import lax
from jax.experimental import pallas as pl
from jax.experimental.pallas import tpu as pltpu
from jax.sharding import PartitionSpec as P

CAP = 2
F32, BF16, I32 = jnp.float32, jnp.bfloat16, jnp.int32
FRESH = 16
STAY_BATCH, LEAVE_BATCH = 76, 26
VMEM = pl.BlockSpec(memory_space=pltpu.VMEM)
SMEM = pl.BlockSpec(memory_space=pltpu.SMEM)
ANY = pl.BlockSpec(memory_space=pltpu.HBM)


def call(kernel, out_shape, in_specs, scratch=(), flops=0, nbytes=0, exps=0, limit=8):
    single = isinstance(out_shape, jax.ShapeDtypeStruct)
    return pl.pallas_call(
        kernel,
        out_shape=out_shape,
        in_specs=in_specs,
        out_specs=VMEM if single else [VMEM] * len(out_shape),
        scratch_shapes=list(scratch),
        cost_estimate=pl.CostEstimate(
            flops=flops, bytes_accessed=nbytes, transcendentals=exps
        ),
        compiler_params=pltpu.CompilerParams(vmem_limit_bytes=limit << 20),
    )


STAY_SLOT, STAY_LENGTH, LEAVE_SLOT, LEAVE_ENTRY, LEAVE_LENGTH, STAY_COUNT = range(6)


def lanes(rows, columns):
    return lax.broadcasted_iota(I32, (rows, columns), 1)


def lines_of(rows, columns):
    return lax.broadcasted_iota(I32, (rows, columns), 0)


def upright(row):
    n = row.shape[1]
    return jnp.sum(jnp.where(lanes(n, n) == lines_of(n, n), row, 0.0), axis=1, keepdims=True)


def plan_kernel(moves_hbm, flags_hbm, lengths_hbm, table_ref, plan_ref, moves_ref, flags_ref, lengths_ref, sem):
    copies = [
        pltpu.make_async_copy(src, dst, sem.at[i])
        for i, (src, dst) in enumerate(
            ((moves_hbm, moves_ref), (flags_hbm, flags_ref), (lengths_hbm, lengths_ref))
        )
    ]
    for copy in copies:
        copy.start()
    for copy in copies:
        copy.wait()
    groups, wide = table_ref.shape
    moves, slots = moves_ref.shape[1], flags_ref.shape[1]
    source, target = moves_ref[0:1, :], moves_ref[1:2, :]
    slot = (moves_ref[2:3, :] + 1).astype(F32)
    hit = lines_of(groups, moves) == target
    earlier = (lines_of(moves, moves) < lanes(moves, moves)).astype(F32)
    before = jnp.dot(hit.astype(F32), earlier, preferred_element_type=F32).astype(I32)
    table = jnp.zeros((groups, wide), I32)
    for c in range(CAP):
        entry = jnp.sum(jnp.where(hit & (before == c), slot, 0.0), axis=1, keepdims=True)
        table = jnp.where(lanes(groups, wide) == c, entry.astype(I32), table)
    table_ref[...] = table

    place = jnp.sum(jnp.where(hit, lines_of(groups, moves) * CAP + before, 0).astype(F32), axis=0, keepdims=True)
    lengths = lengths_ref[...].astype(F32)
    taken = (upright(source.astype(F32)).astype(I32) == lanes(moves, slots)).astype(F32)
    leave_length = jnp.sum(taken * lengths, axis=1, keepdims=True)
    leave_length = jnp.sum(
        jnp.where(lanes(moves, moves) == lines_of(moves, moves), leave_length, 0.0), axis=0, keepdims=True
    )
    gone = jnp.sum(taken, axis=0, keepdims=True)
    stays = ((flags_ref[...] == 0) & (gone == 0.0)).astype(F32)
    rank = jnp.sum(jnp.where(lanes(slots, slots) < lines_of(slots, slots), stays, 0.0), axis=1, keepdims=True)
    chosen = (rank.astype(I32) == lanes(slots, slots)) & (upright(stays) > 0.0)
    listed = jnp.sum(jnp.where(chosen, lines_of(slots, slots).astype(F32), 0.0), axis=0, keepdims=True)
    listed_length = jnp.sum(jnp.where(chosen, upright(lengths), 0.0), axis=0, keepdims=True)
    plan_ref[...] = jnp.zeros(plan_ref.shape, I32)
    plan_ref[STAY_SLOT : STAY_SLOT + 1, :] = listed.astype(I32)
    plan_ref[STAY_LENGTH : STAY_LENGTH + 1, :] = listed_length.astype(I32)
    plan_ref[LEAVE_SLOT : LEAVE_SLOT + 1, 0:moves] = source
    plan_ref[LEAVE_ENTRY : LEAVE_ENTRY + 1, 0:moves] = place.astype(I32)
    plan_ref[LEAVE_LENGTH : LEAVE_LENGTH + 1, 0:moves] = leave_length.astype(I32)
    plan_ref[STAY_COUNT : STAY_COUNT + 1, 0:1] = jnp.sum(stays, axis=1, keepdims=True).astype(I32)


HERE_ENTRY, HERE_SLOT = range(2)


def payload_kernel(slot_ref, table_ref, fresh_ref, out_ref, here_ref):
    for e in range(out_ref.shape[0]):
        out_ref[e] = fresh_ref[jnp.maximum(slot_ref[e // CAP, e % CAP] - 1, 0)]
    groups, width = table_ref.shape
    table = table_ref[...]
    there = (table > 0).astype(F32)
    earlier = (lanes(groups, groups) < lines_of(groups, groups)).astype(F32)
    before = jnp.dot(earlier, there, preferred_element_type=F32)
    whole = jnp.sum(there, axis=0, keepdims=True)
    entry = jnp.zeros((1, width), F32)
    slot = jnp.zeros((1, width), F32)
    base = jnp.zeros((1, 1), F32)
    for c in range(CAP):
        rank = (before[:, c : c + 1] + base).astype(I32)
        chosen = (rank == lanes(groups, width)) & (there[:, c : c + 1] > 0.0)
        entry += jnp.sum(jnp.where(chosen, (lines_of(groups, width) * CAP + c).astype(F32), 0.0), axis=0, keepdims=True)
        slot += jnp.sum(jnp.where(chosen, (table[:, c : c + 1] - 1).astype(F32), 0.0), axis=0, keepdims=True)
        base = base + whole[:, c : c + 1]
    here_ref[...] = jnp.zeros(here_ref.shape, I32)
    here_ref[HERE_ENTRY : HERE_ENTRY + 1, :] = entry.astype(I32)
    here_ref[HERE_SLOT : HERE_SLOT + 1, :] = slot.astype(I32)


def attend(rows, batch, kbuf, vbuf, score, weight, cache, steps, heads, row_of, query_of, fresh_of, length_of, await_keys, await_values, put):
    positions, head = kbuf.shape[1:]
    lines = heads * steps

    def fresh_rows(value):
        pad = jnp.zeros((FRESH - steps, head), F32)
        return jnp.concatenate([value.astype(F32), pad], axis=0).astype(BF16)

    def scores(b, carry):
        lane = lanes(lines, positions)
        step = lax.rem(lines_of(lines, positions), steps)
        visible = (lane >= cache) & (lane - cache <= step)
        for u in range(batch):
            i = b * batch + u
            fresh_key, fresh_value = fresh_of(i)
            kbuf[row_of(i), cache:positions, :] = fresh_rows(fresh_key)
            vbuf[row_of(i), cache:positions, :] = fresh_rows(fresh_value)
        for u in range(batch):
            i = b * batch + u
            query = query_of(i).astype(F32)
            query = jnp.concatenate([query[:, h * head : (h + 1) * head] for h in range(heads)], axis=0)
            products = lax.dot_general(
                query.astype(BF16), kbuf[row_of(i)], (((1,), (1,)), ((), ())), preferred_element_type=F32
            )
            score[pl.ds(pl.multiple_of(i * lines, lines), lines), :] = jnp.where(
                (lane < length_of(i)) | visible, products * head**-0.5, -jnp.inf
            )
        return carry

    await_keys()
    lax.fori_loop(0, rows // batch, scores, 0)

    def soften(b, carry):
        chunk = pl.ds(pl.multiple_of(b * batch * lines, lines), batch * lines)
        s = score[chunk, :]
        e = jnp.exp(s - jnp.max(s, axis=1, keepdims=True))
        weight[chunk, :] = (e * (1.0 / jnp.sum(e, axis=1, keepdims=True))).astype(BF16)
        return carry

    lax.fori_loop(0, rows // batch, soften, 0)

    def mix(b, carry):
        mixed = []
        for u in range(batch):
            i = b * batch + u
            mixed.append(
                jnp.dot(
                    weight[pl.ds(pl.multiple_of(i * lines, lines), lines), :],
                    vbuf[row_of(i)],
                    preferred_element_type=F32,
                )
            )
        put(b, mixed)
        return carry

    await_values()
    lax.fori_loop(0, rows // batch, mix, 0)


def staying_kernel(
    place_ref, plan_ref, query_ref, key_ref, value_ref, keys_ref, values_ref, weight_ref,
    up_ref, down_ref, own_ref, *rest,
):
    terms_refs, fresh_ref = rest[:6], rest[6]
    kbuf, vbuf, score, weight, heads, wbuf, fsem, ksem, vsem, wsem = rest[7:]
    steps, wide = query_ref.shape[1:]
    slots, _, cache, head = keys_ref.shape
    tokens = heads.shape[0]
    ring, columns = 8, up_ref.shape[1]
    fresh = [
        pltpu.make_async_copy(src, fresh_ref.at[:, :, pl.ds(at, src.shape[2])], fsem.at[i])
        for i, (src, at) in enumerate(((query_ref, 0), (key_ref, wide), (value_ref, wide + head)))
    ]
    keys, values = (
        [
            pltpu.make_async_copy(
                ref.at[pl.ds(c * 32, 32), 0], buf.at[pl.ds(c * 32, 32), pl.ds(0, cache)], sem.at[c]
            )
            for c in range(slots // 32)
        ]
        for ref, buf, sem in ((keys_ref, kbuf, ksem), (values_ref, vbuf, vsem))
    )
    order = (4, 3, 5, 2, 6, 1, 7, 0)

    def part(k):
        at = lax.rem(place_ref[0] + k, ring) * columns
        return pl.ds(pl.multiple_of(at, columns), columns)

    parts = [pltpu.make_async_copy(weight_ref.at[:, part(k)], wbuf.at[j], wsem.at[j]) for j, k in enumerate(order)]
    for copy in fresh + keys + values + parts:
        copy.start()

    def put(b, mixed):
        quads = len(mixed) // 4
        for j in range(quads):
            four = mixed[4 * j : 4 * j + 4]
            for h in range(wide // head):
                tile = jnp.concatenate([o[h * steps : (h + 1) * steps] for o in four], axis=0)
                at = pl.ds(pl.multiple_of((b * quads + j) * 16, 16), 16)
                heads[at, h * head : (h + 1) * head] = tile.astype(BF16)

    def slot(i):
        return plan_ref[STAY_SLOT, i]

    for copy in fresh:
        copy.wait()
    attend(
        tokens // steps, STAY_BATCH, kbuf, vbuf, score, weight, cache, steps, wide // head,
        slot,
        lambda i: fresh_ref[slot(i), :, 0:wide],
        lambda i: (fresh_ref[slot(i), :, wide : wide + head], fresh_ref[slot(i), :, wide + head : wide + 2 * head]),
        lambda i: plan_ref[STAY_LENGTH, i],
        lambda: [copy.wait() for copy in keys],
        lambda: [copy.wait() for copy in values],
        put,
    )
    cut = up_ref.shape[0]
    for j, k in enumerate(order):
        parts[j].wait()
        block = jnp.dot(heads[...], wbuf[j], preferred_element_type=F32)
        if k == ring // 2:
            up_ref[...] = block[:cut].astype(BF16)
            down_ref[...] = block[cut:].astype(BF16)
        elif k == 0:
            own_ref[...] = block
        else:
            terms_refs[k - 1 if k < 4 else k - 2][...] = block.astype(BF16)


def leaving_kernel(plan_ref, asked_ref, keys_ref, values_ref, out_ref, kbuf, vbuf, score, weight, ksem, vsem):
    rows, cache, head = kbuf.shape[0], keys_ref.shape[2], keys_ref.shape[3]
    steps, wide = out_ref.shape[1:]
    loads = [
        [
            pltpu.make_async_copy(ref.at[plan_ref[LEAVE_SLOT, i], 0], buf.at[i, pl.ds(0, cache)], sem.at[i])
            for i in range(rows)
        ]
        for ref, buf, sem in ((keys_ref, kbuf, ksem), (values_ref, vbuf, vsem))
    ]
    for copy in loads[0] + loads[1]:
        copy.start()
    out_ref[...] = jnp.zeros(out_ref.shape, BF16)

    def entry(i):
        return plan_ref[LEAVE_ENTRY, i]

    def put(b, mixed):
        for u, o in enumerate(mixed):
            at = entry(b * LEAVE_BATCH + u)
            for h in range(wide // head):
                out_ref[at, :, h * head : (h + 1) * head] = o[h * steps : (h + 1) * steps].astype(BF16)

    attend(
        rows, LEAVE_BATCH, kbuf, vbuf, score, weight, cache, steps, wide // head,
        lambda i: i,
        lambda i: asked_ref[entry(i), :, 0:wide],
        lambda i: (asked_ref[entry(i), :, wide : wide + head], asked_ref[entry(i), :, wide + head : wide + 2 * head]),
        lambda i: plan_ref[LEAVE_LENGTH, i],
        lambda: [copy.wait() for copy in loads[0]],
        lambda: [copy.wait() for copy in loads[1]],
        put,
    )


def arrived_kernel(here_ref, back_ref, weight_ref, out_ref, heads, wbuf, wsem):
    steps = back_ref.shape[1]
    rows, columns = out_ref.shape[1] // steps, out_ref.shape[2]
    parts = [
        pltpu.make_async_copy(weight_ref.at[:, pl.ds(k * columns, columns)], wbuf.at[k], wsem.at[k])
        for k in range(out_ref.shape[0])
    ]
    for copy in parts:
        copy.start()
    for j in range(heads.shape[0] // 16):
        four = [back_ref[here_ref[HERE_ENTRY, min(4 * j + u, rows - 1)]].astype(F32) for u in range(4)]
        heads[16 * j : 16 * j + 16, :] = jnp.concatenate(four, axis=0).astype(BF16)
    for k, copy in enumerate(parts):
        copy.wait()
        terms = jnp.dot(heads[...], wbuf[k], preferred_element_type=F32)
        out_ref[k] = terms[: out_ref.shape[1]].astype(BF16)


def place_kernel(plan_ref, own_ref, up_ref, down_ref, out_ref, total):
    steps = out_ref.shape[1]
    total[...] = own_ref[...] + up_ref[...].astype(F32) + down_ref[...].astype(F32)
    out_ref[...] = jnp.zeros(out_ref.shape, BF16)
    for i in range(own_ref.shape[0] // steps):

        @pl.when(i < plan_ref[STAY_COUNT, 0])
        def _():
            out_ref[plan_ref[STAY_SLOT, i]] = total[i * steps : (i + 1) * steps, :].astype(BF16)


def finish_kernel(here_ref, placed_ref, blocks_ref, out_ref, total):
    steps = out_ref.shape[1]
    out_ref[...] = placed_ref[...]
    terms = blocks_ref[0].astype(F32)
    for k in range(1, blocks_ref.shape[0]):
        terms = terms + blocks_ref[k].astype(F32)
    total[...] = terms
    for n in range(blocks_ref.shape[1] // steps):
        out_ref[here_ref[HERE_SLOT, n]] = total[n * steps : (n + 1) * steps, :].astype(BF16)


def on_device(
    keys_cache,
    values_cache,
    lengths,
    guard_flags,
    migrations,
    queries,
    new_keys,
    new_values,
    out_weight,
):
    shape = jax.ShapeDtypeStruct
    slots, _, cache, head = keys_cache.shape
    steps, wide = queries.shape[1:]
    moves = migrations.shape[0]
    groups, ring = lax.axis_size("group"), lax.axis_size("tp")
    columns = out_weight.shape[1] // ring
    entries = groups * CAP
    staying = slots - 2 * moves
    lines = wide // head * steps
    positions = cache + FRESH
    place = lax.axis_index("tp").astype(I32).reshape(1)
    barrier = lax.optimization_barrier
    keys_cache, values_cache, out_weight, queries, new_keys, new_values, moves_t, flags, reach = (
        pltpu.with_memory_space_constraint(x, pltpu.HBM)
        for x in (
            keys_cache, values_cache, out_weight, queries, new_keys, new_values,
            migrations.T, guard_flags.reshape(1, slots), lengths.reshape(1, slots),
        )
    )

    def exchange(x, axis):
        return lax.all_to_all(x, axis, split_axis=0, concat_axis=0, tiled=True)

    def scratch(held, rows):
        return [
            pltpu.VMEM((held, positions, head), BF16),
            pltpu.VMEM((held, positions, head), BF16),
            pltpu.VMEM((rows * lines, positions), F32),
            pltpu.VMEM((rows * lines, positions), BF16),
        ]

    table, plan = call(
        plan_kernel,
        [shape((groups, 128), I32), shape((8, slots), I32)],
        [ANY] * 3,
        [
            pltpu.VMEM((3, moves), I32),
            pltpu.VMEM((1, slots), I32),
            pltpu.VMEM((1, slots), I32),
            pltpu.SemaphoreType.DMA((3,)),
        ],
        nbytes=1 << 16,
    )(moves_t, flags, reach)
    table = exchange(table.reshape(groups, 1, 128), "group").reshape(groups, 128)

    tokens = staying * steps
    cut = -(-tokens // 32) * 16
    up, down, own, *terms = call(
        staying_kernel,
        [shape((cut, columns), BF16), shape((tokens - cut, columns), BF16), shape((tokens, columns), F32)]
        + [shape((tokens, columns), BF16)] * 6
        + [shape((slots, steps, wide + 2 * head), BF16)],
        [SMEM] * 2 + [ANY] * 6,
        scratch(slots, staying)
        + [
            pltpu.VMEM((tokens, wide), BF16),
            pltpu.VMEM((ring, wide, columns), BF16),
            pltpu.SemaphoreType.DMA((3,)),
            pltpu.SemaphoreType.DMA((slots // 32,)),
            pltpu.SemaphoreType.DMA((slots // 32,)),
            pltpu.SemaphoreType.DMA((ring,)),
        ],
        flops=2 * tokens * wide * out_weight.shape[1],
        nbytes=20 << 20,
        exps=tokens * positions * 4,
        limit=32,
    )(place, plan, queries, new_keys, new_values, keys_cache, values_cache, out_weight)
    fresh = terms.pop()

    ahead = [(i, (i + 1) % ring) for i in range(ring)]
    astern = [(i, (i - 1) % ring) for i in range(ring)]

    def hop(u, d):
        return lax.ppermute(u, "tp", ahead), lax.ppermute(d, "tp", astern)

    def add(k, u, d):
        return (
            (terms[k - 1].astype(F32) + u.astype(F32)).astype(BF16),
            (terms[6 - k].astype(F32) + d.astype(F32)).astype(BF16),
        )

    table, up, down, fresh = barrier((table, up, down, fresh))
    asked, here = call(
        payload_kernel,
        [shape((entries, steps, wide + 2 * head), BF16), shape((8, 128), I32)],
        [SMEM] + [VMEM] * 2,
        nbytes=2 << 20,
    )(table, table, fresh)
    asked = exchange(asked, "group")
    up, down = hop(up, down)
    up = jnp.concatenate([up, jnp.zeros((tokens - cut, columns), BF16)], axis=0)
    down = jnp.concatenate([jnp.zeros((cut, columns), BF16), down], axis=0)

    asked, up, down = barrier((asked, *add(3, up, down)))
    up, down = hop(up, down)
    back = call(
        leaving_kernel,
        shape((entries, steps, wide), BF16),
        [SMEM] + [VMEM] + [ANY] * 2,
        scratch(moves, moves) + [pltpu.SemaphoreType.DMA((moves,)), pltpu.SemaphoreType.DMA((moves,))],
        nbytes=8 << 20,
    )(plan, asked, keys_cache, values_cache)
    back = exchange(back, "group")
    back, up, down = barrier((back, *add(2, up, down)))
    up, down = hop(up, down)
    arrived = moves * steps
    blocks = call(
        arrived_kernel,
        shape((ring, arrived, columns), BF16),
        [SMEM, VMEM, ANY],
        [
            pltpu.VMEM((-(-arrived // 16) * 16, wide), BF16),
            pltpu.VMEM((ring, wide, columns), BF16),
            pltpu.SemaphoreType.DMA((ring,)),
        ],
        nbytes=6 << 20,
        limit=12,
    )(here, back, out_weight)
    blocks, up, down = barrier((blocks, *add(1, up, down)))
    blocks = exchange(blocks, "tp")
    up, down = hop(up, down)

    placed = call(
        place_kernel,
        shape((slots, steps, columns), BF16),
        [SMEM] + [VMEM] * 3,
        [pltpu.VMEM((tokens, columns), F32)],
        nbytes=4 << 20,
    )(plan, own, up, down)
    return call(
        finish_kernel,
        shape((slots, steps, columns), BF16),
        [SMEM] + [VMEM] * 2,
        [pltpu.VMEM((arrived, columns), F32)],
        nbytes=2 << 20,
    )(here, placed, blocks)


def solution(mesh):
    return jax.shard_map(
        on_device,
        mesh=mesh,
        in_specs=(
            P("group", "tp", None, None),
            P("group", "tp", None, None),
            P("group"),
            P("group"),
            P("group", None),
            P("group", None, "tp"),
            P("group", None, "tp"),
            P("group", None, "tp"),
            P("tp", None),
        ),
        out_specs=P("group", None, "tp"),
        check_vma=False,
    )
```

```python
import functools

import jax
import jax.numpy as jnp
from jax import lax
from jax.experimental import pallas as pl
from jax.experimental.pallas import tpu as pltpu
from jax.sharding import PartitionSpec as P

CAP = 2
F32, BF16, I32 = jnp.float32, jnp.bfloat16, jnp.int32
FRESH = 16
VMEM = pl.BlockSpec(memory_space=pltpu.VMEM)
SMEM = pl.BlockSpec(memory_space=pltpu.SMEM)
ANY = pl.BlockSpec(memory_space=pltpu.HBM)


def call(kernel, out_shape, in_specs, scratch=(), flops=0, nbytes=0, exps=0, limit=8):
    single = isinstance(out_shape, jax.ShapeDtypeStruct)
    return pl.pallas_call(
        kernel,
        out_shape=out_shape,
        in_specs=in_specs,
        out_specs=VMEM if single else [VMEM] * len(out_shape),
        scratch_shapes=list(scratch),
        cost_estimate=pl.CostEstimate(
            flops=flops, bytes_accessed=nbytes, transcendentals=exps
        ),
        compiler_params=pltpu.CompilerParams(vmem_limit_bytes=limit << 20),
    )


STAY_SLOT, STAY_LENGTH, LEAVE_SLOT, LEAVE_ENTRY, LEAVE_LENGTH, STAY_FIRST = range(6)


def lanes(rows, columns):
    return lax.broadcasted_iota(I32, (rows, columns), 1)


def lines_of(rows, columns):
    return lax.broadcasted_iota(I32, (rows, columns), 0)


def upright(row):
    n = row.shape[1]
    return jnp.sum(jnp.where(lanes(n, n) == lines_of(n, n), row, 0.0), axis=1, keepdims=True)


def plan_kernel(moves_hbm, flags_hbm, lengths_hbm, table_ref, plan_ref, moves_ref, flags_ref, lengths_ref, sem):
    copies = [
        pltpu.make_async_copy(src, dst, sem.at[i])
        for i, (src, dst) in enumerate(
            ((moves_hbm, moves_ref), (flags_hbm, flags_ref), (lengths_hbm, lengths_ref))
        )
    ]
    for copy in copies:
        copy.start()
    for copy in copies:
        copy.wait()
    groups, wide = table_ref.shape
    moves, slots = moves_ref.shape[1], flags_ref.shape[1]
    source, target = moves_ref[0:1, :], moves_ref[1:2, :]
    slot = (moves_ref[2:3, :] + 1).astype(F32)
    hit = lines_of(groups, moves) == target
    earlier = (lines_of(moves, moves) < lanes(moves, moves)).astype(F32)
    before = jnp.dot(hit.astype(F32), earlier, preferred_element_type=F32).astype(I32)
    table = jnp.zeros((groups, wide), I32)
    for c in range(CAP):
        entry = jnp.sum(jnp.where(hit & (before == c), slot, 0.0), axis=1, keepdims=True)
        table = jnp.where(lanes(groups, wide) == c, entry.astype(I32), table)
    table_ref[...] = table

    place = jnp.sum(jnp.where(hit, lines_of(groups, moves) * CAP + before, 0).astype(F32), axis=0, keepdims=True)
    lengths = lengths_ref[...].astype(F32)
    taken = (upright(source.astype(F32)).astype(I32) == lanes(moves, slots)).astype(F32)
    leave_length = jnp.sum(taken * lengths, axis=1, keepdims=True)
    leave_length = jnp.sum(
        jnp.where(lanes(moves, moves) == lines_of(moves, moves), leave_length, 0.0), axis=0, keepdims=True
    )
    gone = jnp.sum(taken, axis=0, keepdims=True)
    stays = ((flags_ref[...] == 0) & (gone == 0.0)).astype(F32)
    rank = jnp.sum(jnp.where(lanes(slots, slots) < lines_of(slots, slots), stays, 0.0), axis=1, keepdims=True)
    first = slots - 2 * moves - jnp.sum(stays, axis=1, keepdims=True)
    chosen = ((rank + first).astype(I32) == lanes(slots, slots)) & (upright(stays) > 0.0)
    listed = jnp.sum(jnp.where(chosen, lines_of(slots, slots).astype(F32), 0.0), axis=0, keepdims=True)
    listed_length = jnp.sum(jnp.where(chosen, upright(lengths), 0.0), axis=0, keepdims=True)
    plan_ref[...] = jnp.zeros(plan_ref.shape, I32)
    plan_ref[STAY_SLOT : STAY_SLOT + 1, :] = listed.astype(I32)
    plan_ref[STAY_LENGTH : STAY_LENGTH + 1, :] = listed_length.astype(I32)
    plan_ref[LEAVE_SLOT : LEAVE_SLOT + 1, 0:moves] = source
    plan_ref[LEAVE_ENTRY : LEAVE_ENTRY + 1, 0:moves] = place.astype(I32)
    plan_ref[LEAVE_LENGTH : LEAVE_LENGTH + 1, 0:moves] = leave_length.astype(I32)
    plan_ref[STAY_FIRST : STAY_FIRST + 1, 0:1] = first.astype(I32)


HERE_ENTRY, HERE_SLOT = range(2)


def payload_kernel(slot_ref, table_ref, fresh_ref, out_ref, here_ref):
    for e in range(out_ref.shape[0]):
        out_ref[e] = fresh_ref[jnp.maximum(slot_ref[e // CAP, e % CAP] - 1, 0)]
    groups, width = table_ref.shape
    table = table_ref[...]
    there = (table > 0).astype(F32)
    earlier = (lanes(groups, groups) < lines_of(groups, groups)).astype(F32)
    before = jnp.dot(earlier, there, preferred_element_type=F32)
    whole = jnp.sum(there, axis=0, keepdims=True)
    entry = jnp.zeros((1, width), F32)
    slot = jnp.zeros((1, width), F32)
    base = jnp.zeros((1, 1), F32)
    for c in range(CAP):
        rank = (before[:, c : c + 1] + base).astype(I32)
        chosen = (rank == lanes(groups, width)) & (there[:, c : c + 1] > 0.0)
        entry += jnp.sum(jnp.where(chosen, (lines_of(groups, width) * CAP + c).astype(F32), 0.0), axis=0, keepdims=True)
        slot += jnp.sum(jnp.where(chosen, (table[:, c : c + 1] - 1).astype(F32), 0.0), axis=0, keepdims=True)
        base = base + whole[:, c : c + 1]
    here_ref[...] = jnp.zeros(here_ref.shape, I32)
    here_ref[HERE_ENTRY : HERE_ENTRY + 1, :] = entry.astype(I32)
    here_ref[HERE_SLOT : HERE_SLOT + 1, :] = slot.astype(I32)


def attend(batches, kbuf, vbuf, score, weight, cache, steps, heads, row_of, query_of, fresh_of, length_of, await_keys, await_values):
    positions, head = kbuf.shape[1:]
    lines = heads * steps
    lane = lanes(lines, positions)
    step = lax.rem(lines_of(lines, positions), steps)
    visible = (lane >= cache) & (lane - cache <= step)

    def fresh_rows(value):
        pad = jnp.zeros((FRESH - steps, head), F32)
        return jnp.concatenate([value.astype(F32), pad], axis=0).astype(BF16)

    for b, batch in enumerate(batches):
        for i in batch:
            fresh_key, fresh_value = fresh_of(i)
            kbuf[row_of(i), cache:positions, :] = fresh_rows(fresh_key)
            vbuf[row_of(i), cache:positions, :] = fresh_rows(fresh_value)
        await_keys(b)
        for i in batch:
            query = query_of(i).astype(F32)
            query = jnp.concatenate([query[:, h * head : (h + 1) * head] for h in range(heads)], axis=0)
            products = lax.dot_general(
                query.astype(BF16), kbuf[row_of(i)], (((1,), (1,)), ((), ())), preferred_element_type=F32
            )
            score[i * lines : (i + 1) * lines, :] = jnp.where(
                (lane < length_of(i)) | visible, products * head**-0.5, -jnp.inf
            )
    for batch in batches:
        chunk = slice(batch[0] * lines, (batch[-1] + 1) * lines)
        s = score[chunk, :]
        e = jnp.exp(s - jnp.max(s, axis=1, keepdims=True))
        weight[chunk, :] = (e * (1.0 / jnp.sum(e, axis=1, keepdims=True))).astype(BF16)
    mixed = []
    for b, batch in enumerate(batches):
        await_values(b)
        for i in batch:
            mixed.append(
                jnp.dot(weight[i * lines : (i + 1) * lines, :], vbuf[row_of(i)], preferred_element_type=F32)
            )
    return mixed


def staying_kernel(
    place_ref, plan_ref, query_ref, key_ref, value_ref, keys_ref, values_ref, weight_ref,
    up_ref, down_ref, heads_ref, fresh_ref, leave_keys_ref, leave_values_ref,
    kbuf, vbuf, score, weight, wbuf, fsem, ksem, vsem, wsem,
):
    steps, wide = query_ref.shape[1:]
    slots, _, cache, head = keys_ref.shape
    tokens, columns = heads_ref.shape[0], up_ref.shape[1]
    rows, ring = tokens // steps, weight_ref.shape[1] // columns
    chunk = slots // ksem.shape[0]
    fresh = [
        pltpu.make_async_copy(src, fresh_ref.at[:, :, pl.ds(at, src.shape[2])], fsem.at[i])
        for i, (src, at) in enumerate(((query_ref, 0), (key_ref, wide), (value_ref, wide + head)))
    ]
    keys, values = (
        [
            pltpu.make_async_copy(
                ref.at[pl.ds(c * chunk, chunk), 0], buf.at[pl.ds(c * chunk, chunk), pl.ds(0, cache)], sem.at[c]
            )
            for c in range(slots // chunk)
        ]
        for ref, buf, sem in ((keys_ref, kbuf, ksem), (values_ref, vbuf, vsem))
    )
    at = lax.rem(place_ref[0] + ring // 2, ring) * columns
    far = pltpu.make_async_copy(weight_ref.at[:, pl.ds(pl.multiple_of(at, columns), columns)], wbuf, wsem)
    for copy in fresh + keys + values + [far]:
        copy.start()

    last = [(slots - rows + i) // chunk for i in range(rows)]
    batches = [[i for i in range(rows) if last[i] == c] for c in sorted(set(last))]
    due = [[c for c in range(slots // chunk) if c <= last[b[0]] and (j == 0 or c > last[batches[j - 1][0]])] for j, b in enumerate(batches)]

    def slot(i):
        return plan_ref[STAY_SLOT, i]

    for copy in fresh:
        copy.wait()
    mixed = attend(
        batches, kbuf, vbuf, score, weight, cache, steps, wide // head,
        slot,
        lambda i: fresh_ref[slot(i), :, 0:wide],
        lambda i: (fresh_ref[slot(i), :, wide : wide + head], fresh_ref[slot(i), :, wide + head : wide + 2 * head]),
        lambda i: plan_ref[STAY_LENGTH, i],
        lambda b: [keys[c].wait() for c in due[b]],
        lambda b: [values[c].wait() for c in due[b]],
    )
    for j in range(rows // 4):
        for h in range(wide // head):
            tile = jnp.concatenate([o[h * steps : (h + 1) * steps] for o in mixed[4 * j : 4 * j + 4]], axis=0)
            heads_ref[16 * j : 16 * j + 16, h * head : (h + 1) * head] = tile.astype(BF16)
    for i in range(leave_keys_ref.shape[0]):
        leave_keys_ref[i] = kbuf[plan_ref[LEAVE_SLOT, i], 0:cache, :]
        leave_values_ref[i] = vbuf[plan_ref[LEAVE_SLOT, i], 0:cache, :]
    far.wait()
    cut = up_ref.shape[0]
    block = jnp.dot(heads_ref[...], wbuf[...], preferred_element_type=F32)
    up_ref[...] = block[:cut].astype(BF16)
    down_ref[...] = block[cut:].astype(BF16)


def terms_kernel(place_ref, heads_ref, weight_ref, own_ref, *rest):
    terms_refs, wout, wsem = rest[:6], rest[6], rest[7]
    ring, _, columns = wout.shape

    def part(k):
        at = lax.rem(place_ref[0] + k, ring) * columns
        return pl.ds(pl.multiple_of(at, columns), columns)

    order = (3, 5, 2, 6, 1, 7, 0, 4)
    parts = [pltpu.make_async_copy(weight_ref.at[:, part(k)], wout.at[k], wsem.at[k]) for k in order]
    for copy in parts:
        copy.start()
    for k, copy in zip(order, parts):
        copy.wait()
        if k == ring // 2:
            continue
        block = jnp.dot(heads_ref[...], wout[k], preferred_element_type=F32)
        if k == 0:
            own_ref[...] = block
        else:
            terms_refs[k - 1 if k < 4 else k - 2][...] = block.astype(BF16)


def leaving_kernel(plan_ref, asked_ref, keys_ref, values_ref, out_ref, kbuf, vbuf, score, weight):
    rows, cache, head = keys_ref.shape
    steps, wide = out_ref.shape[1:]
    out_ref[...] = jnp.zeros(out_ref.shape, BF16)
    for i in range(rows):
        kbuf[i, 0:cache, :] = keys_ref[i]
        vbuf[i, 0:cache, :] = values_ref[i]

    def entry(i):
        return plan_ref[LEAVE_ENTRY, i]

    mixed = attend(
        [list(range(rows))], kbuf, vbuf, score, weight, cache, steps, wide // head,
        lambda i: i,
        lambda i: asked_ref[entry(i), :, 0:wide],
        lambda i: (asked_ref[entry(i), :, wide : wide + head], asked_ref[entry(i), :, wide + head : wide + 2 * head]),
        lambda i: plan_ref[LEAVE_LENGTH, i],
        lambda b: None,
        lambda b: None,
    )
    for i, o in enumerate(mixed):
        for h in range(wide // head):
            out_ref[entry(i), :, h * head : (h + 1) * head] = o[h * steps : (h + 1) * steps].astype(BF16)


def arrived_kernel(place_ref, here_ref, back_ref, weight_ref, out_ref, heads):
    steps = back_ref.shape[1]
    ring, lines, _ = out_ref.shape
    rows = lines // steps
    for j in range(heads.shape[0] // 16):
        four = [back_ref[here_ref[HERE_ENTRY, min(4 * j + u, rows - 1)]].astype(F32) for u in range(4)]
        heads[16 * j : 16 * j + 16, :] = jnp.concatenate(four, axis=0).astype(BF16)
    for k in range(ring):
        terms = jnp.dot(heads[...], weight_ref[k], preferred_element_type=F32)
        out_ref[lax.rem(place_ref[0] + k, ring)] = terms[:lines].astype(BF16)


def place_kernel(plan_ref, own_ref, up_ref, down_ref, out_ref, total):
    steps = out_ref.shape[1]
    total[...] = own_ref[...] + up_ref[...].astype(F32) + down_ref[...].astype(F32)
    out_ref[...] = jnp.zeros(out_ref.shape, BF16)
    for i in range(own_ref.shape[0] // steps):

        @pl.when(i >= plan_ref[STAY_FIRST, 0])
        def _():
            out_ref[plan_ref[STAY_SLOT, i]] = total[i * steps : (i + 1) * steps, :].astype(BF16)


def finish_kernel(here_ref, placed_ref, blocks_ref, out_ref, total):
    steps = out_ref.shape[1]
    out_ref[...] = placed_ref[...]
    terms = blocks_ref[0].astype(F32)
    for k in range(1, blocks_ref.shape[0]):
        terms = terms + blocks_ref[k].astype(F32)
    total[...] = terms
    for n in range(blocks_ref.shape[1] // steps):
        out_ref[here_ref[HERE_SLOT, n]] = total[n * steps : (n + 1) * steps, :].astype(BF16)


def on_device(
    keys_cache,
    values_cache,
    lengths,
    guard_flags,
    migrations,
    queries,
    new_keys,
    new_values,
    out_weight,
):
    shape = jax.ShapeDtypeStruct
    slots, _, cache, head = keys_cache.shape
    steps, wide = queries.shape[1:]
    moves = migrations.shape[0]
    groups, ring = lax.axis_size("group"), lax.axis_size("tp")
    columns = out_weight.shape[1] // ring
    entries = groups * CAP
    staying = slots - 2 * moves
    lines = wide // head * steps
    positions = cache + FRESH
    place = lax.axis_index("tp").astype(I32).reshape(1)
    barrier = lax.optimization_barrier
    keys_cache, values_cache, out_weight, queries, new_keys, new_values, moves_t, flags, reach = (
        pltpu.with_memory_space_constraint(x, pltpu.HBM)
        for x in (
            keys_cache, values_cache, out_weight, queries, new_keys, new_values,
            migrations.T, guard_flags.reshape(1, slots), lengths.reshape(1, slots),
        )
    )

    def exchange(x, axis):
        return lax.all_to_all(x, axis, split_axis=0, concat_axis=0, tiled=True)

    def scratch(held, rows):
        return [
            pltpu.VMEM((held, positions, head), BF16),
            pltpu.VMEM((held, positions, head), BF16),
            pltpu.VMEM((rows * lines, positions), F32),
            pltpu.VMEM((rows * lines, positions), BF16),
        ]

    table, plan = call(
        plan_kernel,
        [shape((groups, 128), I32), shape((8, slots), I32)],
        [ANY] * 3,
        [
            pltpu.VMEM((3, moves), I32),
            pltpu.VMEM((1, slots), I32),
            pltpu.VMEM((1, slots), I32),
            pltpu.SemaphoreType.DMA((3,)),
        ],
        nbytes=1 << 16,
    )(moves_t, flags, reach)
    table = exchange(table.reshape(groups, 1, 128), "group").reshape(groups, 128)

    tokens = staying * steps
    cut = -(-tokens // 32) * 16
    up, down, heads, fresh, leave_keys, leave_values = call(
        staying_kernel,
        [
            shape((cut, columns), BF16),
            shape((tokens - cut, columns), BF16),
            shape((tokens, wide), BF16),
            shape((slots, steps, wide + 2 * head), BF16),
            shape((moves, cache, head), BF16),
            shape((moves, cache, head), BF16),
        ],
        [SMEM] * 2 + [ANY] * 6,
        scratch(slots, staying)
        + [
            pltpu.VMEM((wide, columns), BF16),
            pltpu.SemaphoreType.DMA((3,)),
            pltpu.SemaphoreType.DMA((4,)),
            pltpu.SemaphoreType.DMA((4,)),
            pltpu.SemaphoreType.DMA,
        ],
        flops=2 * tokens * wide * columns,
        nbytes=16 << 20,
        exps=tokens * positions * 4,
        limit=24,
    )(place, plan, queries, new_keys, new_values, keys_cache, values_cache, out_weight)

    ahead = [(i, (i + 1) % ring) for i in range(ring)]
    astern = [(i, (i - 1) % ring) for i in range(ring)]

    def hop(u, d):
        return lax.ppermute(u, "tp", ahead), lax.ppermute(d, "tp", astern)

    def add(k, u, d):
        return (
            (terms[k - 1].astype(F32) + u.astype(F32)).astype(BF16),
            (terms[6 - k].astype(F32) + d.astype(F32)).astype(BF16),
        )

    table, up, down, fresh, heads = barrier((table, up, down, fresh, heads))
    asked, here = call(
        payload_kernel,
        [shape((entries, steps, wide + 2 * head), BF16), shape((8, 128), I32)],
        [SMEM] + [VMEM] * 2,
        nbytes=2 << 20,
    )(table, table, fresh)
    asked, heads = barrier((asked, heads))
    asked = exchange(asked, "group")
    own, *terms = call(
        terms_kernel,
        [shape((tokens, columns), F32)]
        + [shape((tokens, columns), BF16)] * 6
        + [shape((ring, wide, columns), BF16)],
        [SMEM, VMEM, ANY],
        [pltpu.SemaphoreType.DMA((ring,))],
        flops=2 * tokens * wide * out_weight.shape[1],
        nbytes=8 << 20,
        limit=10,
    )(place, heads, out_weight)
    weight = terms.pop()
    up, down = hop(up, down)
    up = jnp.concatenate([up, jnp.zeros((tokens - cut, columns), BF16)], axis=0)
    down = jnp.concatenate([jnp.zeros((cut, columns), BF16), down], axis=0)

    asked, up, down = barrier((asked, *add(3, up, down)))
    up, down = hop(up, down)
    back = call(
        leaving_kernel,
        shape((entries, steps, wide), BF16),
        [SMEM] + [VMEM] * 3,
        scratch(moves, moves),
        nbytes=4 << 20,
    )(plan, asked, leave_keys, leave_values)
    back = exchange(back, "group")
    back, up, down = barrier((back, *add(2, up, down)))
    up, down = hop(up, down)
    arrived = moves * steps
    blocks = call(
        arrived_kernel,
        shape((ring, arrived, columns), BF16),
        [SMEM] * 2 + [VMEM] * 2,
        [pltpu.VMEM((-(-arrived // 16) * 16, wide), BF16)],
        nbytes=6 << 20,
    )(place, here, back, weight)
    blocks, up, down = barrier((blocks, *add(1, up, down)))
    blocks = exchange(blocks, "tp")
    up, down = hop(up, down)

    placed = call(
        place_kernel,
        shape((slots, steps, columns), BF16),
        [SMEM] + [VMEM] * 3,
        [pltpu.VMEM((tokens, columns), F32)],
        nbytes=4 << 20,
    )(plan, own, up, down)
    return call(
        finish_kernel,
        shape((slots, steps, columns), BF16),
        [SMEM] + [VMEM] * 2,
        [pltpu.VMEM((arrived, columns), F32)],
        nbytes=2 << 20,
    )(here, placed, blocks)


def solution(mesh):
    return jax.shard_map(
        on_device,
        mesh=mesh,
        in_specs=(
            P("group", "tp", None, None),
            P("group", "tp", None, None),
            P("group"),
            P("group"),
            P("group", None),
            P("group", None, "tp"),
            P("group", None, "tp"),
            P("group", None, "tp"),
            P("tp", None),
        ),
        out_specs=P("group", None, "tp"),
        check_vma=False,
    )
```

```python
import functools

import jax
import jax.numpy as jnp
from jax import lax
from jax.experimental import pallas as pl
from jax.experimental.pallas import tpu as pltpu
from jax.sharding import PartitionSpec as P

CAP = 2
F32, BF16, I32 = jnp.float32, jnp.bfloat16, jnp.int32
FRESH = 16
PAYLOAD_COST, HOP_COST, ARRIVED_COST, PLACE_COST = 8_000_000_000, 20_000_000_000, 8_000_000_000, 40_000_000_000
VMEM = pl.BlockSpec(memory_space=pltpu.VMEM)
SMEM = pl.BlockSpec(memory_space=pltpu.SMEM)
ANY = pl.BlockSpec(memory_space=pltpu.HBM)


def call(kernel, out_shape, in_specs, scratch=(), flops=0, nbytes=0, exps=0, limit=8):
    single = isinstance(out_shape, jax.ShapeDtypeStruct)
    return pl.pallas_call(
        kernel,
        out_shape=out_shape,
        in_specs=in_specs,
        out_specs=VMEM if single else [VMEM] * len(out_shape),
        scratch_shapes=list(scratch),
        cost_estimate=pl.CostEstimate(
            flops=flops, bytes_accessed=nbytes, transcendentals=exps
        ),
        compiler_params=pltpu.CompilerParams(vmem_limit_bytes=limit << 20),
    )


STAY_SLOT, STAY_LENGTH, LEAVE_SLOT, LEAVE_ENTRY, LEAVE_LENGTH, STAY_FIRST = range(6)


def lanes(rows, columns):
    return lax.broadcasted_iota(I32, (rows, columns), 1)


def lines_of(rows, columns):
    return lax.broadcasted_iota(I32, (rows, columns), 0)


def upright(row):
    n = row.shape[1]
    return jnp.sum(jnp.where(lanes(n, n) == lines_of(n, n), row, 0.0), axis=1, keepdims=True)


def plan_kernel(moves_hbm, flags_hbm, lengths_hbm, table_ref, plan_ref, moves_ref, flags_ref, lengths_ref, sem):
    copies = [
        pltpu.make_async_copy(src, dst, sem.at[i])
        for i, (src, dst) in enumerate(
            ((moves_hbm, moves_ref), (flags_hbm, flags_ref), (lengths_hbm, lengths_ref))
        )
    ]
    for copy in copies:
        copy.start()
    for copy in copies:
        copy.wait()
    groups, wide = table_ref.shape
    moves, slots = moves_ref.shape[1], flags_ref.shape[1]
    source, target = moves_ref[0:1, :], moves_ref[1:2, :]
    slot = (moves_ref[2:3, :] + 1).astype(F32)
    hit = lines_of(groups, moves) == target
    earlier = (lines_of(moves, moves) < lanes(moves, moves)).astype(F32)
    before = jnp.dot(hit.astype(F32), earlier, preferred_element_type=F32).astype(I32)
    table = jnp.zeros((groups, wide), I32)
    for c in range(CAP):
        entry = jnp.sum(jnp.where(hit & (before == c), slot, 0.0), axis=1, keepdims=True)
        table = jnp.where(lanes(groups, wide) == c, entry.astype(I32), table)
    table_ref[...] = table

    place = jnp.sum(jnp.where(hit, lines_of(groups, moves) * CAP + before, 0).astype(F32), axis=0, keepdims=True)
    lengths = lengths_ref[...].astype(F32)
    taken = (upright(source.astype(F32)).astype(I32) == lanes(moves, slots)).astype(F32)
    leave_length = jnp.sum(taken * lengths, axis=1, keepdims=True)
    leave_length = jnp.sum(
        jnp.where(lanes(moves, moves) == lines_of(moves, moves), leave_length, 0.0), axis=0, keepdims=True
    )
    gone = jnp.sum(taken, axis=0, keepdims=True)
    stays = ((flags_ref[...] == 0) & (gone == 0.0)).astype(F32)
    rank = jnp.sum(jnp.where(lanes(slots, slots) < lines_of(slots, slots), stays, 0.0), axis=1, keepdims=True)
    first = slots - 2 * moves - jnp.sum(stays, axis=1, keepdims=True)
    chosen = ((rank + first).astype(I32) == lanes(slots, slots)) & (upright(stays) > 0.0)
    listed = jnp.sum(jnp.where(chosen, lines_of(slots, slots).astype(F32), 0.0), axis=0, keepdims=True)
    listed_length = jnp.sum(jnp.where(chosen, upright(lengths), 0.0), axis=0, keepdims=True)
    plan_ref[...] = jnp.zeros(plan_ref.shape, I32)
    plan_ref[STAY_SLOT : STAY_SLOT + 1, :] = listed.astype(I32)
    plan_ref[STAY_LENGTH : STAY_LENGTH + 1, :] = listed_length.astype(I32)
    plan_ref[LEAVE_SLOT : LEAVE_SLOT + 1, 0:moves] = source
    plan_ref[LEAVE_ENTRY : LEAVE_ENTRY + 1, 0:moves] = place.astype(I32)
    plan_ref[LEAVE_LENGTH : LEAVE_LENGTH + 1, 0:moves] = leave_length.astype(I32)
    plan_ref[STAY_FIRST : STAY_FIRST + 1, 0:1] = first.astype(I32)


HERE_ENTRY, HERE_SLOT = range(2)


def payload_kernel(slot_ref, table_ref, fresh_ref, out_ref, here_ref):
    for e in range(out_ref.shape[0]):
        out_ref[e] = fresh_ref[jnp.maximum(slot_ref[e // CAP, e % CAP] - 1, 0)]
    groups, width = table_ref.shape
    table = table_ref[...]
    there = (table > 0).astype(F32)
    earlier = (lanes(groups, groups) < lines_of(groups, groups)).astype(F32)
    before = jnp.dot(earlier, there, preferred_element_type=F32)
    whole = jnp.sum(there, axis=0, keepdims=True)
    entry = jnp.zeros((1, width), F32)
    slot = jnp.zeros((1, width), F32)
    base = jnp.zeros((1, 1), F32)
    for c in range(CAP):
        rank = (before[:, c : c + 1] + base).astype(I32)
        chosen = (rank == lanes(groups, width)) & (there[:, c : c + 1] > 0.0)
        entry += jnp.sum(jnp.where(chosen, (lines_of(groups, width) * CAP + c).astype(F32), 0.0), axis=0, keepdims=True)
        slot += jnp.sum(jnp.where(chosen, (table[:, c : c + 1] - 1).astype(F32), 0.0), axis=0, keepdims=True)
        base = base + whole[:, c : c + 1]
    here_ref[...] = jnp.zeros(here_ref.shape, I32)
    here_ref[HERE_ENTRY : HERE_ENTRY + 1, :] = entry.astype(I32)
    here_ref[HERE_SLOT : HERE_SLOT + 1, :] = slot.astype(I32)


def attend(batches, kbuf, vbuf, score, weight, cache, steps, heads, row_of, query_of, fresh_of, length_of, await_keys, await_values):
    positions, head = kbuf.shape[1:]
    lines = heads * steps
    lane = lanes(lines, positions)
    step = lax.rem(lines_of(lines, positions), steps)
    visible = (lane >= cache) & (lane - cache <= step)

    def fresh_rows(value):
        pad = jnp.zeros((FRESH - steps, head), F32)
        return jnp.concatenate([value.astype(F32), pad], axis=0).astype(BF16)

    for b, batch in enumerate(batches):
        for i in batch:
            fresh_key, fresh_value = fresh_of(i)
            kbuf[row_of(i), cache:positions, :] = fresh_rows(fresh_key)
            vbuf[row_of(i), cache:positions, :] = fresh_rows(fresh_value)
        await_keys(b)
        for i in batch:
            query = query_of(i).astype(F32)
            query = jnp.concatenate([query[:, h * head : (h + 1) * head] for h in range(heads)], axis=0)
            products = lax.dot_general(
                query.astype(BF16), kbuf[row_of(i)], (((1,), (1,)), ((), ())), preferred_element_type=F32
            )
            score[i * lines : (i + 1) * lines, :] = jnp.where(
                (lane < length_of(i)) | visible, products * head**-0.5, -jnp.inf
            )
    for batch in batches:
        chunk = slice(batch[0] * lines, (batch[-1] + 1) * lines)
        s = score[chunk, :]
        e = jnp.exp(s - jnp.max(s, axis=1, keepdims=True))
        weight[chunk, :] = (e * (1.0 / jnp.sum(e, axis=1, keepdims=True))).astype(BF16)
    mixed = []
    for b, batch in enumerate(batches):
        await_values(b)
        for i in batch:
            mixed.append(
                jnp.dot(weight[i * lines : (i + 1) * lines, :], vbuf[row_of(i)], preferred_element_type=F32)
            )
    return mixed


def staying_kernel(
    place_ref, plan_ref, query_ref, key_ref, value_ref, keys_ref, values_ref, weight_ref,
    up_ref, down_ref, heads_ref, fresh_ref, leave_keys_ref, leave_values_ref,
    kbuf, vbuf, score, weight, wbuf, fsem, ksem, vsem, wsem,
):
    steps, wide = query_ref.shape[1:]
    slots, _, cache, head = keys_ref.shape
    tokens, columns = heads_ref.shape[0], up_ref.shape[1]
    rows, ring = tokens // steps, weight_ref.shape[1] // columns
    chunk = slots // ksem.shape[0]
    fresh = [
        pltpu.make_async_copy(src, fresh_ref.at[:, :, pl.ds(at, src.shape[2])], fsem.at[i])
        for i, (src, at) in enumerate(((query_ref, 0), (key_ref, wide), (value_ref, wide + head)))
    ]
    keys, values = (
        [
            pltpu.make_async_copy(
                ref.at[pl.ds(c * chunk, chunk), 0], buf.at[pl.ds(c * chunk, chunk), pl.ds(0, cache)], sem.at[c]
            )
            for c in range(slots // chunk)
        ]
        for ref, buf, sem in ((keys_ref, kbuf, ksem), (values_ref, vbuf, vsem))
    )
    at = lax.rem(place_ref[0] + ring // 2, ring) * columns
    far = pltpu.make_async_copy(weight_ref.at[:, pl.ds(pl.multiple_of(at, columns), columns)], wbuf, wsem)
    for copy in fresh + keys + values + [far]:
        copy.start()

    last = [(slots - rows + i) // chunk for i in range(rows)]
    batches = [[i for i in range(rows) if last[i] == c] for c in sorted(set(last))]
    due = [[c for c in range(slots // chunk) if c <= last[b[0]] and (j == 0 or c > last[batches[j - 1][0]])] for j, b in enumerate(batches)]

    def slot(i):
        return plan_ref[STAY_SLOT, i]

    for copy in fresh:
        copy.wait()
    mixed = attend(
        batches, kbuf, vbuf, score, weight, cache, steps, wide // head,
        slot,
        lambda i: fresh_ref[slot(i), :, 0:wide],
        lambda i: (fresh_ref[slot(i), :, wide : wide + head], fresh_ref[slot(i), :, wide + head : wide + 2 * head]),
        lambda i: plan_ref[STAY_LENGTH, i],
        lambda b: [keys[c].wait() for c in due[b]],
        lambda b: [values[c].wait() for c in due[b]],
    )
    for j in range(rows // 4):
        for h in range(wide // head):
            tile = jnp.concatenate([o[h * steps : (h + 1) * steps] for o in mixed[4 * j : 4 * j + 4]], axis=0)
            heads_ref[16 * j : 16 * j + 16, h * head : (h + 1) * head] = tile.astype(BF16)
    for i in range(leave_keys_ref.shape[0]):
        leave_keys_ref[i] = kbuf[plan_ref[LEAVE_SLOT, i], 0:cache, :]
        leave_values_ref[i] = vbuf[plan_ref[LEAVE_SLOT, i], 0:cache, :]
    far.wait()
    cut = up_ref.shape[0]
    block = jnp.dot(heads_ref[...], wbuf[...], preferred_element_type=F32)
    up_ref[...] = block[:cut].astype(BF16)
    down_ref[...] = block[cut:].astype(BF16)


def hop_kernel(k, place_ref, heads_ref, up_ref, down_ref, weight_ref, up_out, down_out, ubuf, dbuf, wbuf, sem):
    columns = wbuf.shape[2]
    ring, tokens = weight_ref.shape[1] // columns, heads_ref.shape[0]
    copies = []
    for j, step in enumerate((k, ring - k)):
        at = pl.multiple_of(lax.rem(place_ref[0] + step, ring) * columns, columns)
        copies.append(pltpu.make_async_copy(weight_ref.at[:, pl.ds(at, columns)], wbuf.at[j], sem.at[j]))
    copies.append(pltpu.make_async_copy(up_ref, ubuf, sem.at[2]))
    copies.append(pltpu.make_async_copy(down_ref, dbuf, sem.at[3]))
    for copy in copies:
        copy.start()
    for j, (buf, out, first) in enumerate(((ubuf, up_out, 0), (dbuf, down_out, tokens - dbuf.shape[0]))):
        copies[j].wait()
        terms = jnp.dot(heads_ref[...], wbuf[j], preferred_element_type=F32)
        copies[2 + j].wait()
        end = first + buf.shape[0]
        out[first:end, :] = (terms[first:end] + buf[...].astype(F32)).astype(BF16)
        if first > 0:
            out[:first, :] = terms[:first].astype(BF16)
        if end < tokens:
            out[end:, :] = terms[end:].astype(BF16)


def leaving_kernel(plan_ref, asked_ref, keys_ref, values_ref, out_ref, kbuf, vbuf, score, weight):
    rows, cache, head = keys_ref.shape
    steps, wide = out_ref.shape[1:]
    out_ref[...] = jnp.zeros(out_ref.shape, BF16)
    for i in range(rows):
        kbuf[i, 0:cache, :] = keys_ref[i]
        vbuf[i, 0:cache, :] = values_ref[i]

    def entry(i):
        return plan_ref[LEAVE_ENTRY, i]

    mixed = attend(
        [list(range(rows))], kbuf, vbuf, score, weight, cache, steps, wide // head,
        lambda i: i,
        lambda i: asked_ref[entry(i), :, 0:wide],
        lambda i: (asked_ref[entry(i), :, wide : wide + head], asked_ref[entry(i), :, wide + head : wide + 2 * head]),
        lambda i: plan_ref[LEAVE_LENGTH, i],
        lambda b: None,
        lambda b: None,
    )
    for i, o in enumerate(mixed):
        for h in range(wide // head):
            out_ref[entry(i), :, h * head : (h + 1) * head] = o[h * steps : (h + 1) * steps].astype(BF16)


def arrived_kernel(here_ref, back_ref, weight_ref, out_ref, heads, wbuf, wsem):
    steps = back_ref.shape[1]
    rows, columns = out_ref.shape[1] // steps, out_ref.shape[2]
    parts = [
        pltpu.make_async_copy(weight_ref.at[:, pl.ds(k * columns, columns)], wbuf.at[k], wsem.at[k])
        for k in range(out_ref.shape[0])
    ]
    for copy in parts:
        copy.start()
    for j in range(heads.shape[0] // 16):
        four = [back_ref[here_ref[HERE_ENTRY, min(4 * j + u, rows - 1)]].astype(F32) for u in range(4)]
        heads[16 * j : 16 * j + 16, :] = jnp.concatenate(four, axis=0).astype(BF16)
    for k, copy in enumerate(parts):
        copy.wait()
        terms = jnp.dot(heads[...], wbuf[k], preferred_element_type=F32)
        out_ref[k] = terms[: out_ref.shape[1]].astype(BF16)


def place_kernel(place_ref, plan_ref, heads_ref, up_ref, down_ref, weight_ref, out_ref, total, wbuf, sem):
    steps, columns = out_ref.shape[1:]
    at = pl.multiple_of(place_ref[0] * columns, columns)
    copy = pltpu.make_async_copy(weight_ref.at[:, pl.ds(at, columns)], wbuf, sem)
    copy.start()
    out_ref[...] = jnp.zeros(out_ref.shape, BF16)
    copy.wait()
    own = jnp.dot(heads_ref[...], wbuf[...], preferred_element_type=F32)
    total[...] = own + up_ref[...].astype(F32) + down_ref[...].astype(F32)
    for i in range(heads_ref.shape[0] // steps):

        @pl.when(i >= plan_ref[STAY_FIRST, 0])
        def _():
            out_ref[plan_ref[STAY_SLOT, i]] = total[i * steps : (i + 1) * steps, :].astype(BF16)


def finish_kernel(here_ref, placed_ref, blocks_ref, out_ref, total):
    steps = out_ref.shape[1]
    out_ref[...] = placed_ref[...]
    terms = blocks_ref[0].astype(F32)
    for k in range(1, blocks_ref.shape[0]):
        terms = terms + blocks_ref[k].astype(F32)
    total[...] = terms
    for n in range(blocks_ref.shape[1] // steps):
        out_ref[here_ref[HERE_SLOT, n]] = total[n * steps : (n + 1) * steps, :].astype(BF16)


def on_device(
    keys_cache,
    values_cache,
    lengths,
    guard_flags,
    migrations,
    queries,
    new_keys,
    new_values,
    out_weight,
):
    shape = jax.ShapeDtypeStruct
    slots, _, cache, head = keys_cache.shape
    steps, wide = queries.shape[1:]
    moves = migrations.shape[0]
    groups, ring = lax.axis_size("group"), lax.axis_size("tp")
    columns = out_weight.shape[1] // ring
    entries = groups * CAP
    staying = slots - 2 * moves
    lines = wide // head * steps
    positions = cache + FRESH
    place = lax.axis_index("tp").astype(I32).reshape(1)
    barrier = lax.optimization_barrier
    keys_cache, values_cache, out_weight, queries, new_keys, new_values, moves_t, flags, reach = (
        pltpu.with_memory_space_constraint(x, pltpu.HBM)
        for x in (
            keys_cache, values_cache, out_weight, queries, new_keys, new_values,
            migrations.T, guard_flags.reshape(1, slots), lengths.reshape(1, slots),
        )
    )

    def exchange(x, axis):
        return lax.all_to_all(x, axis, split_axis=0, concat_axis=0, tiled=True)

    def scratch(held, rows):
        return [
            pltpu.VMEM((held, positions, head), BF16),
            pltpu.VMEM((held, positions, head), BF16),
            pltpu.VMEM((rows * lines, positions), F32),
            pltpu.VMEM((rows * lines, positions), BF16),
        ]

    table, plan = call(
        plan_kernel,
        [shape((groups, 128), I32), shape((8, slots), I32)],
        [ANY] * 3,
        [
            pltpu.VMEM((3, moves), I32),
            pltpu.VMEM((1, slots), I32),
            pltpu.VMEM((1, slots), I32),
            pltpu.SemaphoreType.DMA((3,)),
        ],
        nbytes=1 << 16,
    )(moves_t, flags, reach)
    table = exchange(table.reshape(groups, 1, 128), "group").reshape(groups, 128)

    tokens = staying * steps
    cut = -(-tokens // 32) * 16
    up, down, heads, fresh, leave_keys, leave_values = call(
        staying_kernel,
        [
            shape((cut, columns), BF16),
            shape((tokens - cut, columns), BF16),
            shape((tokens, wide), BF16),
            shape((slots, steps, wide + 2 * head), BF16),
            shape((moves, cache, head), BF16),
            shape((moves, cache, head), BF16),
        ],
        [SMEM] * 2 + [ANY] * 6,
        scratch(slots, staying)
        + [
            pltpu.VMEM((wide, columns), BF16),
            pltpu.SemaphoreType.DMA((3,)),
            pltpu.SemaphoreType.DMA((4,)),
            pltpu.SemaphoreType.DMA((4,)),
            pltpu.SemaphoreType.DMA,
        ],
        flops=2 * tokens * wide * columns,
        nbytes=16 << 20,
        exps=tokens * positions * 4,
        limit=24,
    )(place, plan, queries, new_keys, new_values, keys_cache, values_cache, out_weight)

    ahead = [(i, (i + 1) % ring) for i in range(ring)]
    astern = [(i, (i - 1) % ring) for i in range(ring)]

    def hop(u, d):
        return lax.ppermute(u, "tp", ahead), lax.ppermute(d, "tp", astern)

    def add(k, u, d):
        return call(
            functools.partial(hop_kernel, k),
            [shape((tokens, columns), BF16)] * 2,
            [SMEM, VMEM] + [pl.BlockSpec(memory_space=pl.ANY)] * 2 + [ANY],
            [
                pltpu.VMEM(u.shape, BF16),
                pltpu.VMEM(d.shape, BF16),
                pltpu.VMEM((2, wide, columns), BF16),
                pltpu.SemaphoreType.DMA((4,)),
            ],
            flops=HOP_COST,
        )(place, heads, u, d, out_weight)

    table, fresh, heads, leave_keys = barrier((table, fresh, heads, leave_keys))
    asked, here = call(
        payload_kernel,
        [shape((entries, steps, wide + 2 * head), BF16), shape((8, 128), I32)],
        [SMEM] + [VMEM] * 2,
        flops=PAYLOAD_COST,
    )(table, table, fresh)
    asked, heads = barrier((asked, heads))
    asked = exchange(asked, "group")
    up, down = hop(up, down)

    up, down = add(3, up, down)
    asked = barrier((asked, up, down))[0]
    up, down = hop(up, down)
    back = call(
        leaving_kernel,
        shape((entries, steps, wide), BF16),
        [SMEM] + [VMEM] * 3,
        scratch(moves, moves),
    )(plan, asked, leave_keys, leave_values)
    back, heads = barrier((back, heads))
    back = exchange(back, "group")
    up, down = add(2, up, down)
    back = barrier((back, up, down))[0]
    up, down = hop(up, down)
    arrived = moves * steps
    blocks = call(
        arrived_kernel,
        shape((ring, arrived, columns), BF16),
        [SMEM, VMEM, ANY],
        [
            pltpu.VMEM((-(-arrived // 16) * 16, wide), BF16),
            pltpu.VMEM((ring, wide, columns), BF16),
            pltpu.SemaphoreType.DMA((ring,)),
        ],
        flops=ARRIVED_COST,
        limit=10,
    )(here, back, out_weight)
    blocks, heads = barrier((blocks, heads))
    up, down = add(1, up, down)
    blocks = barrier((blocks, up, down))[0]
    blocks = exchange(blocks, "tp")
    up, down = hop(up, down)

    placed = call(
        place_kernel,
        shape((slots, steps, columns), BF16),
        [SMEM] * 2 + [VMEM] * 3 + [ANY],
        [pltpu.VMEM((tokens, columns), F32), pltpu.VMEM((wide, columns), BF16), pltpu.SemaphoreType.DMA],
        flops=PLACE_COST,
    )(place, plan, heads, up, down, out_weight)
    return call(
        finish_kernel,
        shape((slots, steps, columns), BF16),
        [SMEM] + [VMEM] * 2,
        [pltpu.VMEM((arrived, columns), F32)],
        nbytes=2 << 20,
    )(here, placed, blocks)


def solution(mesh):
    return jax.shard_map(
        on_device,
        mesh=mesh,
        in_specs=(
            P("group", "tp", None, None),
            P("group", "tp", None, None),
            P("group"),
            P("group"),
            P("group", None),
            P("group", None, "tp"),
            P("group", None, "tp"),
            P("group", None, "tp"),
            P("tp", None),
        ),
        out_specs=P("group", None, "tp"),
        check_vma=False,
    )
```

```python
import functools

import jax
import jax.numpy as jnp
from jax import lax
from jax.experimental import pallas as pl
from jax.experimental.pallas import tpu as pltpu
from jax.sharding import PartitionSpec as P

CAP = 2
F32, BF16, I32 = jnp.float32, jnp.bfloat16, jnp.int32
FRESH = 16
PAYLOAD_COST, HOP_COST, ARRIVED_COST, PLACE_COST = 8_000_000_000, 20_000_000_000, 8_000_000_000, 40_000_000_000
VMEM = pl.BlockSpec(memory_space=pltpu.VMEM)
SMEM = pl.BlockSpec(memory_space=pltpu.SMEM)
ANY = pl.BlockSpec(memory_space=pltpu.HBM)


def call(kernel, out_shape, in_specs, scratch=(), flops=0, nbytes=0, exps=0, limit=8, out=VMEM):
    single = isinstance(out_shape, jax.ShapeDtypeStruct)
    return pl.pallas_call(
        kernel,
        out_shape=out_shape,
        in_specs=in_specs,
        out_specs=out if single else [out] * len(out_shape),
        scratch_shapes=list(scratch),
        cost_estimate=pl.CostEstimate(
            flops=flops, bytes_accessed=nbytes, transcendentals=exps
        ),
        compiler_params=pltpu.CompilerParams(vmem_limit_bytes=limit << 20),
    )


STAY_SLOT, STAY_LENGTH, LEAVE_SLOT, LEAVE_ENTRY, LEAVE_LENGTH, STAY_FIRST = range(6)


def lanes(rows, columns):
    return lax.broadcasted_iota(I32, (rows, columns), 1)


def lines_of(rows, columns):
    return lax.broadcasted_iota(I32, (rows, columns), 0)


def upright(row):
    n = row.shape[1]
    return jnp.sum(jnp.where(lanes(n, n) == lines_of(n, n), row, 0.0), axis=1, keepdims=True)


def plan_kernel(moves_hbm, flags_hbm, lengths_hbm, table_ref, plan_ref, moves_ref, flags_ref, lengths_ref, sem):
    copies = [
        pltpu.make_async_copy(src, dst, sem.at[i])
        for i, (src, dst) in enumerate(
            ((moves_hbm, moves_ref), (flags_hbm, flags_ref), (lengths_hbm, lengths_ref))
        )
    ]
    for copy in copies:
        copy.start()
    for copy in copies:
        copy.wait()
    groups, wide = table_ref.shape
    moves, slots = moves_ref.shape[1], flags_ref.shape[1]
    source, target = moves_ref[0:1, :], moves_ref[1:2, :]
    slot = (moves_ref[2:3, :] + 1).astype(F32)
    hit = lines_of(groups, moves) == target
    earlier = (lines_of(moves, moves) < lanes(moves, moves)).astype(F32)
    before = jnp.dot(hit.astype(F32), earlier, preferred_element_type=F32).astype(I32)
    table = jnp.zeros((groups, wide), I32)
    for c in range(CAP):
        entry = jnp.sum(jnp.where(hit & (before == c), slot, 0.0), axis=1, keepdims=True)
        table = jnp.where(lanes(groups, wide) == c, entry.astype(I32), table)
    table_ref[...] = table

    place = jnp.sum(jnp.where(hit, lines_of(groups, moves) * CAP + before, 0).astype(F32), axis=0, keepdims=True)
    lengths = lengths_ref[...].astype(F32)
    taken = (upright(source.astype(F32)).astype(I32) == lanes(moves, slots)).astype(F32)
    leave_length = jnp.sum(taken * lengths, axis=1, keepdims=True)
    leave_length = jnp.sum(
        jnp.where(lanes(moves, moves) == lines_of(moves, moves), leave_length, 0.0), axis=0, keepdims=True
    )
    gone = jnp.sum(taken, axis=0, keepdims=True)
    stays = ((flags_ref[...] == 0) & (gone == 0.0)).astype(F32)
    rank = jnp.sum(jnp.where(lanes(slots, slots) < lines_of(slots, slots), stays, 0.0), axis=1, keepdims=True)
    first = slots - 2 * moves - jnp.sum(stays, axis=1, keepdims=True)
    chosen = ((rank + first).astype(I32) == lanes(slots, slots)) & (upright(stays) > 0.0)
    listed = jnp.sum(jnp.where(chosen, lines_of(slots, slots).astype(F32), 0.0), axis=0, keepdims=True)
    listed_length = jnp.sum(jnp.where(chosen, upright(lengths), 0.0), axis=0, keepdims=True)
    plan_ref[...] = jnp.zeros(plan_ref.shape, I32)
    plan_ref[STAY_SLOT : STAY_SLOT + 1, :] = listed.astype(I32)
    plan_ref[STAY_LENGTH : STAY_LENGTH + 1, :] = listed_length.astype(I32)
    plan_ref[LEAVE_SLOT : LEAVE_SLOT + 1, 0:moves] = source
    plan_ref[LEAVE_ENTRY : LEAVE_ENTRY + 1, 0:moves] = place.astype(I32)
    plan_ref[LEAVE_LENGTH : LEAVE_LENGTH + 1, 0:moves] = leave_length.astype(I32)
    plan_ref[STAY_FIRST : STAY_FIRST + 1, 0:1] = first.astype(I32)


HERE_ENTRY, HERE_SLOT = range(2)


def payload_kernel(slot_src, table_ref, fresh_ref, out_ref, here_ref, slot_ref, sem):
    copy = pltpu.make_async_copy(slot_src, slot_ref, sem)
    copy.start()
    groups, width = table_ref.shape
    table = table_ref[...]
    there = (table > 0).astype(F32)
    earlier = (lanes(groups, groups) < lines_of(groups, groups)).astype(F32)
    before = jnp.dot(earlier, there, preferred_element_type=F32)
    whole = jnp.sum(there, axis=0, keepdims=True)
    entry = jnp.zeros((1, width), F32)
    slot = jnp.zeros((1, width), F32)
    base = jnp.zeros((1, 1), F32)
    for c in range(CAP):
        rank = (before[:, c : c + 1] + base).astype(I32)
        chosen = (rank == lanes(groups, width)) & (there[:, c : c + 1] > 0.0)
        entry += jnp.sum(jnp.where(chosen, (lines_of(groups, width) * CAP + c).astype(F32), 0.0), axis=0, keepdims=True)
        slot += jnp.sum(jnp.where(chosen, (table[:, c : c + 1] - 1).astype(F32), 0.0), axis=0, keepdims=True)
        base = base + whole[:, c : c + 1]
    here_ref[...] = jnp.zeros(here_ref.shape, I32)
    here_ref[HERE_ENTRY : HERE_ENTRY + 1, :] = entry.astype(I32)
    here_ref[HERE_SLOT : HERE_SLOT + 1, :] = slot.astype(I32)
    copy.wait()
    for e in range(out_ref.shape[0]):
        out_ref[e] = fresh_ref[jnp.maximum(slot_ref[e // CAP, e % CAP] - 1, 0)]


def attend(batches, kbuf, vbuf, score, weight, cache, steps, heads, row_of, query_of, fresh_of, length_of, await_keys, await_values):
    positions, head = kbuf.shape[1:]
    lines = heads * steps
    lane = lanes(lines, positions)
    step = lax.rem(lines_of(lines, positions), steps)
    visible = (lane >= cache) & (lane - cache <= step)

    def fresh_rows(value):
        pad = jnp.zeros((FRESH - steps, head), F32)
        return jnp.concatenate([value.astype(F32), pad], axis=0).astype(BF16)

    for b, batch in enumerate(batches):
        for i in batch:
            fresh_key, fresh_value = fresh_of(i)
            kbuf[row_of(i), cache:positions, :] = fresh_rows(fresh_key)
            vbuf[row_of(i), cache:positions, :] = fresh_rows(fresh_value)
        await_keys(b)
        for i in batch:
            query = query_of(i).astype(F32)
            query = jnp.concatenate([query[:, h * head : (h + 1) * head] for h in range(heads)], axis=0)
            products = lax.dot_general(
                query.astype(BF16), kbuf[row_of(i)], (((1,), (1,)), ((), ())), preferred_element_type=F32
            )
            score[i * lines : (i + 1) * lines, :] = jnp.where(
                (lane < length_of(i)) | visible, products * head**-0.5, -jnp.inf
            )
    mixed = []
    for b, batch in enumerate(batches):
        chunk = slice(batch[0] * lines, (batch[-1] + 1) * lines)
        s = score[chunk, :]
        e = jnp.exp(s - jnp.max(s, axis=1, keepdims=True))
        weight[chunk, :] = (e * (1.0 / jnp.sum(e, axis=1, keepdims=True))).astype(BF16)
        await_values(b)
        for i in batch:
            mixed.append(
                jnp.dot(weight[i * lines : (i + 1) * lines, :], vbuf[row_of(i)], preferred_element_type=F32)
            )
    return mixed


def staying_kernel(
    plan_src, query_ref, key_ref, value_ref, keys_ref, values_ref, weight_ref,
    up_ref, down_ref, heads_ref, fresh_ref, leave_keys_ref, leave_values_ref,
    plan_ref, kbuf, vbuf, score, weight, wbuf, psem, fsem, ksem, vsem, wsem,
):
    steps, wide = query_ref.shape[1:]
    slots, _, cache, head = keys_ref.shape
    tokens, columns = heads_ref.shape[0], up_ref.shape[1]
    rows, ring = tokens // steps, weight_ref.shape[1] // columns
    chunk = slots // ksem.shape[0]
    fresh = [
        pltpu.make_async_copy(src, fresh_ref.at[:, :, pl.ds(at, src.shape[2])], fsem.at[i])
        for i, (src, at) in enumerate(((query_ref, 0), (key_ref, wide), (value_ref, wide + head)))
    ]
    keys, values = (
        [
            pltpu.make_async_copy(
                ref.at[pl.ds(c * chunk, chunk), 0], buf.at[pl.ds(c * chunk, chunk), pl.ds(0, cache)], sem.at[c]
            )
            for c in range(slots // chunk)
        ]
        for ref, buf, sem in ((keys_ref, kbuf, ksem), (values_ref, vbuf, vsem))
    )
    listed = pltpu.make_async_copy(plan_src, plan_ref, psem)
    at = lax.rem(lax.axis_index("tp") + ring // 2, ring) * columns
    far = pltpu.make_async_copy(weight_ref.at[:, pl.ds(pl.multiple_of(at, columns), columns)], wbuf, wsem)
    for copy in [listed] + fresh + keys + values + [far]:
        copy.start()

    last = [(slots - rows + i) // chunk for i in range(rows)]
    batches = [[i for i in range(rows) if last[i] == c] for c in sorted(set(last))]
    due = [[c for c in range(slots // chunk) if c <= last[b[0]] and (j == 0 or c > last[batches[j - 1][0]])] for j, b in enumerate(batches)]

    def slot(i):
        return plan_ref[STAY_SLOT, i]

    for copy in [listed] + fresh:
        copy.wait()
    mixed = attend(
        batches, kbuf, vbuf, score, weight, cache, steps, wide // head,
        slot,
        lambda i: fresh_ref[slot(i), :, 0:wide],
        lambda i: (fresh_ref[slot(i), :, wide : wide + head], fresh_ref[slot(i), :, wide + head : wide + 2 * head]),
        lambda i: plan_ref[STAY_LENGTH, i],
        lambda b: [keys[c].wait() for c in due[b]],
        lambda b: [values[c].wait() for c in due[b]],
    )
    for j in range(rows // 4):
        for h in range(wide // head):
            tile = jnp.concatenate([o[h * steps : (h + 1) * steps] for o in mixed[4 * j : 4 * j + 4]], axis=0)
            heads_ref[16 * j : 16 * j + 16, h * head : (h + 1) * head] = tile.astype(BF16)
    for i in range(leave_keys_ref.shape[0]):
        leave_keys_ref[i] = kbuf[plan_ref[LEAVE_SLOT, i], 0:cache, :]
        leave_values_ref[i] = vbuf[plan_ref[LEAVE_SLOT, i], 0:cache, :]
    far.wait()
    cut = up_ref.shape[0]
    block = jnp.dot(heads_ref[...], wbuf[...], preferred_element_type=F32)
    up_ref[...] = block[:cut].astype(BF16)
    down_ref[...] = block[cut:].astype(BF16)


def hop_kernel(k, heads_ref, up_ref, down_ref, weight_ref, up_out, down_out, ubuf, dbuf, wbuf, sem):
    columns = wbuf.shape[2]
    ring, tokens = weight_ref.shape[1] // columns, heads_ref.shape[0]
    copies = []
    for j, step in enumerate((k, ring - k)):
        at = pl.multiple_of(lax.rem(lax.axis_index("tp") + step, ring) * columns, columns)
        copies.append(pltpu.make_async_copy(weight_ref.at[:, pl.ds(at, columns)], wbuf.at[j], sem.at[j]))
    copies.append(pltpu.make_async_copy(up_ref, ubuf, sem.at[2]))
    copies.append(pltpu.make_async_copy(down_ref, dbuf, sem.at[3]))
    for copy in copies:
        copy.start()
    for j, (buf, out, first) in enumerate(((ubuf, up_out, 0), (dbuf, down_out, tokens - dbuf.shape[0]))):
        copies[j].wait()
        terms = jnp.dot(heads_ref[...], wbuf[j], preferred_element_type=F32)
        copies[2 + j].wait()
        end = first + buf.shape[0]
        out[first:end, :] = (terms[first:end] + buf[...].astype(F32)).astype(BF16)
        if first > 0:
            out[:first, :] = terms[:first].astype(BF16)
        if end < tokens:
            out[end:, :] = terms[end:].astype(BF16)


def leaving_kernel(plan_src, asked_ref, keys_ref, values_ref, out_ref, plan_ref, kbuf, vbuf, score, weight, psem):
    listed = pltpu.make_async_copy(plan_src, plan_ref, psem)
    listed.start()
    rows, cache, head = keys_ref.shape
    steps, wide = out_ref.shape[1:]
    out_ref[...] = jnp.zeros(out_ref.shape, BF16)
    for i in range(rows):
        kbuf[i, 0:cache, :] = keys_ref[i]
        vbuf[i, 0:cache, :] = values_ref[i]
    listed.wait()

    def entry(i):
        return plan_ref[LEAVE_ENTRY, i]

    mixed = attend(
        [list(range(rows))], kbuf, vbuf, score, weight, cache, steps, wide // head,
        lambda i: i,
        lambda i: asked_ref[entry(i), :, 0:wide],
        lambda i: (asked_ref[entry(i), :, wide : wide + head], asked_ref[entry(i), :, wide + head : wide + 2 * head]),
        lambda i: plan_ref[LEAVE_LENGTH, i],
        lambda b: None,
        lambda b: None,
    )
    for i, o in enumerate(mixed):
        for h in range(wide // head):
            out_ref[entry(i), :, h * head : (h + 1) * head] = o[h * steps : (h + 1) * steps].astype(BF16)


def arrived_kernel(here_src, back_ref, weight_ref, out_ref, here_ref, heads, wbuf, sums, hsem, wsem, osem):
    listed = pltpu.make_async_copy(here_src, here_ref, hsem)
    listed.start()
    steps = back_ref.shape[1]
    ring, lines, columns = out_ref.shape
    rows = lines // steps
    parts = [
        pltpu.make_async_copy(weight_ref.at[:, pl.ds(k * columns, columns)], wbuf.at[k], wsem.at[k])
        for k in range(ring)
    ]
    for copy in parts:
        copy.start()
    listed.wait()
    for j in range(heads.shape[0] // 16):
        four = [back_ref[here_ref[HERE_ENTRY, min(4 * j + u, rows - 1)]].astype(F32) for u in range(4)]
        heads[16 * j : 16 * j + 16, :] = jnp.concatenate(four, axis=0).astype(BF16)
    done = []
    for k, copy in enumerate(parts):
        copy.wait()
        terms = jnp.dot(heads[...], wbuf[k], preferred_element_type=F32)
        sums[k] = terms[:lines].astype(BF16)
        done.append(pltpu.make_async_copy(sums.at[k], out_ref.at[k], osem.at[k]))
        done[k].start()
    for copy in done:
        copy.wait()


def place_kernel(plan_ref, heads_ref, up_ref, down_ref, weight_ref, out_ref, total, wbuf, sem):
    steps, columns = out_ref.shape[1:]
    at = pl.multiple_of(lax.axis_index("tp") * columns, columns)
    copy = pltpu.make_async_copy(weight_ref.at[:, pl.ds(at, columns)], wbuf, sem)
    copy.start()
    out_ref[...] = jnp.zeros(out_ref.shape, BF16)
    copy.wait()
    own = jnp.dot(heads_ref[...], wbuf[...], preferred_element_type=F32)
    total[...] = own + up_ref[...].astype(F32) + down_ref[...].astype(F32)
    for i in range(heads_ref.shape[0] // steps):

        @pl.when(i >= plan_ref[STAY_FIRST, 0])
        def _():
            out_ref[plan_ref[STAY_SLOT, i]] = total[i * steps : (i + 1) * steps, :].astype(BF16)


def finish_kernel(here_src, placed_ref, blocks_ref, out_ref, here_ref, total, hsem):
    listed = pltpu.make_async_copy(here_src, here_ref, hsem)
    listed.start()
    steps = out_ref.shape[1]
    out_ref[...] = placed_ref[...]
    terms = blocks_ref[0].astype(F32)
    for k in range(1, blocks_ref.shape[0]):
        terms = terms + blocks_ref[k].astype(F32)
    total[...] = terms
    listed.wait()
    for n in range(blocks_ref.shape[1] // steps):
        out_ref[here_ref[HERE_SLOT, n]] = total[n * steps : (n + 1) * steps, :].astype(BF16)


def on_device(
    keys_cache,
    values_cache,
    lengths,
    guard_flags,
    migrations,
    queries,
    new_keys,
    new_values,
    out_weight,
):
    shape = jax.ShapeDtypeStruct
    slots, _, cache, head = keys_cache.shape
    steps, wide = queries.shape[1:]
    moves = migrations.shape[0]
    groups, ring = lax.axis_size("group"), lax.axis_size("tp")
    columns = out_weight.shape[1] // ring
    entries = groups * CAP
    staying = slots - 2 * moves
    lines = wide // head * steps
    positions = cache + FRESH
    barrier = lax.optimization_barrier
    keys_cache, values_cache, out_weight, queries, new_keys, new_values, moves_t, flags, reach = (
        pltpu.with_memory_space_constraint(x, pltpu.HBM)
        for x in (
            keys_cache, values_cache, out_weight, queries, new_keys, new_values,
            migrations.T, guard_flags.reshape(1, slots), lengths.reshape(1, slots),
        )
    )

    def exchange(x, axis):
        return lax.all_to_all(x, axis, split_axis=0, concat_axis=0, tiled=True)

    def scratch(held, rows):
        return [
            pltpu.VMEM((held, positions, head), BF16),
            pltpu.VMEM((held, positions, head), BF16),
            pltpu.VMEM((rows * lines, positions), F32),
            pltpu.VMEM((rows * lines, positions), BF16),
        ]

    table, plan = call(
        plan_kernel,
        [shape((groups, 128), I32), shape((8, slots), I32)],
        [ANY] * 3,
        [
            pltpu.VMEM((3, moves), I32),
            pltpu.VMEM((1, slots), I32),
            pltpu.VMEM((1, slots), I32),
            pltpu.SemaphoreType.DMA((3,)),
        ],
        nbytes=1 << 16,
    )(moves_t, flags, reach)
    table = exchange(table.reshape(groups, 1, 128), "group").reshape(groups, 128)

    tokens = staying * steps
    cut = -(-tokens // 32) * 16
    up, down, heads, fresh, leave_keys, leave_values = call(
        staying_kernel,
        [
            shape((cut, columns), BF16),
            shape((tokens - cut, columns), BF16),
            shape((tokens, wide), BF16),
            shape((slots, steps, wide + 2 * head), BF16),
            shape((moves, cache, head), BF16),
            shape((moves, cache, head), BF16),
        ],
        [pl.BlockSpec(memory_space=pl.ANY)] + [ANY] * 6,
        [pltpu.SMEM((8, slots), I32)]
        + scratch(slots, staying)
        + [
            pltpu.VMEM((wide, columns), BF16),
            pltpu.SemaphoreType.DMA,
            pltpu.SemaphoreType.DMA((3,)),
            pltpu.SemaphoreType.DMA((4,)),
            pltpu.SemaphoreType.DMA((4,)),
            pltpu.SemaphoreType.DMA,
        ],
        flops=2 * tokens * wide * columns,
        nbytes=16 << 20,
        exps=tokens * positions * 4,
        limit=24,
    )(plan, queries, new_keys, new_values, keys_cache, values_cache, out_weight)

    ahead = [(i, (i + 1) % ring) for i in range(ring)]
    astern = [(i, (i - 1) % ring) for i in range(ring)]

    def hop(u, d):
        return lax.ppermute(u, "tp", ahead), lax.ppermute(d, "tp", astern)

    def add(k, u, d):
        return call(
            functools.partial(hop_kernel, k),
            [shape((tokens, columns), BF16)] * 2,
            [VMEM] + [pl.BlockSpec(memory_space=pl.ANY)] * 2 + [ANY],
            [
                pltpu.VMEM(u.shape, BF16),
                pltpu.VMEM(d.shape, BF16),
                pltpu.VMEM((2, wide, columns), BF16),
                pltpu.SemaphoreType.DMA((4,)),
            ],
            flops=HOP_COST,
        )(heads, u, d, out_weight)

    table, fresh, heads, leave_keys = barrier((table, fresh, heads, leave_keys))
    asked, here = call(
        payload_kernel,
        [shape((entries, steps, wide + 2 * head), BF16), shape((8, 128), I32)],
        [pl.BlockSpec(memory_space=pl.ANY)] + [VMEM] * 2,
        [pltpu.SMEM((groups, 128), I32), pltpu.SemaphoreType.DMA],
        flops=PAYLOAD_COST,
    )(table, table, fresh)
    asked, heads = barrier((asked, heads))
    asked = exchange(asked, "group")
    up, down = hop(up, down)

    up, down = add(3, up, down)
    asked = barrier((asked, up, down))[0]
    up, down = hop(up, down)
    back = call(
        leaving_kernel,
        shape((entries, steps, wide), BF16),
        [pl.BlockSpec(memory_space=pl.ANY)] + [VMEM] * 3,
        [pltpu.SMEM((8, slots), I32)] + scratch(moves, moves) + [pltpu.SemaphoreType.DMA],
    )(plan, asked, leave_keys, leave_values)
    back, heads = barrier((back, heads))
    back = exchange(back, "group")
    up, down = add(2, up, down)
    back = barrier((back, up, down))[0]
    up, down = hop(up, down)
    arrived = moves * steps
    blocks = call(
        arrived_kernel,
        shape((ring, arrived, columns), BF16),
        [pl.BlockSpec(memory_space=pl.ANY), VMEM, ANY],
        [
            pltpu.SMEM((8, 128), I32),
            pltpu.VMEM((-(-arrived // 16) * 16, wide), BF16),
            pltpu.VMEM((ring, wide, columns), BF16),
            pltpu.VMEM((ring, arrived, columns), BF16),
            pltpu.SemaphoreType.DMA,
            pltpu.SemaphoreType.DMA((ring,)),
            pltpu.SemaphoreType.DMA((ring,)),
        ],
        out=ANY,
        flops=ARRIVED_COST,
        limit=10,
    )(here, back, out_weight)
    blocks, heads = barrier((blocks, heads))
    up, down = add(1, up, down)
    blocks = barrier((blocks, up, down))[0]
    blocks = exchange(blocks, "tp")
    up, down = hop(up, down)

    placed = call(
        place_kernel,
        shape((slots, steps, columns), BF16),
        [SMEM] + [VMEM] * 3 + [ANY],
        [pltpu.VMEM((tokens, columns), F32), pltpu.VMEM((wide, columns), BF16), pltpu.SemaphoreType.DMA],
        flops=PLACE_COST,
    )(plan, heads, up, down, out_weight)
    return call(
        finish_kernel,
        shape((slots, steps, columns), BF16),
        [pl.BlockSpec(memory_space=pl.ANY)] + [VMEM] * 2,
        [pltpu.SMEM((8, 128), I32), pltpu.VMEM((arrived, columns), F32), pltpu.SemaphoreType.DMA],
        nbytes=2 << 20,
    )(here, placed, blocks)


def solution(mesh):
    return jax.shard_map(
        on_device,
        mesh=mesh,
        in_specs=(
            P("group", "tp", None, None),
            P("group", "tp", None, None),
            P("group"),
            P("group"),
            P("group", None),
            P("group", None, "tp"),
            P("group", None, "tp"),
            P("group", None, "tp"),
            P("tp", None),
        ),
        out_specs=P("group", None, "tp"),
        check_vma=False,
    )
```

```python
import functools

import jax
import jax.numpy as jnp
from jax import lax
from jax.experimental import pallas as pl
from jax.experimental.pallas import tpu as pltpu
from jax.sharding import PartitionSpec as P

CAP = 2
F32, BF16, I32 = jnp.float32, jnp.bfloat16, jnp.int32
FRESH = 16
PAYLOAD_COST, HOP_COST, ARRIVED_COST, PLACE_COST = 8_000_000_000, 20_000_000_000, 8_000_000_000, 40_000_000_000
VMEM = pl.BlockSpec(memory_space=pltpu.VMEM)
SMEM = pl.BlockSpec(memory_space=pltpu.SMEM)
ANY = pl.BlockSpec(memory_space=pltpu.HBM)


def call(kernel, out_shape, in_specs, scratch=(), flops=0, nbytes=0, exps=0, limit=8, out=VMEM):
    single = isinstance(out_shape, jax.ShapeDtypeStruct)
    return pl.pallas_call(
        kernel,
        out_shape=out_shape,
        in_specs=in_specs,
        out_specs=out if single else [out] * len(out_shape),
        scratch_shapes=list(scratch),
        cost_estimate=pl.CostEstimate(
            flops=flops, bytes_accessed=nbytes, transcendentals=exps
        ),
        compiler_params=pltpu.CompilerParams(vmem_limit_bytes=limit << 20),
    )


STAY_SLOT, STAY_LENGTH, LEAVE_SLOT, LEAVE_ENTRY, LEAVE_LENGTH, STAY_FIRST = range(6)


def lanes(rows, columns):
    return lax.broadcasted_iota(I32, (rows, columns), 1)


def lines_of(rows, columns):
    return lax.broadcasted_iota(I32, (rows, columns), 0)


def upright(row):
    n = row.shape[1]
    return jnp.sum(jnp.where(lanes(n, n) == lines_of(n, n), row, 0.0), axis=1, keepdims=True)


def plan_kernel(moves_hbm, flags_hbm, lengths_hbm, table_ref, plan_ref, moves_ref, flags_ref, lengths_ref, sem):
    copies = [
        pltpu.make_async_copy(src, dst, sem.at[i])
        for i, (src, dst) in enumerate(
            ((moves_hbm, moves_ref), (flags_hbm, flags_ref), (lengths_hbm, lengths_ref))
        )
    ]
    for copy in copies:
        copy.start()
    for copy in copies:
        copy.wait()
    groups, wide = table_ref.shape
    moves, slots = moves_ref.shape[1], flags_ref.shape[1]
    source, target = moves_ref[0:1, :], moves_ref[1:2, :]
    slot = (moves_ref[2:3, :] + 1).astype(F32)
    hit = lines_of(groups, moves) == target
    earlier = (lines_of(moves, moves) < lanes(moves, moves)).astype(F32)
    before = jnp.dot(hit.astype(F32), earlier, preferred_element_type=F32).astype(I32)
    table = jnp.zeros((groups, wide), I32)
    for c in range(CAP):
        entry = jnp.sum(jnp.where(hit & (before == c), slot, 0.0), axis=1, keepdims=True)
        table = jnp.where(lanes(groups, wide) == c, entry.astype(I32), table)
    table_ref[...] = table

    place = jnp.sum(jnp.where(hit, lines_of(groups, moves) * CAP + before, 0).astype(F32), axis=0, keepdims=True)
    lengths = lengths_ref[...].astype(F32)
    taken = (upright(source.astype(F32)).astype(I32) == lanes(moves, slots)).astype(F32)
    leave_length = jnp.sum(taken * lengths, axis=1, keepdims=True)
    leave_length = jnp.sum(
        jnp.where(lanes(moves, moves) == lines_of(moves, moves), leave_length, 0.0), axis=0, keepdims=True
    )
    gone = jnp.sum(taken, axis=0, keepdims=True)
    stays = ((flags_ref[...] == 0) & (gone == 0.0)).astype(F32)
    rank = jnp.sum(jnp.where(lanes(slots, slots) < lines_of(slots, slots), stays, 0.0), axis=1, keepdims=True)
    first = slots - 2 * moves - jnp.sum(stays, axis=1, keepdims=True)
    chosen = ((rank + first).astype(I32) == lanes(slots, slots)) & (upright(stays) > 0.0)
    listed = jnp.sum(jnp.where(chosen, lines_of(slots, slots).astype(F32), 0.0), axis=0, keepdims=True)
    listed_length = jnp.sum(jnp.where(chosen, upright(lengths), 0.0), axis=0, keepdims=True)
    plan_ref[...] = jnp.zeros(plan_ref.shape, I32)
    plan_ref[STAY_SLOT : STAY_SLOT + 1, :] = listed.astype(I32)
    plan_ref[STAY_LENGTH : STAY_LENGTH + 1, :] = listed_length.astype(I32)
    plan_ref[LEAVE_SLOT : LEAVE_SLOT + 1, 0:moves] = source
    plan_ref[LEAVE_ENTRY : LEAVE_ENTRY + 1, 0:moves] = place.astype(I32)
    plan_ref[LEAVE_LENGTH : LEAVE_LENGTH + 1, 0:moves] = leave_length.astype(I32)
    plan_ref[STAY_FIRST : STAY_FIRST + 1, 0:1] = first.astype(I32)


HERE_ENTRY, HERE_SLOT = range(2)


def payload_kernel(slot_src, table_ref, fresh_ref, out_ref, here_ref, slot_ref, sem):
    copy = pltpu.make_async_copy(slot_src, slot_ref, sem)
    copy.start()
    groups, width = table_ref.shape
    table = table_ref[...]
    there = (table > 0).astype(F32)
    earlier = (lanes(groups, groups) < lines_of(groups, groups)).astype(F32)
    before = jnp.dot(earlier, there, preferred_element_type=F32)
    whole = jnp.sum(there, axis=0, keepdims=True)
    entry = jnp.zeros((1, width), F32)
    slot = jnp.zeros((1, width), F32)
    base = jnp.zeros((1, 1), F32)
    for c in range(CAP):
        rank = (before[:, c : c + 1] + base).astype(I32)
        chosen = (rank == lanes(groups, width)) & (there[:, c : c + 1] > 0.0)
        entry += jnp.sum(jnp.where(chosen, (lines_of(groups, width) * CAP + c).astype(F32), 0.0), axis=0, keepdims=True)
        slot += jnp.sum(jnp.where(chosen, (table[:, c : c + 1] - 1).astype(F32), 0.0), axis=0, keepdims=True)
        base = base + whole[:, c : c + 1]
    here_ref[...] = jnp.zeros(here_ref.shape, I32)
    here_ref[HERE_ENTRY : HERE_ENTRY + 1, :] = entry.astype(I32)
    here_ref[HERE_SLOT : HERE_SLOT + 1, :] = slot.astype(I32)
    copy.wait()
    for e in range(out_ref.shape[0]):
        out_ref[e] = fresh_ref[jnp.maximum(slot_ref[e // CAP, e % CAP] - 1, 0)]


def attend(batches, kbuf, vbuf, score, weight, cache, steps, heads, row_of, query_of, fresh_of, length_of, await_keys, await_values):
    positions, head = kbuf.shape[1:]
    lines = heads * steps
    lane = lanes(lines, positions)
    step = lax.rem(lines_of(lines, positions), steps)
    visible = (lane >= cache) & (lane - cache <= step)

    def fresh_rows(value):
        pad = jnp.zeros((FRESH - steps, head), F32)
        return jnp.concatenate([value.astype(F32), pad], axis=0).astype(BF16)

    for b, batch in enumerate(batches):
        for i in batch:
            fresh_key, fresh_value = fresh_of(i)
            kbuf[row_of(i), cache:positions, :] = fresh_rows(fresh_key)
            vbuf[row_of(i), cache:positions, :] = fresh_rows(fresh_value)
        await_keys(b)
        for i in batch:
            query = query_of(i).astype(F32)
            query = jnp.concatenate([query[:, h * head : (h + 1) * head] for h in range(heads)], axis=0)
            products = lax.dot_general(
                query.astype(BF16), kbuf[row_of(i)], (((1,), (1,)), ((), ())), preferred_element_type=F32
            )
            score[i * lines : (i + 1) * lines, :] = jnp.where(
                (lane < length_of(i)) | visible, products * head**-0.5, -jnp.inf
            )
    mixed = []
    for b, batch in enumerate(batches):
        chunk = slice(batch[0] * lines, (batch[-1] + 1) * lines)
        s = score[chunk, :]
        e = jnp.exp(s - jnp.max(s, axis=1, keepdims=True))
        weight[chunk, :] = (e * (1.0 / jnp.sum(e, axis=1, keepdims=True))).astype(BF16)
        await_values(b)
        for i in batch:
            mixed.append(
                jnp.dot(weight[i * lines : (i + 1) * lines, :], vbuf[row_of(i)], preferred_element_type=F32)
            )
    return mixed


def staying_kernel(
    plan_src, query_ref, key_ref, value_ref, keys_ref, values_ref, weight_ref,
    up_ref, down_ref, heads_ref, fresh_ref, leave_keys_ref, leave_values_ref,
    plan_ref, kbuf, vbuf, score, weight, wbuf, psem, fsem, ksem, vsem, wsem,
):
    steps, wide = query_ref.shape[1:]
    slots, _, cache, head = keys_ref.shape
    tokens, columns = heads_ref.shape[0], up_ref.shape[1]
    rows, ring = tokens // steps, weight_ref.shape[1] // columns
    chunk = slots // ksem.shape[0]
    fresh = [
        pltpu.make_async_copy(src, fresh_ref.at[:, :, pl.ds(at, src.shape[2])], fsem.at[i])
        for i, (src, at) in enumerate(((query_ref, 0), (key_ref, wide), (value_ref, wide + head)))
    ]
    keys, values = (
        [
            pltpu.make_async_copy(
                ref.at[pl.ds(c * chunk, chunk), 0], buf.at[pl.ds(c * chunk, chunk), pl.ds(0, cache)], sem.at[c]
            )
            for c in range(slots // chunk)
        ]
        for ref, buf, sem in ((keys_ref, kbuf, ksem), (values_ref, vbuf, vsem))
    )
    listed = pltpu.make_async_copy(plan_src, plan_ref, psem)
    at = lax.rem(lax.axis_index("tp") + ring // 2, ring) * columns
    far = pltpu.make_async_copy(weight_ref.at[:, pl.ds(pl.multiple_of(at, columns), columns)], wbuf, wsem)
    for copy in [listed] + fresh + keys + values + [far]:
        copy.start()

    last = [(slots - rows + i) // chunk for i in range(rows)]
    batches = [[i for i in range(rows) if last[i] == c] for c in sorted(set(last))]
    due = [[c for c in range(slots // chunk) if c <= last[b[0]] and (j == 0 or c > last[batches[j - 1][0]])] for j, b in enumerate(batches)]

    def slot(i):
        return plan_ref[STAY_SLOT, i]

    for copy in [listed] + fresh:
        copy.wait()
    mixed = attend(
        batches, kbuf, vbuf, score, weight, cache, steps, wide // head,
        slot,
        lambda i: fresh_ref[slot(i), :, 0:wide],
        lambda i: (fresh_ref[slot(i), :, wide : wide + head], fresh_ref[slot(i), :, wide + head : wide + 2 * head]),
        lambda i: plan_ref[STAY_LENGTH, i],
        lambda b: [keys[c].wait() for c in due[b]],
        lambda b: [values[c].wait() for c in due[b]],
    )
    for j in range(rows // 4):
        for h in range(wide // head):
            tile = jnp.concatenate([o[h * steps : (h + 1) * steps] for o in mixed[4 * j : 4 * j + 4]], axis=0)
            heads_ref[16 * j : 16 * j + 16, h * head : (h + 1) * head] = tile.astype(BF16)
    for i in range(leave_keys_ref.shape[0]):
        leave_keys_ref[i] = kbuf[plan_ref[LEAVE_SLOT, i], 0:cache, :]
        leave_values_ref[i] = vbuf[plan_ref[LEAVE_SLOT, i], 0:cache, :]
    far.wait()
    cut = up_ref.shape[0]
    block = jnp.dot(heads_ref[...], wbuf[...], preferred_element_type=F32)
    up_ref[...] = block[:cut].astype(BF16)
    down_ref[...] = block[cut:].astype(BF16)


def hop_kernel(blocks, held, heads_ref, up_ref, down_ref, weight_ref, *rest):
    held_refs, rest = rest[:held], rest[held:]
    outs, kept, (ubuf, dbuf, sem, *scratch) = rest[:2], rest[2 : len(blocks)], rest[len(blocks) :]
    tokens, columns = heads_ref.shape[0], up_ref.shape[1]
    ring = weight_ref.shape[1] // columns
    parts = [*held_refs, *scratch, *kept]
    loads = {}
    for j in range(held, len(blocks)):
        at = pl.multiple_of(lax.rem(lax.axis_index("tp") + blocks[j], ring) * columns, columns)
        loads[j] = pltpu.make_async_copy(weight_ref.at[:, pl.ds(at, columns)], parts[j], sem.at[2 + j])
    sums = [pltpu.make_async_copy(up_ref, ubuf, sem.at[0]), pltpu.make_async_copy(down_ref, dbuf, sem.at[1])]
    for copy in [loads[j] for j in loads if j < 2] + sums + [loads[j] for j in loads if j >= 2]:
        copy.start()
    for j, (buf, out, first) in enumerate(((ubuf, outs[0], 0), (dbuf, outs[1], tokens - dbuf.shape[0]))):
        if j in loads:
            loads[j].wait()
        terms = jnp.dot(heads_ref[...], parts[j][...], preferred_element_type=F32)
        sums[j].wait()
        end = first + buf.shape[0]
        out[first:end, :] = (terms[first:end] + buf[...].astype(F32)).astype(BF16)
        if first > 0:
            out[:first, :] = terms[:first].astype(BF16)
        if end < tokens:
            out[end:, :] = terms[end:].astype(BF16)
    for j in loads:
        if j >= 2:
            loads[j].wait()


def leaving_kernel(plan_src, asked_ref, keys_ref, values_ref, out_ref, plan_ref, kbuf, vbuf, score, weight, psem):
    listed = pltpu.make_async_copy(plan_src, plan_ref, psem)
    listed.start()
    rows, cache, head = keys_ref.shape
    steps, wide = out_ref.shape[1:]
    out_ref[...] = jnp.zeros(out_ref.shape, BF16)
    for i in range(rows):
        kbuf[i, 0:cache, :] = keys_ref[i]
        vbuf[i, 0:cache, :] = values_ref[i]
    listed.wait()

    def entry(i):
        return plan_ref[LEAVE_ENTRY, i]

    mixed = attend(
        [list(range(rows))], kbuf, vbuf, score, weight, cache, steps, wide // head,
        lambda i: i,
        lambda i: asked_ref[entry(i), :, 0:wide],
        lambda i: (asked_ref[entry(i), :, wide : wide + head], asked_ref[entry(i), :, wide + head : wide + 2 * head]),
        lambda i: plan_ref[LEAVE_LENGTH, i],
        lambda b: None,
        lambda b: None,
    )
    for i, o in enumerate(mixed):
        for h in range(wide // head):
            out_ref[entry(i), :, h * head : (h + 1) * head] = o[h * steps : (h + 1) * steps].astype(BF16)


def arrived_kernel(here_src, back_ref, weight_ref, out_ref, here_ref, heads, wbuf, sums, hsem, wsem, osem):
    listed = pltpu.make_async_copy(here_src, here_ref, hsem)
    listed.start()
    steps = back_ref.shape[1]
    ring, lines, columns = out_ref.shape
    rows = lines // steps
    parts = [
        pltpu.make_async_copy(weight_ref.at[:, pl.ds(k * columns, columns)], wbuf.at[k], wsem.at[k])
        for k in range(ring)
    ]
    for copy in parts:
        copy.start()
    listed.wait()
    for j in range(heads.shape[0] // 16):
        four = [back_ref[here_ref[HERE_ENTRY, min(4 * j + u, rows - 1)]].astype(F32) for u in range(4)]
        heads[16 * j : 16 * j + 16, :] = jnp.concatenate(four, axis=0).astype(BF16)
    done = []
    for k, copy in enumerate(parts):
        copy.wait()
        terms = jnp.dot(heads[...], wbuf[k], preferred_element_type=F32)
        sums[k] = terms[:lines].astype(BF16)
        done.append(pltpu.make_async_copy(sums.at[k], out_ref.at[k], osem.at[k]))
        done[k].start()
    for copy in done:
        copy.wait()


def place_kernel(plan_ref, heads_ref, up_ref, down_ref, weight_ref, out_ref, total, wbuf, sem):
    steps, columns = out_ref.shape[1:]
    at = pl.multiple_of(lax.axis_index("tp") * columns, columns)
    copy = pltpu.make_async_copy(weight_ref.at[:, pl.ds(at, columns)], wbuf, sem)
    copy.start()
    out_ref[...] = jnp.zeros(out_ref.shape, BF16)
    copy.wait()
    own = jnp.dot(heads_ref[...], wbuf[...], preferred_element_type=F32)
    total[...] = own + up_ref[...].astype(F32) + down_ref[...].astype(F32)
    for i in range(heads_ref.shape[0] // steps):

        @pl.when(i >= plan_ref[STAY_FIRST, 0])
        def _():
            out_ref[plan_ref[STAY_SLOT, i]] = total[i * steps : (i + 1) * steps, :].astype(BF16)


def finish_kernel(here_src, placed_ref, blocks_ref, out_ref, here_ref, total, hsem):
    listed = pltpu.make_async_copy(here_src, here_ref, hsem)
    listed.start()
    steps = out_ref.shape[1]
    out_ref[...] = placed_ref[...]
    terms = blocks_ref[0].astype(F32)
    for k in range(1, blocks_ref.shape[0]):
        terms = terms + blocks_ref[k].astype(F32)
    total[...] = terms
    listed.wait()
    for n in range(blocks_ref.shape[1] // steps):
        out_ref[here_ref[HERE_SLOT, n]] = total[n * steps : (n + 1) * steps, :].astype(BF16)


def on_device(
    keys_cache,
    values_cache,
    lengths,
    guard_flags,
    migrations,
    queries,
    new_keys,
    new_values,
    out_weight,
):
    shape = jax.ShapeDtypeStruct
    slots, _, cache, head = keys_cache.shape
    steps, wide = queries.shape[1:]
    moves = migrations.shape[0]
    groups, ring = lax.axis_size("group"), lax.axis_size("tp")
    columns = out_weight.shape[1] // ring
    entries = groups * CAP
    staying = slots - 2 * moves
    lines = wide // head * steps
    positions = cache + FRESH
    barrier = lax.optimization_barrier
    keys_cache, values_cache, out_weight, queries, new_keys, new_values, moves_t, flags, reach = (
        pltpu.with_memory_space_constraint(x, pltpu.HBM)
        for x in (
            keys_cache, values_cache, out_weight, queries, new_keys, new_values,
            migrations.T, guard_flags.reshape(1, slots), lengths.reshape(1, slots),
        )
    )

    def exchange(x, axis):
        return lax.all_to_all(x, axis, split_axis=0, concat_axis=0, tiled=True)

    def scratch(held, rows):
        return [
            pltpu.VMEM((held, positions, head), BF16),
            pltpu.VMEM((held, positions, head), BF16),
            pltpu.VMEM((rows * lines, positions), F32),
            pltpu.VMEM((rows * lines, positions), BF16),
        ]

    table, plan = call(
        plan_kernel,
        [shape((groups, 128), I32), shape((8, slots), I32)],
        [ANY] * 3,
        [
            pltpu.VMEM((3, moves), I32),
            pltpu.VMEM((1, slots), I32),
            pltpu.VMEM((1, slots), I32),
            pltpu.SemaphoreType.DMA((3,)),
        ],
        nbytes=1 << 16,
    )(moves_t, flags, reach)
    table = exchange(table.reshape(groups, 1, 128), "group").reshape(groups, 128)

    tokens = staying * steps
    cut = -(-tokens // 32) * 16
    up, down, heads, fresh, leave_keys, leave_values = call(
        staying_kernel,
        [
            shape((cut, columns), BF16),
            shape((tokens - cut, columns), BF16),
            shape((tokens, wide), BF16),
            shape((slots, steps, wide + 2 * head), BF16),
            shape((moves, cache, head), BF16),
            shape((moves, cache, head), BF16),
        ],
        [pl.BlockSpec(memory_space=pl.ANY)] + [ANY] * 6,
        [pltpu.SMEM((8, slots), I32)]
        + scratch(slots, staying)
        + [
            pltpu.VMEM((wide, columns), BF16),
            pltpu.SemaphoreType.DMA,
            pltpu.SemaphoreType.DMA((3,)),
            pltpu.SemaphoreType.DMA((4,)),
            pltpu.SemaphoreType.DMA((4,)),
            pltpu.SemaphoreType.DMA,
        ],
        flops=2 * tokens * wide * columns,
        nbytes=16 << 20,
        exps=tokens * positions * 4,
        limit=24,
    )(plan, queries, new_keys, new_values, keys_cache, values_cache, out_weight)

    ahead = [(i, (i + 1) % ring) for i in range(ring)]
    astern = [(i, (i - 1) % ring) for i in range(ring)]

    def hop(u, d):
        return lax.ppermute(u, "tp", ahead), lax.ppermute(d, "tp", astern)

    part = ((wide, columns), BF16)

    def add(k, u, d, keep=(), held=()):
        blocks = (k, ring - k, *keep)
        return call(
            functools.partial(hop_kernel, blocks, len(held)),
            [shape((tokens, columns), BF16)] * 2 + [shape(*part)] * len(keep),
            [VMEM] + [pl.BlockSpec(memory_space=pl.ANY)] * 2 + [ANY] + [VMEM] * len(held),
            [pltpu.VMEM(u.shape, BF16), pltpu.VMEM(d.shape, BF16), pltpu.SemaphoreType.DMA((2 + ring,))]
            + [pltpu.VMEM(*part)] * (2 - len(held)),
            flops=HOP_COST,
        )(heads, u, d, out_weight, *held)

    table, fresh, heads, leave_keys = barrier((table, fresh, heads, leave_keys))
    asked, here = call(
        payload_kernel,
        [shape((entries, steps, wide + 2 * head), BF16), shape((8, 128), I32)],
        [pl.BlockSpec(memory_space=pl.ANY)] + [VMEM] * 2,
        [pltpu.SMEM((groups, 128), I32), pltpu.SemaphoreType.DMA],
        flops=PAYLOAD_COST,
    )(table, table, fresh)
    asked, heads = barrier((asked, heads))
    asked = exchange(asked, "group")
    up, down = hop(up, down)

    up, down = add(3, up, down)
    asked = barrier((asked, up, down))[0]
    up, down = hop(up, down)
    back = call(
        leaving_kernel,
        shape((entries, steps, wide), BF16),
        [pl.BlockSpec(memory_space=pl.ANY)] + [VMEM] * 3,
        [pltpu.SMEM((8, slots), I32)] + scratch(moves, moves) + [pltpu.SemaphoreType.DMA],
    )(plan, asked, leave_keys, leave_values)
    back, heads = barrier((back, heads))
    back = exchange(back, "group")
    up, down, *kept = add(2, up, down, keep=(1, ring - 1))
    back = barrier((back, up, down))[0]
    up, down = hop(up, down)
    arrived = moves * steps
    blocks = call(
        arrived_kernel,
        shape((ring, arrived, columns), BF16),
        [pl.BlockSpec(memory_space=pl.ANY), VMEM, ANY],
        [
            pltpu.SMEM((8, 128), I32),
            pltpu.VMEM((-(-arrived // 16) * 16, wide), BF16),
            pltpu.VMEM((ring, wide, columns), BF16),
            pltpu.VMEM((ring, arrived, columns), BF16),
            pltpu.SemaphoreType.DMA,
            pltpu.SemaphoreType.DMA((ring,)),
            pltpu.SemaphoreType.DMA((ring,)),
        ],
        out=ANY,
        flops=ARRIVED_COST,
        limit=10,
    )(here, back, out_weight)
    blocks, heads = barrier((blocks, heads))
    up, down = add(1, up, down, held=kept)
    blocks = barrier((blocks, up, down))[0]
    blocks = exchange(blocks, "tp")
    up, down = hop(up, down)

    placed = call(
        place_kernel,
        shape((slots, steps, columns), BF16),
        [SMEM] + [VMEM] * 3 + [ANY],
        [pltpu.VMEM((tokens, columns), F32), pltpu.VMEM((wide, columns), BF16), pltpu.SemaphoreType.DMA],
        flops=PLACE_COST,
    )(plan, heads, up, down, out_weight)
    return call(
        finish_kernel,
        shape((slots, steps, columns), BF16),
        [pl.BlockSpec(memory_space=pl.ANY)] + [VMEM] * 2,
        [pltpu.SMEM((8, 128), I32), pltpu.VMEM((arrived, columns), F32), pltpu.SemaphoreType.DMA],
        nbytes=2 << 20,
    )(here, placed, blocks)


def solution(mesh):
    return jax.shard_map(
        on_device,
        mesh=mesh,
        in_specs=(
            P("group", "tp", None, None),
            P("group", "tp", None, None),
            P("group"),
            P("group"),
            P("group", None),
            P("group", None, "tp"),
            P("group", None, "tp"),
            P("group", None, "tp"),
            P("tp", None),
        ),
        out_specs=P("group", None, "tp"),
        check_vma=False,
    )
```

```python
import functools

import jax
import jax.numpy as jnp
from jax import lax
from jax.experimental import pallas as pl
from jax.experimental.pallas import tpu as pltpu
from jax.sharding import PartitionSpec as P

CAP = 2
F32, BF16, I32 = jnp.float32, jnp.bfloat16, jnp.int32
FRESH = 16
PAYLOAD_COST, HOP_COST, ARRIVED_COST, PLACE_COST = 8_000_000_000, 20_000_000_000, 8_000_000_000, 40_000_000_000
VMEM = pl.BlockSpec(memory_space=pltpu.VMEM)
SMEM = pl.BlockSpec(memory_space=pltpu.SMEM)
ANY = pl.BlockSpec(memory_space=pltpu.HBM)


def call(kernel, out_shape, in_specs, scratch=(), flops=0, nbytes=0, exps=0, limit=8, out=VMEM):
    single = isinstance(out_shape, jax.ShapeDtypeStruct)
    return pl.pallas_call(
        kernel,
        out_shape=out_shape,
        in_specs=in_specs,
        out_specs=out if single else [out] * len(out_shape),
        scratch_shapes=list(scratch),
        cost_estimate=pl.CostEstimate(
            flops=flops, bytes_accessed=nbytes, transcendentals=exps
        ),
        compiler_params=pltpu.CompilerParams(vmem_limit_bytes=limit << 20),
    )


STAY_SLOT, STAY_LENGTH, LEAVE_SLOT, LEAVE_ENTRY, LEAVE_LENGTH, STAY_FIRST = range(6)


def lanes(rows, columns):
    return lax.broadcasted_iota(I32, (rows, columns), 1)


def lines_of(rows, columns):
    return lax.broadcasted_iota(I32, (rows, columns), 0)


def upright(row):
    n = row.shape[1]
    return jnp.sum(jnp.where(lanes(n, n) == lines_of(n, n), row, 0.0), axis=1, keepdims=True)


def plan_kernel(moves_hbm, flags_hbm, lengths_hbm, table_ref, plan_ref, moves_ref, flags_ref, lengths_ref, sem):
    copies = [
        pltpu.make_async_copy(src, dst, sem.at[i])
        for i, (src, dst) in enumerate(
            ((moves_hbm, moves_ref), (flags_hbm, flags_ref), (lengths_hbm, lengths_ref))
        )
    ]
    for copy in copies:
        copy.start()
    for copy in copies:
        copy.wait()
    groups, wide = table_ref.shape
    moves, slots = moves_ref.shape[1], flags_ref.shape[1]
    source, target = moves_ref[0:1, :], moves_ref[1:2, :]
    slot = (moves_ref[2:3, :] + 1).astype(F32)
    hit = lines_of(groups, moves) == target
    earlier = (lines_of(moves, moves) < lanes(moves, moves)).astype(F32)
    before = jnp.dot(hit.astype(F32), earlier, preferred_element_type=F32).astype(I32)
    table = jnp.zeros((groups, wide), I32)
    for c in range(CAP):
        entry = jnp.sum(jnp.where(hit & (before == c), slot, 0.0), axis=1, keepdims=True)
        table = jnp.where(lanes(groups, wide) == c, entry.astype(I32), table)
    table_ref[...] = table

    place = jnp.sum(jnp.where(hit, lines_of(groups, moves) * CAP + before, 0).astype(F32), axis=0, keepdims=True)
    lengths = lengths_ref[...].astype(F32)
    taken = (upright(source.astype(F32)).astype(I32) == lanes(moves, slots)).astype(F32)
    leave_length = jnp.sum(taken * lengths, axis=1, keepdims=True)
    leave_length = jnp.sum(
        jnp.where(lanes(moves, moves) == lines_of(moves, moves), leave_length, 0.0), axis=0, keepdims=True
    )
    gone = jnp.sum(taken, axis=0, keepdims=True)
    stays = ((flags_ref[...] == 0) & (gone == 0.0)).astype(F32)
    rank = jnp.sum(jnp.where(lanes(slots, slots) < lines_of(slots, slots), stays, 0.0), axis=1, keepdims=True)
    first = slots - 2 * moves - jnp.sum(stays, axis=1, keepdims=True)
    chosen = ((rank + first).astype(I32) == lanes(slots, slots)) & (upright(stays) > 0.0)
    listed = jnp.sum(jnp.where(chosen, lines_of(slots, slots).astype(F32), 0.0), axis=0, keepdims=True)
    listed_length = jnp.sum(jnp.where(chosen, upright(lengths), 0.0), axis=0, keepdims=True)
    plan_ref[...] = jnp.zeros(plan_ref.shape, I32)
    plan_ref[STAY_SLOT : STAY_SLOT + 1, :] = listed.astype(I32)
    plan_ref[STAY_LENGTH : STAY_LENGTH + 1, :] = listed_length.astype(I32)
    plan_ref[LEAVE_SLOT : LEAVE_SLOT + 1, 0:moves] = source
    plan_ref[LEAVE_ENTRY : LEAVE_ENTRY + 1, 0:moves] = place.astype(I32)
    plan_ref[LEAVE_LENGTH : LEAVE_LENGTH + 1, 0:moves] = leave_length.astype(I32)
    plan_ref[STAY_FIRST : STAY_FIRST + 1, 0:1] = first.astype(I32)


HERE_ENTRY, HERE_SLOT = range(2)


def payload_kernel(slot_src, table_ref, fresh_ref, out_ref, here_ref, slot_ref, sem):
    copy = pltpu.make_async_copy(slot_src, slot_ref, sem)
    copy.start()
    groups, width = table_ref.shape
    table = table_ref[...]
    there = (table > 0).astype(F32)
    earlier = (lanes(groups, groups) < lines_of(groups, groups)).astype(F32)
    before = jnp.dot(earlier, there, preferred_element_type=F32)
    whole = jnp.sum(there, axis=0, keepdims=True)
    entry = jnp.zeros((1, width), F32)
    slot = jnp.zeros((1, width), F32)
    base = jnp.zeros((1, 1), F32)
    for c in range(CAP):
        rank = (before[:, c : c + 1] + base).astype(I32)
        chosen = (rank == lanes(groups, width)) & (there[:, c : c + 1] > 0.0)
        entry += jnp.sum(jnp.where(chosen, (lines_of(groups, width) * CAP + c).astype(F32), 0.0), axis=0, keepdims=True)
        slot += jnp.sum(jnp.where(chosen, (table[:, c : c + 1] - 1).astype(F32), 0.0), axis=0, keepdims=True)
        base = base + whole[:, c : c + 1]
    here_ref[...] = jnp.zeros(here_ref.shape, I32)
    here_ref[HERE_ENTRY : HERE_ENTRY + 1, :] = entry.astype(I32)
    here_ref[HERE_SLOT : HERE_SLOT + 1, :] = slot.astype(I32)
    copy.wait()
    for e in range(out_ref.shape[0]):
        out_ref[e] = fresh_ref[jnp.maximum(slot_ref[e // CAP, e % CAP] - 1, 0)]


def attend(batches, kbuf, vbuf, score, weight, cache, steps, heads, row_of, query_of, fresh_of, length_of, await_keys, await_values):
    positions, head = kbuf.shape[1:]
    lines = heads * steps
    lane = lanes(lines, positions)
    step = lax.rem(lines_of(lines, positions), steps)
    visible = (lane >= cache) & (lane - cache <= step)

    def fresh_rows(value):
        pad = jnp.zeros((FRESH - steps, head), F32)
        return jnp.concatenate([value.astype(F32), pad], axis=0).astype(BF16)

    for b, batch in enumerate(batches):
        for i in batch:
            fresh_key, fresh_value = fresh_of(i)
            kbuf[row_of(i), cache:positions, :] = fresh_rows(fresh_key)
            vbuf[row_of(i), cache:positions, :] = fresh_rows(fresh_value)
        await_keys(b)
        for i in batch:
            query = query_of(i).astype(F32)
            query = jnp.concatenate([query[:, h * head : (h + 1) * head] for h in range(heads)], axis=0)
            products = lax.dot_general(
                query.astype(BF16), kbuf[row_of(i)], (((1,), (1,)), ((), ())), preferred_element_type=F32
            )
            score[i * lines : (i + 1) * lines, :] = jnp.where(
                (lane < length_of(i)) | visible, products * head**-0.5, -jnp.inf
            )
    mixed = []
    for b, batch in enumerate(batches):
        chunk = slice(batch[0] * lines, (batch[-1] + 1) * lines)
        s = score[chunk, :]
        e = jnp.exp(s - jnp.max(s, axis=1, keepdims=True))
        weight[chunk, :] = (e * (1.0 / jnp.sum(e, axis=1, keepdims=True))).astype(BF16)
        await_values(b)
        for i in batch:
            mixed.append(
                jnp.dot(weight[i * lines : (i + 1) * lines, :], vbuf[row_of(i)], preferred_element_type=F32)
            )
    return mixed


def staying_kernel(
    plan_src, query_ref, key_ref, value_ref, keys_ref, values_ref, weight_ref,
    up_ref, heads_ref, fresh_ref, leave_keys_ref, leave_values_ref,
    plan_ref, kbuf, vbuf, score, weight, wbuf, psem, fsem, ksem, vsem, wsem,
):
    steps, wide = query_ref.shape[1:]
    slots, _, cache, head = keys_ref.shape
    tokens, columns = heads_ref.shape[0], up_ref.shape[1]
    rows, ring = tokens // steps, weight_ref.shape[1] // columns
    chunk = slots // ksem.shape[0]
    fresh = [
        pltpu.make_async_copy(src, fresh_ref.at[:, :, pl.ds(at, src.shape[2])], fsem.at[i])
        for i, (src, at) in enumerate(((query_ref, 0), (key_ref, wide), (value_ref, wide + head)))
    ]
    keys, values = (
        [
            pltpu.make_async_copy(
                ref.at[pl.ds(c * chunk, chunk), 0], buf.at[pl.ds(c * chunk, chunk), pl.ds(0, cache)], sem.at[c]
            )
            for c in range(slots // chunk)
        ]
        for ref, buf, sem in ((keys_ref, kbuf, ksem), (values_ref, vbuf, vsem))
    )
    listed = pltpu.make_async_copy(plan_src, plan_ref, psem)
    at = lax.rem(lax.axis_index("tp") + ring // 2, ring) * columns
    far = pltpu.make_async_copy(weight_ref.at[:, pl.ds(pl.multiple_of(at, columns), columns)], wbuf, wsem)
    for copy in [listed] + fresh + keys + values + [far]:
        copy.start()

    last = [(slots - rows + i) // chunk for i in range(rows)]
    batches = [[i for i in range(rows) if last[i] == c] for c in sorted(set(last))]
    due = [[c for c in range(slots // chunk) if c <= last[b[0]] and (j == 0 or c > last[batches[j - 1][0]])] for j, b in enumerate(batches)]

    def slot(i):
        return plan_ref[STAY_SLOT, i]

    for copy in [listed] + fresh:
        copy.wait()
    mixed = attend(
        batches, kbuf, vbuf, score, weight, cache, steps, wide // head,
        slot,
        lambda i: fresh_ref[slot(i), :, 0:wide],
        lambda i: (fresh_ref[slot(i), :, wide : wide + head], fresh_ref[slot(i), :, wide + head : wide + 2 * head]),
        lambda i: plan_ref[STAY_LENGTH, i],
        lambda b: [keys[c].wait() for c in due[b]],
        lambda b: [values[c].wait() for c in due[b]],
    )
    for j in range(rows // 4):
        for h in range(wide // head):
            tile = jnp.concatenate([o[h * steps : (h + 1) * steps] for o in mixed[4 * j : 4 * j + 4]], axis=0)
            heads_ref[16 * j : 16 * j + 16, h * head : (h + 1) * head] = tile.astype(BF16)
    for i in range(leave_keys_ref.shape[0]):
        leave_keys_ref[i] = kbuf[plan_ref[LEAVE_SLOT, i], 0:cache, :]
        leave_values_ref[i] = vbuf[plan_ref[LEAVE_SLOT, i], 0:cache, :]
    far.wait()
    up_ref[...] = jnp.dot(heads_ref[...], wbuf[...], preferred_element_type=F32).astype(BF16)


def hop_kernel(blocks, came, held, heads_ref, *rest):
    sums, weight_ref, rest = rest[:came], rest[came], rest[came + 1 :]
    held_refs, rest = rest[:held], rest[held:]
    outs, kept, rest = rest[:2], rest[2 : len(blocks)], rest[len(blocks) :]
    bufs, sem, scratch = rest[:came], rest[came], rest[came + 1 :]
    columns = outs[0].shape[1]
    ring = weight_ref.shape[1] // columns
    parts = [*held_refs, *scratch, *kept]
    loads = {}
    for j in range(held, len(blocks)):
        at = pl.multiple_of(lax.rem(lax.axis_index("tp") + blocks[j], ring) * columns, columns)
        loads[j] = pltpu.make_async_copy(weight_ref.at[:, pl.ds(at, columns)], parts[j], sem.at[2 + j])
    sums = [pltpu.make_async_copy(src, dst, sem.at[i]) for i, (src, dst) in enumerate(zip(sums, bufs))]
    for copy in [loads[j] for j in loads if j < 2] + sums + [loads[j] for j in loads if j >= 2]:
        copy.start()
    for j, out in enumerate(outs):
        if j in loads:
            loads[j].wait()
        terms = jnp.dot(heads_ref[...], parts[j][...], preferred_element_type=F32)
        if j < came:
            sums[j].wait()
            terms = terms + bufs[j][...].astype(F32)
        out[...] = terms.astype(BF16)
    for j in loads:
        if j >= 2:
            loads[j].wait()


def leaving_kernel(plan_src, asked_ref, keys_ref, values_ref, out_ref, plan_ref, kbuf, vbuf, score, weight, psem):
    listed = pltpu.make_async_copy(plan_src, plan_ref, psem)
    listed.start()
    rows, cache, head = keys_ref.shape
    steps, wide = out_ref.shape[1:]
    out_ref[...] = jnp.zeros(out_ref.shape, BF16)
    for i in range(rows):
        kbuf[i, 0:cache, :] = keys_ref[i]
        vbuf[i, 0:cache, :] = values_ref[i]
    listed.wait()

    def entry(i):
        return plan_ref[LEAVE_ENTRY, i]

    mixed = attend(
        [list(range(rows))], kbuf, vbuf, score, weight, cache, steps, wide // head,
        lambda i: i,
        lambda i: asked_ref[entry(i), :, 0:wide],
        lambda i: (asked_ref[entry(i), :, wide : wide + head], asked_ref[entry(i), :, wide + head : wide + 2 * head]),
        lambda i: plan_ref[LEAVE_LENGTH, i],
        lambda b: None,
        lambda b: None,
    )
    for i, o in enumerate(mixed):
        for h in range(wide // head):
            out_ref[entry(i), :, h * head : (h + 1) * head] = o[h * steps : (h + 1) * steps].astype(BF16)


def arrived_kernel(here_src, back_ref, weight_ref, out_ref, here_ref, heads, wbuf, sums, hsem, wsem, osem):
    listed = pltpu.make_async_copy(here_src, here_ref, hsem)
    listed.start()
    steps = back_ref.shape[1]
    ring, lines, columns = out_ref.shape
    rows = lines // steps
    parts = [
        pltpu.make_async_copy(weight_ref.at[:, pl.ds(k * columns, columns)], wbuf.at[k], wsem.at[k])
        for k in range(ring)
    ]
    for copy in parts:
        copy.start()
    listed.wait()
    for j in range(heads.shape[0] // 16):
        four = [back_ref[here_ref[HERE_ENTRY, min(4 * j + u, rows - 1)]].astype(F32) for u in range(4)]
        heads[16 * j : 16 * j + 16, :] = jnp.concatenate(four, axis=0).astype(BF16)
    done = []
    for k, copy in enumerate(parts):
        copy.wait()
        terms = jnp.dot(heads[...], wbuf[k], preferred_element_type=F32)
        sums[k] = terms[:lines].astype(BF16)
        done.append(pltpu.make_async_copy(sums.at[k], out_ref.at[k], osem.at[k]))
        done[k].start()
    for copy in done:
        copy.wait()


def place_kernel(plan_ref, heads_ref, up_ref, down_ref, weight_ref, out_ref, total, wbuf, sem):
    steps, columns = out_ref.shape[1:]
    at = pl.multiple_of(lax.axis_index("tp") * columns, columns)
    copy = pltpu.make_async_copy(weight_ref.at[:, pl.ds(at, columns)], wbuf, sem)
    copy.start()
    out_ref[...] = jnp.zeros(out_ref.shape, BF16)
    copy.wait()
    own = jnp.dot(heads_ref[...], wbuf[...], preferred_element_type=F32)
    total[...] = own + up_ref[...].astype(F32) + down_ref[...].astype(F32)
    for i in range(heads_ref.shape[0] // steps):

        @pl.when(i >= plan_ref[STAY_FIRST, 0])
        def _():
            out_ref[plan_ref[STAY_SLOT, i]] = total[i * steps : (i + 1) * steps, :].astype(BF16)


def finish_kernel(here_src, placed_ref, blocks_ref, out_ref, here_ref, total, hsem):
    listed = pltpu.make_async_copy(here_src, here_ref, hsem)
    listed.start()
    steps = out_ref.shape[1]
    out_ref[...] = placed_ref[...]
    terms = blocks_ref[0].astype(F32)
    for k in range(1, blocks_ref.shape[0]):
        terms = terms + blocks_ref[k].astype(F32)
    total[...] = terms
    listed.wait()
    for n in range(blocks_ref.shape[1] // steps):
        out_ref[here_ref[HERE_SLOT, n]] = total[n * steps : (n + 1) * steps, :].astype(BF16)


def on_device(
    keys_cache,
    values_cache,
    lengths,
    guard_flags,
    migrations,
    queries,
    new_keys,
    new_values,
    out_weight,
):
    shape = jax.ShapeDtypeStruct
    slots, _, cache, head = keys_cache.shape
    steps, wide = queries.shape[1:]
    moves = migrations.shape[0]
    groups, ring = lax.axis_size("group"), lax.axis_size("tp")
    columns = out_weight.shape[1] // ring
    entries = groups * CAP
    staying = slots - 2 * moves
    lines = wide // head * steps
    positions = cache + FRESH
    barrier = lax.optimization_barrier
    keys_cache, values_cache, out_weight, queries, new_keys, new_values, moves_t, flags, reach = (
        pltpu.with_memory_space_constraint(x, pltpu.HBM)
        for x in (
            keys_cache, values_cache, out_weight, queries, new_keys, new_values,
            migrations.T, guard_flags.reshape(1, slots), lengths.reshape(1, slots),
        )
    )

    def exchange(x, axis):
        return lax.all_to_all(x, axis, split_axis=0, concat_axis=0, tiled=True)

    def scratch(held, rows):
        return [
            pltpu.VMEM((held, positions, head), BF16),
            pltpu.VMEM((held, positions, head), BF16),
            pltpu.VMEM((rows * lines, positions), F32),
            pltpu.VMEM((rows * lines, positions), BF16),
        ]

    table, plan = call(
        plan_kernel,
        [shape((groups, 128), I32), shape((8, slots), I32)],
        [ANY] * 3,
        [
            pltpu.VMEM((3, moves), I32),
            pltpu.VMEM((1, slots), I32),
            pltpu.VMEM((1, slots), I32),
            pltpu.SemaphoreType.DMA((3,)),
        ],
        nbytes=1 << 16,
    )(moves_t, flags, reach)
    table = exchange(table.reshape(groups, 1, 128), "group").reshape(groups, 128)

    tokens = staying * steps
    up, heads, fresh, leave_keys, leave_values = call(
        staying_kernel,
        [
            shape((tokens, columns), BF16),
            shape((tokens, wide), BF16),
            shape((slots, steps, wide + 2 * head), BF16),
            shape((moves, cache, head), BF16),
            shape((moves, cache, head), BF16),
        ],
        [pl.BlockSpec(memory_space=pl.ANY)] + [ANY] * 6,
        [pltpu.SMEM((8, slots), I32)]
        + scratch(slots, staying)
        + [
            pltpu.VMEM((wide, columns), BF16),
            pltpu.SemaphoreType.DMA,
            pltpu.SemaphoreType.DMA((3,)),
            pltpu.SemaphoreType.DMA((4,)),
            pltpu.SemaphoreType.DMA((4,)),
            pltpu.SemaphoreType.DMA,
        ],
        flops=2 * tokens * wide * columns,
        nbytes=16 << 20,
        exps=tokens * positions * 4,
        limit=24,
    )(plan, queries, new_keys, new_values, keys_cache, values_cache, out_weight)

    ahead = [(i, (i + 1) % ring) for i in range(ring)]
    astern = [(i, (i - 1) % ring) for i in range(ring)]

    def hop(u, d):
        return lax.ppermute(u, "tp", ahead), lax.ppermute(d, "tp", astern)

    part = ((wide, columns), BF16)

    def add(k, *sums, keep=(), held=()):
        blocks = (k, ring - k, *keep)
        return call(
            functools.partial(hop_kernel, blocks, len(sums), len(held)),
            [shape((tokens, columns), BF16)] * 2 + [shape(*part)] * len(keep),
            [VMEM] + [pl.BlockSpec(memory_space=pl.ANY)] * len(sums) + [ANY] + [VMEM] * len(held),
            [pltpu.VMEM(x.shape, BF16) for x in sums]
            + [pltpu.SemaphoreType.DMA((2 + ring,))]
            + [pltpu.VMEM(*part)] * (2 - len(held)),
            flops=HOP_COST,
        )(heads, *sums, out_weight, *held)

    table, fresh, heads, leave_keys = barrier((table, fresh, heads, leave_keys))
    asked, here = call(
        payload_kernel,
        [shape((entries, steps, wide + 2 * head), BF16), shape((8, 128), I32)],
        [pl.BlockSpec(memory_space=pl.ANY)] + [VMEM] * 2,
        [pltpu.SMEM((groups, 128), I32), pltpu.SemaphoreType.DMA],
        flops=PAYLOAD_COST,
    )(table, table, fresh)
    asked, heads = barrier((asked, heads))
    asked = exchange(asked, "group")
    up = lax.ppermute(up, "tp", ahead)

    up, down = add(3, up)
    asked = barrier((asked, up, down))[0]
    up, down = hop(up, down)
    back = call(
        leaving_kernel,
        shape((entries, steps, wide), BF16),
        [pl.BlockSpec(memory_space=pl.ANY)] + [VMEM] * 3,
        [pltpu.SMEM((8, slots), I32)] + scratch(moves, moves) + [pltpu.SemaphoreType.DMA],
    )(plan, asked, leave_keys, leave_values)
    back, heads = barrier((back, heads))
    back = exchange(back, "group")
    up, down, *kept = add(2, up, down, keep=(1, ring - 1))
    back = barrier((back, up, down))[0]
    up, down = hop(up, down)
    arrived = moves * steps
    blocks = call(
        arrived_kernel,
        shape((ring, arrived, columns), BF16),
        [pl.BlockSpec(memory_space=pl.ANY), VMEM, ANY],
        [
            pltpu.SMEM((8, 128), I32),
            pltpu.VMEM((-(-arrived // 16) * 16, wide), BF16),
            pltpu.VMEM((ring, wide, columns), BF16),
            pltpu.VMEM((ring, arrived, columns), BF16),
            pltpu.SemaphoreType.DMA,
            pltpu.SemaphoreType.DMA((ring,)),
            pltpu.SemaphoreType.DMA((ring,)),
        ],
        out=ANY,
        flops=ARRIVED_COST,
        limit=10,
    )(here, back, out_weight)
    blocks, heads = barrier((blocks, heads))
    up, down = add(1, up, down, held=kept)
    blocks = barrier((blocks, up, down))[0]
    blocks = exchange(blocks, "tp")
    up, down = hop(up, down)

    placed = call(
        place_kernel,
        shape((slots, steps, columns), BF16),
        [SMEM] + [VMEM] * 3 + [ANY],
        [pltpu.VMEM((tokens, columns), F32), pltpu.VMEM((wide, columns), BF16), pltpu.SemaphoreType.DMA],
        flops=PLACE_COST,
    )(plan, heads, up, down, out_weight)
    return call(
        finish_kernel,
        shape((slots, steps, columns), BF16),
        [pl.BlockSpec(memory_space=pl.ANY)] + [VMEM] * 2,
        [pltpu.SMEM((8, 128), I32), pltpu.VMEM((arrived, columns), F32), pltpu.SemaphoreType.DMA],
        nbytes=2 << 20,
    )(here, placed, blocks)


def solution(mesh):
    return jax.shard_map(
        on_device,
        mesh=mesh,
        in_specs=(
            P("group", "tp", None, None),
            P("group", "tp", None, None),
            P("group"),
            P("group"),
            P("group", None),
            P("group", None, "tp"),
            P("group", None, "tp"),
            P("group", None, "tp"),
            P("tp", None),
        ),
        out_specs=P("group", None, "tp"),
        check_vma=False,
    )
```

```python
import functools

import jax
import jax.numpy as jnp
from jax import lax
from jax.experimental import pallas as pl
from jax.experimental.pallas import tpu as pltpu
from jax.sharding import PartitionSpec as P

CAP = 2
F32, BF16, I32 = jnp.float32, jnp.bfloat16, jnp.int32
FRESH = 16
PAYLOAD_COST, HOP_COST, ARRIVED_COST, PLACE_COST = 8_000_000_000, 20_000_000_000, 8_000_000_000, 40_000_000_000
VMEM = pl.BlockSpec(memory_space=pltpu.VMEM)
SMEM = pl.BlockSpec(memory_space=pltpu.SMEM)
ANY = pl.BlockSpec(memory_space=pltpu.HBM)


def call(kernel, out_shape, in_specs, scratch=(), flops=0, nbytes=0, exps=0, limit=8, out=VMEM):
    single = isinstance(out_shape, jax.ShapeDtypeStruct)
    return pl.pallas_call(
        kernel,
        out_shape=out_shape,
        in_specs=in_specs,
        out_specs=out if single or isinstance(out, list) else [out] * len(out_shape),
        scratch_shapes=list(scratch),
        cost_estimate=pl.CostEstimate(
            flops=flops, bytes_accessed=nbytes, transcendentals=exps
        ),
        compiler_params=pltpu.CompilerParams(vmem_limit_bytes=limit << 20),
    )


STAY_SLOT, STAY_LENGTH, LEAVE_SLOT, LEAVE_ENTRY, LEAVE_LENGTH, STAY_FIRST = range(6)


def lanes(rows, columns):
    return lax.broadcasted_iota(I32, (rows, columns), 1)


def lines_of(rows, columns):
    return lax.broadcasted_iota(I32, (rows, columns), 0)


def upright(row):
    n = row.shape[1]
    return jnp.sum(jnp.where(lanes(n, n) == lines_of(n, n), row, 0.0), axis=1, keepdims=True)


def plan_kernel(moves_hbm, flags_hbm, lengths_hbm, table_ref, plan_ref, moves_ref, flags_ref, lengths_ref, sem):
    copies = [
        pltpu.make_async_copy(src, dst, sem.at[i])
        for i, (src, dst) in enumerate(
            ((moves_hbm, moves_ref), (flags_hbm, flags_ref), (lengths_hbm, lengths_ref))
        )
    ]
    for copy in copies:
        copy.start()
    for copy in copies:
        copy.wait()
    groups, wide = table_ref.shape
    moves, slots = moves_ref.shape[1], flags_ref.shape[1]
    source, target = moves_ref[0:1, :], moves_ref[1:2, :]
    slot = (moves_ref[2:3, :] + 1).astype(F32)
    hit = lines_of(groups, moves) == target
    earlier = (lines_of(moves, moves) < lanes(moves, moves)).astype(F32)
    before = jnp.dot(hit.astype(F32), earlier, preferred_element_type=F32).astype(I32)
    table = jnp.zeros((groups, wide), I32)
    for c in range(CAP):
        entry = jnp.sum(jnp.where(hit & (before == c), slot, 0.0), axis=1, keepdims=True)
        table = jnp.where(lanes(groups, wide) == c, entry.astype(I32), table)
    table_ref[...] = table

    place = jnp.sum(jnp.where(hit, lines_of(groups, moves) * CAP + before, 0).astype(F32), axis=0, keepdims=True)
    lengths = lengths_ref[...].astype(F32)
    taken = (upright(source.astype(F32)).astype(I32) == lanes(moves, slots)).astype(F32)
    leave_length = jnp.sum(taken * lengths, axis=1, keepdims=True)
    leave_length = jnp.sum(
        jnp.where(lanes(moves, moves) == lines_of(moves, moves), leave_length, 0.0), axis=0, keepdims=True
    )
    gone = jnp.sum(taken, axis=0, keepdims=True)
    stays = ((flags_ref[...] == 0) & (gone == 0.0)).astype(F32)
    rank = jnp.sum(jnp.where(lanes(slots, slots) < lines_of(slots, slots), stays, 0.0), axis=1, keepdims=True)
    first = slots - 2 * moves - jnp.sum(stays, axis=1, keepdims=True)
    chosen = ((rank + first).astype(I32) == lanes(slots, slots)) & (upright(stays) > 0.0)
    listed = jnp.sum(jnp.where(chosen, lines_of(slots, slots).astype(F32), 0.0), axis=0, keepdims=True)
    listed_length = jnp.sum(jnp.where(chosen, upright(lengths), 0.0), axis=0, keepdims=True)
    plan_ref[...] = jnp.zeros(plan_ref.shape, I32)
    plan_ref[STAY_SLOT : STAY_SLOT + 1, :] = listed.astype(I32)
    plan_ref[STAY_LENGTH : STAY_LENGTH + 1, :] = listed_length.astype(I32)
    plan_ref[LEAVE_SLOT : LEAVE_SLOT + 1, 0:moves] = source
    plan_ref[LEAVE_ENTRY : LEAVE_ENTRY + 1, 0:moves] = place.astype(I32)
    plan_ref[LEAVE_LENGTH : LEAVE_LENGTH + 1, 0:moves] = leave_length.astype(I32)
    plan_ref[STAY_FIRST : STAY_FIRST + 1, 0:1] = first.astype(I32)


HERE_ENTRY, HERE_SLOT = range(2)


def payload_kernel(slot_src, table_ref, fresh_ref, out_ref, here_ref, slot_ref, sem):
    copy = pltpu.make_async_copy(slot_src, slot_ref, sem)
    copy.start()
    groups, width = table_ref.shape
    table = table_ref[...]
    there = (table > 0).astype(F32)
    earlier = (lanes(groups, groups) < lines_of(groups, groups)).astype(F32)
    before = jnp.dot(earlier, there, preferred_element_type=F32)
    whole = jnp.sum(there, axis=0, keepdims=True)
    entry = jnp.zeros((1, width), F32)
    slot = jnp.zeros((1, width), F32)
    base = jnp.zeros((1, 1), F32)
    for c in range(CAP):
        rank = (before[:, c : c + 1] + base).astype(I32)
        chosen = (rank == lanes(groups, width)) & (there[:, c : c + 1] > 0.0)
        entry += jnp.sum(jnp.where(chosen, (lines_of(groups, width) * CAP + c).astype(F32), 0.0), axis=0, keepdims=True)
        slot += jnp.sum(jnp.where(chosen, (table[:, c : c + 1] - 1).astype(F32), 0.0), axis=0, keepdims=True)
        base = base + whole[:, c : c + 1]
    here_ref[...] = jnp.zeros(here_ref.shape, I32)
    here_ref[HERE_ENTRY : HERE_ENTRY + 1, :] = entry.astype(I32)
    here_ref[HERE_SLOT : HERE_SLOT + 1, :] = slot.astype(I32)
    copy.wait()
    for e in range(out_ref.shape[0]):
        out_ref[e] = fresh_ref[jnp.maximum(slot_ref[e // CAP, e % CAP] - 1, 0)]


def attend(batches, kbuf, vbuf, score, weight, cache, steps, heads, row_of, query_of, fresh_of, length_of, await_keys, await_values):
    positions, head = kbuf.shape[1:]
    lines = heads * steps
    lane = lanes(lines, positions)
    step = lax.rem(lines_of(lines, positions), steps)
    visible = (lane >= cache) & (lane - cache <= step)

    def fresh_rows(value):
        pad = jnp.zeros((FRESH - steps, head), F32)
        return jnp.concatenate([value.astype(F32), pad], axis=0).astype(BF16)

    for b, batch in enumerate(batches):
        for i in batch:
            fresh_key, fresh_value = fresh_of(i)
            kbuf[row_of(i), cache:positions, :] = fresh_rows(fresh_key)
            vbuf[row_of(i), cache:positions, :] = fresh_rows(fresh_value)
        await_keys(b)
        for i in batch:
            query = query_of(i).astype(F32)
            query = jnp.concatenate([query[:, h * head : (h + 1) * head] for h in range(heads)], axis=0)
            products = lax.dot_general(
                query.astype(BF16), kbuf[row_of(i)], (((1,), (1,)), ((), ())), preferred_element_type=F32
            )
            score[i * lines : (i + 1) * lines, :] = jnp.where(
                (lane < length_of(i)) | visible, products * head**-0.5, -jnp.inf
            )
    mixed = []
    for b, batch in enumerate(batches):
        chunk = slice(batch[0] * lines, (batch[-1] + 1) * lines)
        s = score[chunk, :]
        e = jnp.exp(s - jnp.max(s, axis=1, keepdims=True))
        weight[chunk, :] = (e * (1.0 / jnp.sum(e, axis=1, keepdims=True))).astype(BF16)
        await_values(b)
        for i in batch:
            mixed.append(
                jnp.dot(weight[i * lines : (i + 1) * lines, :], vbuf[row_of(i)], preferred_element_type=F32)
            )
    return mixed


def staying_kernel(
    plan_src, query_ref, key_ref, value_ref, keys_ref, values_ref, weight_ref,
    up_ref, heads_ref, fresh_ref, leave_keys_ref, leave_values_ref,
    plan_ref, kbuf, vbuf, score, weight, wbuf, psem, fsem, ksem, vsem, wsem,
):
    steps, wide = query_ref.shape[1:]
    slots, _, cache, head = keys_ref.shape
    tokens, columns = heads_ref.shape[0], up_ref.shape[1]
    rows, ring = tokens // steps, weight_ref.shape[1] // columns
    chunk = slots // ksem.shape[0]
    fresh = [
        pltpu.make_async_copy(src, fresh_ref.at[:, :, pl.ds(at, src.shape[2])], fsem.at[i])
        for i, (src, at) in enumerate(((query_ref, 0), (key_ref, wide), (value_ref, wide + head)))
    ]
    keys, values = (
        [
            pltpu.make_async_copy(
                ref.at[pl.ds(c * chunk, chunk), 0], buf.at[pl.ds(c * chunk, chunk), pl.ds(0, cache)], sem.at[c]
            )
            for c in range(slots // chunk)
        ]
        for ref, buf, sem in ((keys_ref, kbuf, ksem), (values_ref, vbuf, vsem))
    )
    listed = pltpu.make_async_copy(plan_src, plan_ref, psem)
    at = lax.rem(lax.axis_index("tp") + ring // 2, ring) * columns
    far = pltpu.make_async_copy(weight_ref.at[:, pl.ds(pl.multiple_of(at, columns), columns)], wbuf, wsem)
    for copy in [listed] + fresh + keys + values + [far]:
        copy.start()

    last = [(slots - rows + i) // chunk for i in range(rows)]
    batches = [[i for i in range(rows) if last[i] == c] for c in sorted(set(last))]
    due = [[c for c in range(slots // chunk) if c <= last[b[0]] and (j == 0 or c > last[batches[j - 1][0]])] for j, b in enumerate(batches)]

    def slot(i):
        return plan_ref[STAY_SLOT, i]

    for copy in [listed] + fresh:
        copy.wait()
    mixed = attend(
        batches, kbuf, vbuf, score, weight, cache, steps, wide // head,
        slot,
        lambda i: fresh_ref[slot(i), :, 0:wide],
        lambda i: (fresh_ref[slot(i), :, wide : wide + head], fresh_ref[slot(i), :, wide + head : wide + 2 * head]),
        lambda i: plan_ref[STAY_LENGTH, i],
        lambda b: [keys[c].wait() for c in due[b]],
        lambda b: [values[c].wait() for c in due[b]],
    )
    for j in range(rows // 4):
        for h in range(wide // head):
            tile = jnp.concatenate([o[h * steps : (h + 1) * steps] for o in mixed[4 * j : 4 * j + 4]], axis=0)
            heads_ref[16 * j : 16 * j + 16, h * head : (h + 1) * head] = tile.astype(BF16)
    for i in range(leave_keys_ref.shape[0]):
        leave_keys_ref[i] = kbuf[plan_ref[LEAVE_SLOT, i], 0:cache, :]
        leave_values_ref[i] = vbuf[plan_ref[LEAVE_SLOT, i], 0:cache, :]
    far.wait()
    up_ref[...] = jnp.dot(heads_ref[...], wbuf[...], preferred_element_type=F32).astype(BF16)


def load_blocks(blocks, weight_ref, parts, sem):
    columns = parts[0].shape[1] if parts else 1
    ring = weight_ref.shape[1] // columns
    copies = []
    for j, step in enumerate(blocks):
        at = pl.multiple_of(lax.rem(lax.axis_index("tp") + step, ring) * columns, columns)
        copies.append(pltpu.make_async_copy(weight_ref.at[:, pl.ds(at, columns)], parts[j], sem.at[j]))
    return copies


def hop_kernel(blocks, came, held, heads_ref, *rest):
    sums, weight_ref, rest = rest[:came], rest[came], rest[came + 1 :]
    held_refs, rest = rest[:held], rest[held:]
    outs, kept, rest = rest[:2], rest[2 : len(blocks)], rest[len(blocks) :]
    bufs, sem, scratch = rest[:came], rest[came], rest[came + 1 :]
    parts = [*held_refs, *scratch, *kept]
    loads = dict(enumerate(load_blocks(blocks[held:], weight_ref, parts[held:], sem.at[pl.ds(2, 8)]), held))
    sums = [pltpu.make_async_copy(src, dst, sem.at[i]) for i, (src, dst) in enumerate(zip(sums, bufs))]
    for copy in [loads[j] for j in loads if j < 2] + sums + [loads[j] for j in loads if j >= 2]:
        copy.start()
    for j, out in enumerate(outs):
        if j in loads:
            loads[j].wait()
        terms = jnp.dot(heads_ref[...], parts[j][...], preferred_element_type=F32)
        if j < came:
            sums[j].wait()
            terms = terms + bufs[j][...].astype(F32)
        out[...] = terms.astype(BF16)
    for j in loads:
        if j >= 2:
            loads[j].wait()


def leaving_kernel(plan_src, asked_ref, keys_ref, values_ref, out_ref, plan_ref, kbuf, vbuf, score, weight, psem):
    listed = pltpu.make_async_copy(plan_src, plan_ref, psem)
    listed.start()
    rows, cache, head = keys_ref.shape
    steps, wide = out_ref.shape[1:]
    out_ref[...] = jnp.zeros(out_ref.shape, BF16)
    for i in range(rows):
        kbuf[i, 0:cache, :] = keys_ref[i]
        vbuf[i, 0:cache, :] = values_ref[i]
    listed.wait()

    def entry(i):
        return plan_ref[LEAVE_ENTRY, i]

    mixed = attend(
        [list(range(rows))], kbuf, vbuf, score, weight, cache, steps, wide // head,
        lambda i: i,
        lambda i: asked_ref[entry(i), :, 0:wide],
        lambda i: (asked_ref[entry(i), :, wide : wide + head], asked_ref[entry(i), :, wide + head : wide + 2 * head]),
        lambda i: plan_ref[LEAVE_LENGTH, i],
        lambda b: None,
        lambda b: None,
    )
    for i, o in enumerate(mixed):
        for h in range(wide // head):
            out_ref[entry(i), :, h * head : (h + 1) * head] = o[h * steps : (h + 1) * steps].astype(BF16)


def arrived_kernel(order, here_src, back_ref, weight_ref, out_ref, *rest):
    kept, (here_ref, heads, wbuf, sums, hsem, wsem, osem) = rest[:2], rest[2:]
    listed = pltpu.make_async_copy(here_src, here_ref, hsem)
    listed.start()
    steps = back_ref.shape[1]
    ring, lines, _ = out_ref.shape
    rows = lines // steps
    parts = [*kept, *(wbuf.at[j] for j in range(ring - 2))]
    loads = load_blocks(order, weight_ref, parts, wsem)
    for copy in loads:
        copy.start()
    listed.wait()
    for j in range(heads.shape[0] // 16):
        four = [back_ref[here_ref[HERE_ENTRY, min(4 * j + u, rows - 1)]].astype(F32) for u in range(4)]
        heads[16 * j : 16 * j + 16, :] = jnp.concatenate(four, axis=0).astype(BF16)
    done = []
    for j, k in enumerate(order):
        loads[j].wait()
        terms = jnp.dot(heads[...], parts[j][...], preferred_element_type=F32)
        sums[j] = terms[:lines].astype(BF16)
        to = lax.rem(lax.axis_index("tp") + k, ring)
        done.append(pltpu.make_async_copy(sums.at[j], out_ref.at[to], osem.at[j]))
        done[j].start()
    for copy in done:
        copy.wait()


def place_kernel(plan_ref, heads_ref, up_ref, down_ref, weight_ref, out_ref, total, wbuf, sem):
    steps, columns = out_ref.shape[1:]
    at = pl.multiple_of(lax.axis_index("tp") * columns, columns)
    copy = pltpu.make_async_copy(weight_ref.at[:, pl.ds(at, columns)], wbuf, sem)
    copy.start()
    out_ref[...] = jnp.zeros(out_ref.shape, BF16)
    copy.wait()
    own = jnp.dot(heads_ref[...], wbuf[...], preferred_element_type=F32)
    total[...] = own + up_ref[...].astype(F32) + down_ref[...].astype(F32)
    for i in range(heads_ref.shape[0] // steps):

        @pl.when(i >= plan_ref[STAY_FIRST, 0])
        def _():
            out_ref[plan_ref[STAY_SLOT, i]] = total[i * steps : (i + 1) * steps, :].astype(BF16)


def finish_kernel(here_src, placed_ref, blocks_ref, out_ref, here_ref, total, hsem):
    listed = pltpu.make_async_copy(here_src, here_ref, hsem)
    listed.start()
    steps = out_ref.shape[1]
    out_ref[...] = placed_ref[...]
    terms = blocks_ref[0].astype(F32)
    for k in range(1, blocks_ref.shape[0]):
        terms = terms + blocks_ref[k].astype(F32)
    total[...] = terms
    listed.wait()
    for n in range(blocks_ref.shape[1] // steps):
        out_ref[here_ref[HERE_SLOT, n]] = total[n * steps : (n + 1) * steps, :].astype(BF16)


def on_device(
    keys_cache,
    values_cache,
    lengths,
    guard_flags,
    migrations,
    queries,
    new_keys,
    new_values,
    out_weight,
):
    shape = jax.ShapeDtypeStruct
    slots, _, cache, head = keys_cache.shape
    steps, wide = queries.shape[1:]
    moves = migrations.shape[0]
    groups, ring = lax.axis_size("group"), lax.axis_size("tp")
    columns = out_weight.shape[1] // ring
    entries = groups * CAP
    staying = slots - 2 * moves
    lines = wide // head * steps
    positions = cache + FRESH
    barrier = lax.optimization_barrier
    keys_cache, values_cache, out_weight, queries, new_keys, new_values, moves_t, flags, reach = (
        pltpu.with_memory_space_constraint(x, pltpu.HBM)
        for x in (
            keys_cache, values_cache, out_weight, queries, new_keys, new_values,
            migrations.T, guard_flags.reshape(1, slots), lengths.reshape(1, slots),
        )
    )

    def exchange(x, axis):
        return lax.all_to_all(x, axis, split_axis=0, concat_axis=0, tiled=True)

    def scratch(held, rows):
        return [
            pltpu.VMEM((held, positions, head), BF16),
            pltpu.VMEM((held, positions, head), BF16),
            pltpu.VMEM((rows * lines, positions), F32),
            pltpu.VMEM((rows * lines, positions), BF16),
        ]

    table, plan = call(
        plan_kernel,
        [shape((groups, 128), I32), shape((8, slots), I32)],
        [ANY] * 3,
        [
            pltpu.VMEM((3, moves), I32),
            pltpu.VMEM((1, slots), I32),
            pltpu.VMEM((1, slots), I32),
            pltpu.SemaphoreType.DMA((3,)),
        ],
        nbytes=1 << 16,
    )(moves_t, flags, reach)
    table = exchange(table.reshape(groups, 1, 128), "group").reshape(groups, 128)

    tokens = staying * steps
    up, heads, fresh, leave_keys, leave_values = call(
        staying_kernel,
        [
            shape((tokens, columns), BF16),
            shape((tokens, wide), BF16),
            shape((slots, steps, wide + 2 * head), BF16),
            shape((moves, cache, head), BF16),
            shape((moves, cache, head), BF16),
        ],
        [pl.BlockSpec(memory_space=pl.ANY)] + [ANY] * 6,
        [pltpu.SMEM((8, slots), I32)]
        + scratch(slots, staying)
        + [
            pltpu.VMEM((wide, columns), BF16),
            pltpu.SemaphoreType.DMA,
            pltpu.SemaphoreType.DMA((3,)),
            pltpu.SemaphoreType.DMA((4,)),
            pltpu.SemaphoreType.DMA((4,)),
            pltpu.SemaphoreType.DMA,
        ],
        flops=2 * tokens * wide * columns,
        nbytes=16 << 20,
        exps=tokens * positions * 4,
        limit=24,
    )(plan, queries, new_keys, new_values, keys_cache, values_cache, out_weight)

    ahead = [(i, (i + 1) % ring) for i in range(ring)]
    astern = [(i, (i - 1) % ring) for i in range(ring)]

    def hop(u, d):
        return lax.ppermute(u, "tp", ahead), lax.ppermute(d, "tp", astern)

    part = ((wide, columns), BF16)

    def add(k, *sums, keep=(), held=()):
        blocks = (k, ring - k, *keep)
        return call(
            functools.partial(hop_kernel, blocks, len(sums), len(held)),
            [shape((tokens, columns), BF16)] * 2 + [shape(*part)] * len(keep),
            [VMEM] + [pl.BlockSpec(memory_space=pl.ANY)] * len(sums) + [ANY] + [VMEM] * len(held),
            [pltpu.VMEM(x.shape, BF16) for x in sums]
            + [pltpu.SemaphoreType.DMA((2 + ring,))]
            + [pltpu.VMEM(*part)] * (2 - len(held)),
            flops=HOP_COST,
        )(heads, *sums, out_weight, *held)

    table, fresh, heads, leave_keys = barrier((table, fresh, heads, leave_keys))
    asked, here = call(
        payload_kernel,
        [shape((entries, steps, wide + 2 * head), BF16), shape((8, 128), I32)],
        [pl.BlockSpec(memory_space=pl.ANY)] + [VMEM] * 2,
        [pltpu.SMEM((groups, 128), I32), pltpu.SemaphoreType.DMA],
        flops=PAYLOAD_COST,
    )(table, table, fresh)
    asked, heads = barrier((asked, heads))
    asked = exchange(asked, "group")
    up = lax.ppermute(up, "tp", ahead)

    up, down = add(3, up)
    asked = barrier((asked, up, down))[0]
    up, down = hop(up, down)
    back = call(
        leaving_kernel,
        shape((entries, steps, wide), BF16),
        [pl.BlockSpec(memory_space=pl.ANY)] + [VMEM] * 3,
        [pltpu.SMEM((8, slots), I32)] + scratch(moves, moves) + [pltpu.SemaphoreType.DMA],
    )(plan, asked, leave_keys, leave_values)
    back, heads = barrier((back, heads))
    back = exchange(back, "group")
    up, down = add(2, up, down)
    back = barrier((back, up, down))[0]
    up, down = hop(up, down)
    arrived = moves * steps
    order = (1, ring - 1, 0, *range(2, ring - 1))
    blocks, *late = call(
        functools.partial(arrived_kernel, order),
        [shape((ring, arrived, columns), BF16)] + [shape(*part)] * 2,
        [pl.BlockSpec(memory_space=pl.ANY), VMEM, ANY],
        [
            pltpu.SMEM((8, 128), I32),
            pltpu.VMEM((-(-arrived // 16) * 16, wide), BF16),
            pltpu.VMEM((ring - 2, wide, columns), BF16),
            pltpu.VMEM((ring, arrived, columns), BF16),
            pltpu.SemaphoreType.DMA,
            pltpu.SemaphoreType.DMA((ring,)),
            pltpu.SemaphoreType.DMA((ring,)),
        ],
        out=[ANY, VMEM, VMEM],
        flops=ARRIVED_COST,
        limit=10,
    )(here, back, out_weight)
    blocks, heads = barrier((blocks, heads))
    up, down = add(1, up, down, held=late)
    blocks = barrier((blocks, up, down))[0]
    blocks = exchange(blocks, "tp")
    up, down = hop(up, down)

    placed = call(
        place_kernel,
        shape((slots, steps, columns), BF16),
        [SMEM] + [VMEM] * 3 + [ANY],
        [pltpu.VMEM((tokens, columns), F32), pltpu.VMEM((wide, columns), BF16), pltpu.SemaphoreType.DMA],
        flops=PLACE_COST,
    )(plan, heads, up, down, out_weight)
    return call(
        finish_kernel,
        shape((slots, steps, columns), BF16),
        [pl.BlockSpec(memory_space=pl.ANY)] + [VMEM] * 2,
        [pltpu.SMEM((8, 128), I32), pltpu.VMEM((arrived, columns), F32), pltpu.SemaphoreType.DMA],
        nbytes=2 << 20,
    )(here, placed, blocks)


def solution(mesh):
    return jax.shard_map(
        on_device,
        mesh=mesh,
        in_specs=(
            P("group", "tp", None, None),
            P("group", "tp", None, None),
            P("group"),
            P("group"),
            P("group", None),
            P("group", None, "tp"),
            P("group", None, "tp"),
            P("group", None, "tp"),
            P("tp", None),
        ),
        out_specs=P("group", None, "tp"),
        check_vma=False,
    )
```

```python
import functools

import jax
import jax.numpy as jnp
from jax import lax
from jax.experimental import pallas as pl
from jax.experimental.pallas import tpu as pltpu
from jax.sharding import PartitionSpec as P

CAP = 2
F32, BF16, I32 = jnp.float32, jnp.bfloat16, jnp.int32
FRESH = 16
PAYLOAD_COST, HOP_COST, ARRIVED_COST, PLACE_COST = 8_000_000_000, 20_000_000_000, 8_000_000_000, 40_000_000_000
VMEM = pl.BlockSpec(memory_space=pltpu.VMEM)
SMEM = pl.BlockSpec(memory_space=pltpu.SMEM)
ANY = pl.BlockSpec(memory_space=pltpu.HBM)


def call(kernel, out_shape, in_specs, scratch=(), flops=0, nbytes=0, exps=0, limit=8, out=VMEM):
    single = isinstance(out_shape, jax.ShapeDtypeStruct)
    return pl.pallas_call(
        kernel,
        out_shape=out_shape,
        in_specs=in_specs,
        out_specs=out if single or isinstance(out, list) else [out] * len(out_shape),
        scratch_shapes=list(scratch),
        cost_estimate=pl.CostEstimate(
            flops=flops, bytes_accessed=nbytes, transcendentals=exps
        ),
        compiler_params=pltpu.CompilerParams(vmem_limit_bytes=limit << 20),
    )


STAY_SLOT, STAY_LENGTH, LEAVE_SLOT, LEAVE_ENTRY, LEAVE_LENGTH, STAY_FIRST = range(6)


def lanes(rows, columns):
    return lax.broadcasted_iota(I32, (rows, columns), 1)


def lines_of(rows, columns):
    return lax.broadcasted_iota(I32, (rows, columns), 0)


def upright(row):
    n = row.shape[1]
    return jnp.sum(jnp.where(lanes(n, n) == lines_of(n, n), row, 0.0), axis=1, keepdims=True)


def plan_kernel(moves_hbm, flags_hbm, lengths_hbm, table_ref, plan_ref, moves_ref, flags_ref, lengths_ref, sem):
    copies = [
        pltpu.make_async_copy(src, dst, sem.at[i])
        for i, (src, dst) in enumerate(
            ((moves_hbm, moves_ref), (flags_hbm, flags_ref), (lengths_hbm, lengths_ref))
        )
    ]
    for copy in copies:
        copy.start()
    for copy in copies:
        copy.wait()
    groups, wide = table_ref.shape
    moves, slots = moves_ref.shape[1], flags_ref.shape[1]
    source, target = moves_ref[0:1, :], moves_ref[1:2, :]
    slot = (moves_ref[2:3, :] + 1).astype(F32)
    hit = lines_of(groups, moves) == target
    earlier = (lines_of(moves, moves) < lanes(moves, moves)).astype(F32)
    before = jnp.dot(hit.astype(F32), earlier, preferred_element_type=F32).astype(I32)
    table = jnp.zeros((groups, wide), I32)
    for c in range(CAP):
        entry = jnp.sum(jnp.where(hit & (before == c), slot, 0.0), axis=1, keepdims=True)
        table = jnp.where(lanes(groups, wide) == c, entry.astype(I32), table)
    table_ref[...] = table

    place = jnp.sum(jnp.where(hit, lines_of(groups, moves) * CAP + before, 0).astype(F32), axis=0, keepdims=True)
    lengths = lengths_ref[...].astype(F32)
    taken = (upright(source.astype(F32)).astype(I32) == lanes(moves, slots)).astype(F32)
    leave_length = jnp.sum(taken * lengths, axis=1, keepdims=True)
    leave_length = jnp.sum(
        jnp.where(lanes(moves, moves) == lines_of(moves, moves), leave_length, 0.0), axis=0, keepdims=True
    )
    gone = jnp.sum(taken, axis=0, keepdims=True)
    stays = ((flags_ref[...] == 0) & (gone == 0.0)).astype(F32)
    rank = jnp.sum(jnp.where(lanes(slots, slots) < lines_of(slots, slots), stays, 0.0), axis=1, keepdims=True)
    first = slots - 2 * moves - jnp.sum(stays, axis=1, keepdims=True)
    chosen = ((rank + first).astype(I32) == lanes(slots, slots)) & (upright(stays) > 0.0)
    listed = jnp.sum(jnp.where(chosen, lines_of(slots, slots).astype(F32), 0.0), axis=0, keepdims=True)
    listed_length = jnp.sum(jnp.where(chosen, upright(lengths), 0.0), axis=0, keepdims=True)
    plan_ref[...] = jnp.zeros(plan_ref.shape, I32)
    plan_ref[STAY_SLOT : STAY_SLOT + 1, :] = listed.astype(I32)
    plan_ref[STAY_LENGTH : STAY_LENGTH + 1, :] = listed_length.astype(I32)
    plan_ref[LEAVE_SLOT : LEAVE_SLOT + 1, 0:moves] = source
    plan_ref[LEAVE_ENTRY : LEAVE_ENTRY + 1, 0:moves] = place.astype(I32)
    plan_ref[LEAVE_LENGTH : LEAVE_LENGTH + 1, 0:moves] = leave_length.astype(I32)
    plan_ref[STAY_FIRST : STAY_FIRST + 1, 0:1] = first.astype(I32)


HERE_ENTRY, HERE_SLOT = range(2)


def payload_kernel(slot_src, table_ref, fresh_ref, out_ref, here_ref, slot_ref, sem):
    copy = pltpu.make_async_copy(slot_src, slot_ref, sem)
    copy.start()
    groups, width = table_ref.shape
    table = table_ref[...]
    there = (table > 0).astype(F32)
    earlier = (lanes(groups, groups) < lines_of(groups, groups)).astype(F32)
    before = jnp.dot(earlier, there, preferred_element_type=F32)
    whole = jnp.sum(there, axis=0, keepdims=True)
    entry = jnp.zeros((1, width), F32)
    slot = jnp.zeros((1, width), F32)
    base = jnp.zeros((1, 1), F32)
    for c in range(CAP):
        rank = (before[:, c : c + 1] + base).astype(I32)
        chosen = (rank == lanes(groups, width)) & (there[:, c : c + 1] > 0.0)
        entry += jnp.sum(jnp.where(chosen, (lines_of(groups, width) * CAP + c).astype(F32), 0.0), axis=0, keepdims=True)
        slot += jnp.sum(jnp.where(chosen, (table[:, c : c + 1] - 1).astype(F32), 0.0), axis=0, keepdims=True)
        base = base + whole[:, c : c + 1]
    here_ref[...] = jnp.zeros(here_ref.shape, I32)
    here_ref[HERE_ENTRY : HERE_ENTRY + 1, :] = entry.astype(I32)
    here_ref[HERE_SLOT : HERE_SLOT + 1, :] = slot.astype(I32)
    copy.wait()
    for e in range(out_ref.shape[0]):
        out_ref[e] = fresh_ref[jnp.maximum(slot_ref[e // CAP, e % CAP] - 1, 0)]


def attend(batches, kbuf, vbuf, score, weight, cache, steps, heads, row_of, query_of, fresh_of, length_of, await_keys, await_values):
    positions, head = kbuf.shape[1:]
    lines = heads * steps
    lane = lanes(lines, positions)
    step = lax.rem(lines_of(lines, positions), steps)
    visible = (lane >= cache) & (lane - cache <= step)

    def fresh_rows(value):
        pad = jnp.zeros((FRESH - steps, head), F32)
        return jnp.concatenate([value.astype(F32), pad], axis=0).astype(BF16)

    for b, batch in enumerate(batches):
        for i in batch:
            fresh_key, fresh_value = fresh_of(i)
            kbuf[row_of(i), cache:positions, :] = fresh_rows(fresh_key)
            vbuf[row_of(i), cache:positions, :] = fresh_rows(fresh_value)
        await_keys(b)
        for i in batch:
            query = query_of(i).astype(F32)
            query = jnp.concatenate([query[:, h * head : (h + 1) * head] for h in range(heads)], axis=0)
            products = lax.dot_general(
                query.astype(BF16), kbuf[row_of(i)], (((1,), (1,)), ((), ())), preferred_element_type=F32
            )
            score[i * lines : (i + 1) * lines, :] = jnp.where(
                (lane < length_of(i)) | visible, products * head**-0.5, -jnp.inf
            )
    mixed = []
    for b, batch in enumerate(batches):
        chunk = slice(batch[0] * lines, (batch[-1] + 1) * lines)
        s = score[chunk, :]
        e = jnp.exp(s - jnp.max(s, axis=1, keepdims=True))
        weight[chunk, :] = (e * (1.0 / jnp.sum(e, axis=1, keepdims=True))).astype(BF16)
        await_values(b)
        for i in batch:
            mixed.append(
                jnp.dot(weight[i * lines : (i + 1) * lines, :], vbuf[row_of(i)], preferred_element_type=F32)
            )
    return mixed


def staying_kernel(
    plan_src, query_ref, key_ref, value_ref, keys_ref, values_ref, weight_ref,
    up_ref, heads_ref, fresh_ref, leave_keys_ref, leave_values_ref,
    plan_ref, kbuf, vbuf, score, weight, wbuf, psem, fsem, ksem, vsem, wsem,
):
    steps, wide = query_ref.shape[1:]
    slots, _, cache, head = keys_ref.shape
    tokens, columns = heads_ref.shape[0], up_ref.shape[1]
    rows, ring = tokens // steps, weight_ref.shape[1] // columns
    chunk = slots // ksem.shape[0]
    fresh = [
        pltpu.make_async_copy(src, fresh_ref.at[:, :, pl.ds(at, src.shape[2])], fsem.at[i])
        for i, (src, at) in enumerate(((query_ref, 0), (key_ref, wide), (value_ref, wide + head)))
    ]
    keys, values = (
        [
            pltpu.make_async_copy(
                ref.at[pl.ds(c * chunk, chunk), 0], buf.at[pl.ds(c * chunk, chunk), pl.ds(0, cache)], sem.at[c]
            )
            for c in range(slots // chunk)
        ]
        for ref, buf, sem in ((keys_ref, kbuf, ksem), (values_ref, vbuf, vsem))
    )
    listed = pltpu.make_async_copy(plan_src, plan_ref, psem)
    at = lax.rem(lax.axis_index("tp") + ring // 2, ring) * columns
    far = pltpu.make_async_copy(weight_ref.at[:, pl.ds(pl.multiple_of(at, columns), columns)], wbuf, wsem)
    for copy in [listed] + fresh + keys + values + [far]:
        copy.start()

    last = [(slots - rows + i) // chunk for i in range(rows)]
    batches = [[i for i in range(rows) if last[i] == c] for c in sorted(set(last))]
    due = [[c for c in range(slots // chunk) if c <= last[b[0]] and (j == 0 or c > last[batches[j - 1][0]])] for j, b in enumerate(batches)]

    def slot(i):
        return plan_ref[STAY_SLOT, i]

    def await_values(b):
        if b == 0:
            for i in range(leave_keys_ref.shape[0]):
                leave_keys_ref[i] = kbuf[plan_ref[LEAVE_SLOT, i], 0:cache, :]
        for c in due[b]:
            values[c].wait()

    for copy in [listed] + fresh:
        copy.wait()
    mixed = attend(
        batches, kbuf, vbuf, score, weight, cache, steps, wide // head,
        slot,
        lambda i: fresh_ref[slot(i), :, 0:wide],
        lambda i: (fresh_ref[slot(i), :, wide : wide + head], fresh_ref[slot(i), :, wide + head : wide + 2 * head]),
        lambda i: plan_ref[STAY_LENGTH, i],
        lambda b: [keys[c].wait() for c in due[b]],
        await_values,
    )
    for j in range(rows // 4):
        for h in range(wide // head):
            tile = jnp.concatenate([o[h * steps : (h + 1) * steps] for o in mixed[4 * j : 4 * j + 4]], axis=0)
            heads_ref[16 * j : 16 * j + 16, h * head : (h + 1) * head] = tile.astype(BF16)
    for i in range(leave_keys_ref.shape[0]):
        leave_values_ref[i] = vbuf[plan_ref[LEAVE_SLOT, i], 0:cache, :]
    far.wait()
    up_ref[...] = jnp.dot(heads_ref[...], wbuf[...], preferred_element_type=F32).astype(BF16)


def load_blocks(blocks, weight_ref, parts, sem):
    columns = parts[0].shape[1] if parts else 1
    ring = weight_ref.shape[1] // columns
    copies = []
    for j, step in enumerate(blocks):
        at = pl.multiple_of(lax.rem(lax.axis_index("tp") + step, ring) * columns, columns)
        copies.append(pltpu.make_async_copy(weight_ref.at[:, pl.ds(at, columns)], parts[j], sem.at[j]))
    return copies


def hop_kernel(blocks, came, held, heads_ref, *rest):
    sums, weight_ref, rest = rest[:came], rest[came], rest[came + 1 :]
    held_refs, rest = rest[:held], rest[held:]
    outs, kept, rest = rest[:2], rest[2 : len(blocks)], rest[len(blocks) :]
    bufs, sem, scratch = rest[:came], rest[came], rest[came + 1 :]
    parts = [*held_refs, *scratch, *kept]
    loads = dict(enumerate(load_blocks(blocks[held:], weight_ref, parts[held:], sem.at[pl.ds(2, 8)]), held))
    sums = [pltpu.make_async_copy(src, dst, sem.at[i]) for i, (src, dst) in enumerate(zip(sums, bufs))]
    for copy in [loads[j] for j in loads if j < 2] + sums + [loads[j] for j in loads if j >= 2]:
        copy.start()
    for j, out in enumerate(outs):
        if j in loads:
            loads[j].wait()
        terms = jnp.dot(heads_ref[...], parts[j][...], preferred_element_type=F32)
        if j < came:
            sums[j].wait()
            terms = terms + bufs[j][...].astype(F32)
        out[...] = terms.astype(BF16)
    for j in loads:
        if j >= 2:
            loads[j].wait()


def leaving_kernel(plan_src, asked_ref, keys_ref, values_ref, out_ref, plan_ref, kbuf, vbuf, score, weight, psem):
    listed = pltpu.make_async_copy(plan_src, plan_ref, psem)
    listed.start()
    rows, cache, head = keys_ref.shape
    steps, wide = out_ref.shape[1:]
    out_ref[...] = jnp.zeros(out_ref.shape, BF16)
    for i in range(rows):
        kbuf[i, 0:cache, :] = keys_ref[i]
        vbuf[i, 0:cache, :] = values_ref[i]
    listed.wait()

    def entry(i):
        return plan_ref[LEAVE_ENTRY, i]

    mixed = attend(
        [list(range(rows))], kbuf, vbuf, score, weight, cache, steps, wide // head,
        lambda i: i,
        lambda i: asked_ref[entry(i), :, 0:wide],
        lambda i: (asked_ref[entry(i), :, wide : wide + head], asked_ref[entry(i), :, wide + head : wide + 2 * head]),
        lambda i: plan_ref[LEAVE_LENGTH, i],
        lambda b: None,
        lambda b: None,
    )
    for i, o in enumerate(mixed):
        for h in range(wide // head):
            out_ref[entry(i), :, h * head : (h + 1) * head] = o[h * steps : (h + 1) * steps].astype(BF16)


def arrived_kernel(order, here_src, back_ref, weight_ref, out_ref, *rest):
    kept, (here_ref, heads, wbuf, sums, hsem, wsem, osem) = rest[:2], rest[2:]
    listed = pltpu.make_async_copy(here_src, here_ref, hsem)
    listed.start()
    steps = back_ref.shape[1]
    ring, lines, _ = out_ref.shape
    rows = lines // steps
    parts = [*kept, *(wbuf.at[j] for j in range(ring - 2))]
    loads = load_blocks(order, weight_ref, parts, wsem)
    for copy in loads:
        copy.start()
    listed.wait()
    for j in range(heads.shape[0] // 16):
        four = [back_ref[here_ref[HERE_ENTRY, min(4 * j + u, rows - 1)]].astype(F32) for u in range(4)]
        heads[16 * j : 16 * j + 16, :] = jnp.concatenate(four, axis=0).astype(BF16)
    done = []
    for j, k in enumerate(order):
        loads[j].wait()
        terms = jnp.dot(heads[...], parts[j][...], preferred_element_type=F32)
        sums[j] = terms[:lines].astype(BF16)
        to = lax.rem(lax.axis_index("tp") + k, ring)
        done.append(pltpu.make_async_copy(sums.at[j], out_ref.at[to], osem.at[j]))
        done[j].start()
    for copy in done:
        copy.wait()


def place_kernel(plan_ref, heads_ref, up_ref, down_ref, weight_ref, out_ref, total, wbuf, sem):
    steps, columns = out_ref.shape[1:]
    at = pl.multiple_of(lax.axis_index("tp") * columns, columns)
    copy = pltpu.make_async_copy(weight_ref.at[:, pl.ds(at, columns)], wbuf, sem)
    copy.start()
    out_ref[...] = jnp.zeros(out_ref.shape, BF16)
    copy.wait()
    own = jnp.dot(heads_ref[...], wbuf[...], preferred_element_type=F32)
    total[...] = own + up_ref[...].astype(F32) + down_ref[...].astype(F32)
    for i in range(heads_ref.shape[0] // steps):

        @pl.when(i >= plan_ref[STAY_FIRST, 0])
        def _():
            out_ref[plan_ref[STAY_SLOT, i]] = total[i * steps : (i + 1) * steps, :].astype(BF16)


def finish_kernel(here_src, placed_ref, blocks_ref, out_ref, here_ref, total, hsem):
    listed = pltpu.make_async_copy(here_src, here_ref, hsem)
    listed.start()
    steps = out_ref.shape[1]
    out_ref[...] = placed_ref[...]
    terms = blocks_ref[0].astype(F32)
    for k in range(1, blocks_ref.shape[0]):
        terms = terms + blocks_ref[k].astype(F32)
    total[...] = terms
    listed.wait()
    for n in range(blocks_ref.shape[1] // steps):
        out_ref[here_ref[HERE_SLOT, n]] = total[n * steps : (n + 1) * steps, :].astype(BF16)


def on_device(
    keys_cache,
    values_cache,
    lengths,
    guard_flags,
    migrations,
    queries,
    new_keys,
    new_values,
    out_weight,
):
    shape = jax.ShapeDtypeStruct
    slots, _, cache, head = keys_cache.shape
    steps, wide = queries.shape[1:]
    moves = migrations.shape[0]
    groups, ring = lax.axis_size("group"), lax.axis_size("tp")
    columns = out_weight.shape[1] // ring
    entries = groups * CAP
    staying = slots - 2 * moves
    lines = wide // head * steps
    positions = cache + FRESH
    barrier = lax.optimization_barrier
    keys_cache, values_cache, out_weight, queries, new_keys, new_values, moves_t, flags, reach = (
        pltpu.with_memory_space_constraint(x, pltpu.HBM)
        for x in (
            keys_cache, values_cache, out_weight, queries, new_keys, new_values,
            migrations.T, guard_flags.reshape(1, slots), lengths.reshape(1, slots),
        )
    )

    def exchange(x, axis):
        return lax.all_to_all(x, axis, split_axis=0, concat_axis=0, tiled=True)

    def scratch(held, rows):
        return [
            pltpu.VMEM((held, positions, head), BF16),
            pltpu.VMEM((held, positions, head), BF16),
            pltpu.VMEM((rows * lines, positions), F32),
            pltpu.VMEM((rows * lines, positions), BF16),
        ]

    table, plan = call(
        plan_kernel,
        [shape((groups, 128), I32), shape((8, slots), I32)],
        [ANY] * 3,
        [
            pltpu.VMEM((3, moves), I32),
            pltpu.VMEM((1, slots), I32),
            pltpu.VMEM((1, slots), I32),
            pltpu.SemaphoreType.DMA((3,)),
        ],
        nbytes=1 << 16,
    )(moves_t, flags, reach)
    table = exchange(table.reshape(groups, 1, 128), "group").reshape(groups, 128)

    tokens = staying * steps
    up, heads, fresh, leave_keys, leave_values = call(
        staying_kernel,
        [
            shape((tokens, columns), BF16),
            shape((tokens, wide), BF16),
            shape((slots, steps, wide + 2 * head), BF16),
            shape((moves, cache, head), BF16),
            shape((moves, cache, head), BF16),
        ],
        [pl.BlockSpec(memory_space=pl.ANY)] + [ANY] * 6,
        [pltpu.SMEM((8, slots), I32)]
        + scratch(slots, staying)
        + [
            pltpu.VMEM((wide, columns), BF16),
            pltpu.SemaphoreType.DMA,
            pltpu.SemaphoreType.DMA((3,)),
            pltpu.SemaphoreType.DMA((4,)),
            pltpu.SemaphoreType.DMA((4,)),
            pltpu.SemaphoreType.DMA,
        ],
        flops=2 * tokens * wide * columns,
        nbytes=16 << 20,
        exps=tokens * positions * 4,
        limit=24,
    )(plan, queries, new_keys, new_values, keys_cache, values_cache, out_weight)

    ahead = [(i, (i + 1) % ring) for i in range(ring)]
    astern = [(i, (i - 1) % ring) for i in range(ring)]

    def hop(u, d):
        return lax.ppermute(u, "tp", ahead), lax.ppermute(d, "tp", astern)

    part = ((wide, columns), BF16)

    def add(k, *sums, keep=(), held=()):
        blocks = (k, ring - k, *keep)
        return call(
            functools.partial(hop_kernel, blocks, len(sums), len(held)),
            [shape((tokens, columns), BF16)] * 2 + [shape(*part)] * len(keep),
            [VMEM] + [pl.BlockSpec(memory_space=pl.ANY)] * len(sums) + [ANY] + [VMEM] * len(held),
            [pltpu.VMEM(x.shape, BF16) for x in sums]
            + [pltpu.SemaphoreType.DMA((2 + ring,))]
            + [pltpu.VMEM(*part)] * (2 - len(held)),
            flops=HOP_COST,
        )(heads, *sums, out_weight, *held)

    table, fresh, heads, leave_keys = barrier((table, fresh, heads, leave_keys))
    asked, here = call(
        payload_kernel,
        [shape((entries, steps, wide + 2 * head), BF16), shape((8, 128), I32)],
        [pl.BlockSpec(memory_space=pl.ANY)] + [VMEM] * 2,
        [pltpu.SMEM((groups, 128), I32), pltpu.SemaphoreType.DMA],
        flops=PAYLOAD_COST,
    )(table, table, fresh)
    asked, heads = barrier((asked, heads))
    asked = exchange(asked, "group")
    up = lax.ppermute(up, "tp", ahead)

    up, down = add(3, up)
    asked = barrier((asked, up, down))[0]
    up, down = hop(up, down)
    back = call(
        leaving_kernel,
        shape((entries, steps, wide), BF16),
        [pl.BlockSpec(memory_space=pl.ANY)] + [VMEM] * 3,
        [pltpu.SMEM((8, slots), I32)] + scratch(moves, moves) + [pltpu.SemaphoreType.DMA],
    )(plan, asked, leave_keys, leave_values)
    back, heads = barrier((back, heads))
    back = exchange(back, "group")
    up, down = add(2, up, down)
    back = barrier((back, up, down))[0]
    up, down = hop(up, down)
    arrived = moves * steps
    order = (1, ring - 1, 0, *range(2, ring - 1))
    blocks, *late = call(
        functools.partial(arrived_kernel, order),
        [shape((ring, arrived, columns), BF16)] + [shape(*part)] * 2,
        [pl.BlockSpec(memory_space=pl.ANY), VMEM, ANY],
        [
            pltpu.SMEM((8, 128), I32),
            pltpu.VMEM((-(-arrived // 16) * 16, wide), BF16),
            pltpu.VMEM((ring - 2, wide, columns), BF16),
            pltpu.VMEM((ring, arrived, columns), BF16),
            pltpu.SemaphoreType.DMA,
            pltpu.SemaphoreType.DMA((ring,)),
            pltpu.SemaphoreType.DMA((ring,)),
        ],
        out=[ANY, VMEM, VMEM],
        flops=ARRIVED_COST,
        limit=10,
    )(here, back, out_weight)
    blocks, heads = barrier((blocks, heads))
    up, down = add(1, up, down, held=late)
    blocks = barrier((blocks, up, down))[0]
    blocks = exchange(blocks, "tp")
    up, down = hop(up, down)

    placed = call(
        place_kernel,
        shape((slots, steps, columns), BF16),
        [SMEM] + [VMEM] * 3 + [ANY],
        [pltpu.VMEM((tokens, columns), F32), pltpu.VMEM((wide, columns), BF16), pltpu.SemaphoreType.DMA],
        flops=PLACE_COST,
    )(plan, heads, up, down, out_weight)
    return call(
        finish_kernel,
        shape((slots, steps, columns), BF16),
        [pl.BlockSpec(memory_space=pl.ANY)] + [VMEM] * 2,
        [pltpu.SMEM((8, 128), I32), pltpu.VMEM((arrived, columns), F32), pltpu.SemaphoreType.DMA],
        nbytes=2 << 20,
    )(here, placed, blocks)


def solution(mesh):
    return jax.shard_map(
        on_device,
        mesh=mesh,
        in_specs=(
            P("group", "tp", None, None),
            P("group", "tp", None, None),
            P("group"),
            P("group"),
            P("group", None),
            P("group", None, "tp"),
            P("group", None, "tp"),
            P("group", None, "tp"),
            P("tp", None),
        ),
        out_specs=P("group", None, "tp"),
        check_vma=False,
    )
```
